256 devices in a mesh: feat: 32 (over z, y), node: 8 (over x, core).
Axes of the slice: x: 4, y: 4, z: 8, core: 2. Of those that a mesh axis runs over, the one named last changes fastest.
Arguments:
- features: bfloat16 [1280, 8, 24576], P('feat', 'node'), may hold values from -6 to 6
- first_neighbours: int32 [10, 8, 6144], P(None, 'node'), may hold values from 0 to 24575
- first_mask: int32 [10, 8, 6144], P(None, 'node'), may hold values 0 or 1
- second_neighbours: int32 [10, 8, 4096], P(None, 'node', 'feat'), may hold values from 0 to 6143, as said below
- second_mask: int32 [10, 8, 4096], P(None, 'node', 'feat'), may hold values 0 or 1
- target_index: int32 [8, 4096], P('node', 'feat'), may hold values from 0 to 6143
- labels: int32 [8, 4096], P('node', 'feat'), may hold values from 0 to 10239
- first_weight: bfloat16 [2, 1280, 256], P(None, 'feat'), may hold values from -0.15625 to 0.15625
- first_bias: float32 [256], replicated, may hold values from -3 to 3
- class_weight: bfloat16 [512, 10240], P(None, 'node'), may hold values from -2.5 to 2.5
Outputs:
- hidden: bfloat16 [8, 6144, 256], P('node', 'feat')
- loss: float32 [8, 4096], P('node', 'feat')
The draws below stay inside these ranges and needn't reach their ends.
Inputs may be any that keep to these rules, and one draw needn't show every extreme that they name: In every group, the 128 targets of each aligned block of target positions name, through second_neighbours (masked slots included) and target_index together, exactly 24 distinct first-layer nodes among the 192 nodes o * 192 to (o + 1) * 192 - 1, for every o.
All inputs are finite; a program needn't handle non-finite values. No bound on the sum of `first_mask` or of `second_mask` on one device may be relied on, other than what follows from the above.
Results may differ from the reference program's by a relative error of at most 0.0027.
Values may be sent and summed in bfloat16 or wider, within the bound.
No kernel may reach another device: no remote copies, remote signals or barrier semaphores. Data moves between devices by JAX's collectives and lax.ppermute only.
A program may use at most 128 MiB of HBM per device.

```python
import math
import jax
import jax.numpy as jnp

F = 1280
H = 256
C = 10240
FAN = 10
TGT_DEV = 128
H1_DEV = 192
R1 = 6144
R2 = 24576
TGT_GROUP = 4096
N_NODE = 8


def shared_references(key):
    blocks = TGT_GROUP // TGT_DEV
    limit = H1_DEV // 8
    amount = (FAN + 1) * TGT_DEV
    union_size = blocks * limit
    key_rows, key_pick, key_order = jax.random.split(key, 3)
    scores = jax.random.randint(key_rows, (N_NODE, blocks, blocks, H1_DEV), 0, 2 ** 18) * H1_DEV + jnp.arange(H1_DEV, dtype=jnp.int32)
    chosen = jnp.argsort(scores, axis=-1)[..., :limit].astype(jnp.int32)
    chosen = chosen + (jnp.arange(blocks, dtype=jnp.int32) * H1_DEV)[None, None, :, None]
    union = chosen.reshape(N_NODE, blocks, union_size)
    position = jnp.arange(amount, dtype=jnp.int32)
    extra = jax.random.randint(key_pick, (N_NODE, blocks, amount), 0, union_size)
    pick = jnp.where(position[None, None, :] < union_size, jnp.broadcast_to(position, (N_NODE, blocks, amount)), extra)
    order_scores = jax.random.randint(key_order, (N_NODE, blocks, amount), 0, 2 ** 18) * amount + position
    order = jnp.argsort(order_scores, axis=-1).astype(jnp.int32)
    pick = jnp.take_along_axis(pick, order, axis=-1)
    return jnp.take_along_axis(union, pick, axis=-1).astype(jnp.int32)


def draw_second_neighbours(key, part):
    references = shared_references(key)
    blocks = TGT_GROUP // TGT_DEV
    slots = references[:, :, :FAN * TGT_DEV].reshape(N_NODE, blocks, FAN, TGT_DEV)
    return jnp.transpose(slots, (2, 0, 1, 3)).reshape(FAN, N_NODE, TGT_GROUP)


def draw_target_index(key, part):
    references = shared_references(key)
    return references[:, :, FAN * TGT_DEV:].reshape(N_NODE, TGT_GROUP)


def draw_class_weight(key, part):
    key = jax.random.fold_in(key, 7)
    base_key, scale_key = jax.random.split(key, 2)
    column_scale = jnp.exp(jax.random.uniform(scale_key, (C,), jnp.float32, math.log(0.4), math.log(4.0)))
    base = jax.random.truncated_normal(base_key, -6.0, 6.0, (2 * H, C), jnp.float32) * (2 * H) ** (-0.5)
    base = base * column_scale[None, :]
    return jnp.clip(base, -2.5, 2.5).astype(jnp.bfloat16)


def place_ends(drawn, stream_key, low, top_value):
    shape = drawn.shape
    index_at = [jax.random.randint(jax.random.fold_in(stream_key, axis), (), 0, shape[axis]) for axis in range(len(shape))]
    drawn = drawn.at[tuple(index_at)].set(low)
    longest = shape.index(max(shape))
    index_at[longest] = (index_at[longest] + 1) % shape[longest]
    return drawn.at[tuple(index_at)].set(top_value)


def block_scale(key, dims, cuts, low, largest):
    def one(dim, blocks):
        steps = jax.random.uniform(jax.random.fold_in(jax.random.fold_in(key, 6), dim), (blocks,), jnp.float32, low / len(cuts), largest / len(cuts))
        return jnp.repeat(jnp.exp(steps), dims[dim] // blocks).reshape((-1,) + (1,) * (len(dims) - dim - 1))

    loudness = one(*cuts[0])
    for cut in cuts[1:]:
        loudness = loudness * one(*cut)
    return loudness


def noise(key, extent, width, most, shards=(), kind=jnp.bfloat16):
    entries = width * jax.random.normal(key, extent, jnp.float32)
    if shards:
        entries = entries * block_scale(key, extent, shards, -0.22, 0.18)
    return jnp.clip(entries, -most, most).astype(kind)


def setup_inputs(seed: int = 0) -> dict:
    streams_of = jax.random.split(jax.random.key(seed), 11)
    features = noise(streams_of[0], (F, N_NODE, R2), 1.0, 6.0, ((0, 32), (1, 8)))
    first_neighbours = place_ends(jax.random.randint(streams_of[1], (FAN, N_NODE, R1), 0, R2), jax.random.fold_in(streams_of[1], 1), 0, R2 - 1).astype(jnp.int32)
    first_mask = place_ends((jax.random.randint(streams_of[2], (FAN, N_NODE, R1), 0, 2) < 1).astype(jnp.int32), jax.random.fold_in(streams_of[2], 1), 0, 1)
    second_neighbours = draw_second_neighbours(jax.random.fold_in(streams_of[10], 71), 0)
    second_mask = place_ends((jax.random.randint(streams_of[4], (FAN, N_NODE, TGT_GROUP), 0, 2) < 1).astype(jnp.int32), jax.random.fold_in(streams_of[4], 1), 0, 1)
    target_index = draw_target_index(jax.random.fold_in(streams_of[10], 71), 0)
    labels = place_ends(jax.random.randint(streams_of[6], (N_NODE, TGT_GROUP), 0, C), jax.random.fold_in(streams_of[6], 1), 0, C - 1).astype(jnp.int32)
    first_weight = noise(streams_of[7], (2, F, H), F ** -0.5, 0.15625, ((1, 32),))
    first_bias = noise(streams_of[8], (H,), 0.5, 3.0, (), jnp.float32)
    class_weight = draw_class_weight(jax.random.fold_in(streams_of[10], 71), 0)
    return dict(features=features, first_neighbours=first_neighbours, first_mask=first_mask, second_neighbours=second_neighbours, second_mask=second_mask, target_index=target_index, labels=labels, first_weight=first_weight, first_bias=first_bias, class_weight=class_weight)


def average_columns(table, lists, mask):
    total = jnp.zeros((table.shape[0], lists.shape[1]), jnp.float32)
    count = jnp.zeros((lists.shape[1],), jnp.float32)
    for slot in range(FAN):
        weight = mask[slot].astype(jnp.float32)
        total = total + table[:, lists[slot]].astype(jnp.float32) * weight[None, :]
        count = count + weight
    return (total / jnp.maximum(count, 1.0)[None, :]).astype(jnp.bfloat16)


def average_rows(table, lists, mask):
    total = jnp.zeros((lists.shape[1], table.shape[1]), jnp.float32)
    count = jnp.zeros((lists.shape[1],), jnp.float32)
    for slot in range(FAN):
        weight = mask[slot].astype(jnp.float32)
        total = total + table[lists[slot]].astype(jnp.float32) * weight[:, None]
        count = count + weight
    return (total / jnp.maximum(count, 1.0)[:, None]).astype(jnp.bfloat16)


def reference(features, first_neighbours, first_mask, second_neighbours, second_mask, target_index, labels, first_weight, first_bias, class_weight):
    hidden_all = []
    loss_all = []
    for group in range(N_NODE):
        columns = features[:, group, :]
        agg_one = average_columns(columns, first_neighbours[:, group, :], first_mask[:, group, :])
        stacked = jnp.stack([columns[:, :R1], agg_one]).astype(jnp.float32)
        pre_one = jnp.einsum("sfr,sfh->rh", stacked, first_weight.astype(jnp.float32)) + first_bias
        hidden_now = jax.nn.relu(pre_one).astype(jnp.bfloat16)
        agg_two = average_rows(hidden_now, second_neighbours[:, group, :], second_mask[:, group, :])
        inputs = jnp.concatenate([hidden_now[target_index[group]], agg_two], axis=1)
        logits = jnp.dot(inputs.astype(jnp.float32), class_weight.astype(jnp.float32))
        total = jax.nn.logsumexp(logits, axis=1)
        picked = jnp.take_along_axis(logits, labels[group][:, None], axis=1)[:, 0]
        hidden_all.append(hidden_now)
        loss_all.append(total - picked)
    return jnp.stack(hidden_all), jnp.stack(loss_all)
```

```python
import functools

import jax
import jax.numpy as jnp
from jax import lax
from jax.experimental import pallas as pl
from jax.experimental.pallas import tpu as pltpu
from jax.sharding import PartitionSpec as P

FEAT = 32
NODE = 8
WIDTH = 40
INPUTS = 24576
ROWS = 6144
OWN = 192
FAN = 10
TARGETS = 128
HIDDEN = 256
UNION = 24
SLAB = 256
UNROLL = 16
TABLE_STEP = 8
F32 = jnp.float32
BF16 = jnp.bfloat16


def iota(shape, dim):
    return lax.broadcasted_iota(jnp.int32, shape, dim)


def contract(a, b, dim_a, dim_b):
    return lax.dot_general(a, b, (((dim_a,), (dim_b,)), ((), ())), preferred_element_type=F32)


def earlier(size):
    return jnp.where(iota((size, size), 0) < iota((size, size), 1), 1.0, 0.0).astype(BF16)


def add_all(terms):
    while len(terms) > 1:
        paired = [terms[k] + terms[k + 1] for k in range(0, len(terms) - 1, 2)]
        terms = paired + terms[len(terms) - len(terms) % 2 :]
    return terms[0]


def gather_kernel(slots, features, second, send, place, table, sums, flags):
    def fill(step, carry):
        for part in range(TABLE_STEP):
            at = pl.multiple_of((step * TABLE_STEP + part) * 128, 128)
            block = jnp.concatenate(
                [features[:, pl.ds(at, 128)].astype(F32), jnp.ones((8, 128), F32)], axis=0
            )
            table[pl.ds(at, 128), pl.ds(0, WIDTH + 8)] = block.T
        return carry

    lax.fori_loop(0, INPUTS // 128 // TABLE_STEP, fill, 0)
    table[pl.ds(INPUTS, 8), :] = jnp.zeros((8, 128), F32)

    owners, lanes = [], []
    named = jnp.zeros((FEAT, SLAB), F32)
    for slot in range(FAN + 1):
        index = second[pl.ds(slot, 1), :]
        owner = ((index.astype(F32) + 0.5) * (1.0 / OWN)).astype(jnp.int32)
        row = index - owner * OWN
        owner_hot = jnp.where(iota((FEAT, TARGETS), 0) == owner, 1.0, 0.0).astype(BF16)
        row_hot = jnp.where(iota((SLAB, TARGETS), 0) == row, 1.0, 0.0)
        named = named + contract(owner_hot, row_hot.astype(BF16), 1, 1)
        owners.append((owner, owner_hot))
        lanes.append(row_hot)
    marked = jnp.where(named > 0.0, 1.0, 0.0)
    flags[...] = marked
    rank = contract(marked.astype(BF16), earlier(SLAB), 1, 0).astype(BF16)
    places = []
    for slot in range(FAN + 1):
        owner, owner_hot = owners[slot]
        mine = jnp.sum(contract(rank, owner_hot, 0, 0) * lanes[slot], axis=0, keepdims=True)
        places.append(owner * UNION + mine.astype(jnp.int32))
    place[...] = jnp.concatenate(places + [jnp.zeros((5, TARGETS), jnp.int32)], axis=0)

    def owner_step(owner, carry):
        first = pl.multiple_of(owner * OWN, 64)

        def block(step, inner):
            at = first + step * UNROLL
            lists = [slots.at[pl.ds(slot * ROWS + at, UNROLL)] for slot in range(FAN)]
            result = sums.at[pl.ds(pl.multiple_of(step * UNROLL, UNROLL), UNROLL), :]
            for row in range(UNROLL):
                result[pl.ds(row, 1), :] = add_all(
                    [table[pl.ds(lists[slot][row], 1), :] for slot in range(FAN)]
                )
            return inner

        lax.fori_loop(0, OWN // UNROLL, block, 0)
        own = table[pl.ds(first, 128), :].T
        head = sums[pl.ds(0, 128), :].T
        tail = jnp.concatenate(
            [table[pl.ds(first + 128, 64), :], sums[pl.ds(128, 64), :]], axis=0
        ).T
        marks = flags[pl.ds(owner, 1), :]
        send[owner] = jnp.concatenate(
            [
                own[:WIDTH],
                head[:WIDTH] / jnp.maximum(head[WIDTH : WIDTH + 1], 1.0),
                tail[:WIDTH] / jnp.maximum(tail[WIDTH : WIDTH + 1], 1.0),
                marks[:, :128],
                marks[:, 128:],
                jnp.zeros((6, 128), F32),
            ],
            axis=0,
        ).astype(BF16)
        return carry

    lax.fori_loop(0, FEAT, owner_step, 0)


def hidden_kernel(got, weights, bias, hidden, rows, head, tail, tail_weights, marks, chosen):
    for source in range(FEAT):
        block = got[source].astype(F32)
        head[pl.ds(source * 80, 80), :] = block[:80].astype(BF16)
        tail[pl.ds(source * 40, 40), :] = block[80:120].astype(BF16)
        marks[pl.ds(source, 1), pl.ds(0, 128)] = block[120:121]
        marks[pl.ds(source, 1), pl.ds(128, 128)] = block[121:122]
        pair = weights[pl.ds(source * 80, 80), :].astype(F32)
        tail_weights[pl.ds(source * 40, 40), pl.ds(0, HIDDEN)] = pair[:40].astype(BF16)
        tail_weights[pl.ds(source * 40, 40), pl.ds(HIDDEN, HIDDEN)] = pair[40:].astype(BF16)
    most = contract(head[...], weights[...], 0, 0)
    rest = contract(tail[...], tail_weights[...], 0, 0)
    rest = rest[:64, :HIDDEN] + rest[64:, HIDDEN:]
    pre = jnp.concatenate([most, rest], axis=0) + bias[...]
    result = jnp.maximum(pre, 0.0).astype(BF16)
    hidden[...] = result
    rank = contract(marks[...].astype(BF16), earlier(SLAB), 1, 0)
    for source in range(FEAT):
        hit = (iota((UNION, SLAB), 0).astype(F32) == rank[source : source + 1]) & (
            marks[pl.ds(source, 1), :] > 0.0
        )
        chosen[pl.ds(source * UNION, UNION), :] = jnp.where(hit, 1.0, 0.0)
    padded = jnp.concatenate([result, jnp.zeros((SLAB - OWN, HIDDEN), BF16)], axis=0)
    rows[...] = contract(chosen[...].astype(BF16), padded, 1, 0).astype(BF16)


def loss_kernel(rows, place, mask, labels, weights, loss, inputs, largest, summed, picked):
    step = pl.program_id(0)
    width = weights.shape[2]

    @pl.when(step == 0)
    def _():
        spots = iota((FEAT * UNION, TARGETS), 0)
        total = jnp.zeros((FEAT * UNION, TARGETS), F32)
        for slot in range(FAN):
            used = mask[pl.ds(slot, 1), :].astype(F32)
            total = total + jnp.where(spots == place[pl.ds(slot, 1), :], used, 0.0)
        total = total.astype(BF16)
        self_hot = jnp.where(spots == place[pl.ds(FAN, 1), :], 1.0, 0.0).astype(BF16)
        count = contract(total, jnp.ones((FEAT * UNION, 128), BF16), 0, 0)[:, :1]
        agg = contract(total, rows[...], 0, 0) / jnp.maximum(count, 1.0)
        inputs[:, pl.ds(0, HIDDEN)] = contract(self_hot, rows[...], 0, 0).astype(BF16)
        inputs[:, pl.ds(HIDDEN, HIDDEN)] = agg.astype(BF16)
        largest[...] = jnp.full((TARGETS, 1), -jnp.inf, F32)
        summed[...] = jnp.zeros((TARGETS, 1), F32)
        picked[...] = jnp.zeros((TARGETS, 1), F32)

    logits = contract(inputs[...], weights[0], 1, 0)
    before = largest[...]
    now = jnp.maximum(before, jnp.max(logits, axis=1, keepdims=True))
    part = jnp.sum(jnp.exp(logits - now), axis=1, keepdims=True)
    summed[...] = summed[...] * jnp.exp(before - now) + part
    largest[...] = now
    classes = iota((TARGETS, width), 1) + step * width
    picked[...] += jnp.sum(jnp.where(classes == labels[...], logits, 0.0), axis=1, keepdims=True)

    @pl.when(step == NODE - 1)
    def _():
        loss[...] = largest[...] + jnp.log(summed[...]) - picked[...]


VMEM = pl.BlockSpec(memory_space=pltpu.VMEM)
SMEM = pl.BlockSpec(memory_space=pltpu.SMEM)


def body(
    features,
    first_neighbours,
    first_mask,
    second_neighbours,
    second_mask,
    target_index,
    labels,
    first_weight,
    first_bias,
    class_weight,
):
    slots = jnp.where(first_mask[:, 0, :] > 0, first_neighbours[:, 0, :], INPUTS).reshape(-1)
    second = jnp.concatenate(
        [second_neighbours[:, 0, :], target_index, jnp.zeros((5, TARGETS), jnp.int32)], axis=0
    )
    all_first = lax.all_gather(first_weight, "feat", axis=0).reshape(FEAT * 2 * WIDTH, HIDDEN)
    all_class = lax.all_gather(class_weight, "node", axis=0)
    send, place = pl.pallas_call(
        gather_kernel,
        out_shape=(
            jax.ShapeDtypeStruct((FEAT, 128, 128), BF16),
            jax.ShapeDtypeStruct((16, TARGETS), jnp.int32),
        ),
        in_specs=[SMEM, VMEM, VMEM],
        out_specs=(VMEM, VMEM),
        scratch_shapes=[
            pltpu.VMEM((INPUTS + 8, 128), F32),
            pltpu.VMEM((OWN, 128), F32),
            pltpu.VMEM((FEAT, SLAB), F32),
        ],
        compiler_params=pltpu.CompilerParams(vmem_limit_bytes=40 * 2**20),
        cost_estimate=pl.CostEstimate(flops=10**9, bytes_accessed=150 * 10**6, transcendentals=0),
    )(slots, features[:, 0, :], second)
    got = lax.all_to_all(send, "feat", 0, 0)
    hidden, rows = pl.pallas_call(
        hidden_kernel,
        out_shape=(
            jax.ShapeDtypeStruct((OWN, HIDDEN), BF16),
            jax.ShapeDtypeStruct((FEAT * UNION, HIDDEN), BF16),
        ),
        in_specs=[VMEM] * 3,
        out_specs=(VMEM, VMEM),
        scratch_shapes=[
            pltpu.VMEM((FEAT * 80, 128), BF16),
            pltpu.VMEM((FEAT * 40, 128), BF16),
            pltpu.VMEM((FEAT * 40, 2 * HIDDEN), BF16),
            pltpu.VMEM((FEAT, SLAB), F32),
            pltpu.VMEM((FEAT * UNION, SLAB), F32),
        ],
        compiler_params=pltpu.CompilerParams(vmem_limit_bytes=40 * 2**20),
    )(got, all_first, first_bias[None, :])
    rows = lax.all_to_all(rows.reshape(FEAT, UNION, HIDDEN), "feat", 0, 0)
    rows = rows.reshape(FEAT * UNION, HIDDEN)
    width = class_weight.shape[1]
    whole = lambda *shape: pl.BlockSpec(shape, lambda i: (0,) * len(shape))
    loss = pl.pallas_call(
        loss_kernel,
        grid=(NODE,),
        out_shape=jax.ShapeDtypeStruct((TARGETS, 1), F32),
        in_specs=[
            whole(FEAT * UNION, HIDDEN),
            whole(16, TARGETS),
            whole(FAN, TARGETS),
            whole(TARGETS, 1),
            pl.BlockSpec((1, 2 * HIDDEN, width), lambda i: (i, 0, 0)),
        ],
        out_specs=whole(TARGETS, 1),
        scratch_shapes=[
            pltpu.VMEM((TARGETS, 2 * HIDDEN), BF16),
            pltpu.VMEM((TARGETS, 1), F32),
            pltpu.VMEM((TARGETS, 1), F32),
            pltpu.VMEM((TARGETS, 1), F32),
        ],
        compiler_params=pltpu.CompilerParams(vmem_limit_bytes=40 * 2**20),
    )(rows, place, second_mask[:, 0, :], labels.reshape(TARGETS, 1), all_class)
    return (hidden[None], loss.reshape(1, TARGETS))


def solution(mesh):
    placed = (
        P("feat", "node", None),
        P(None, "node", None),
        P(None, "node", None),
        P(None, "node", "feat"),
        P(None, "node", "feat"),
        P("node", "feat"),
        P("node", "feat"),
        P(None, "feat", None),
        P(),
        P(None, "node"),
    )
    return jax.shard_map(
        body,
        mesh=mesh,
        in_specs=placed,
        out_specs=(P("node", "feat", None), P("node", "feat")),
        check_vma=False,
    )
```

```python
import functools

import jax
import jax.numpy as jnp
from jax import lax
from jax.experimental import pallas as pl
from jax.experimental.pallas import tpu as pltpu
from jax.sharding import PartitionSpec as P

FEAT = 32
NODE = 8
WIDTH = 40
INPUTS = 24576
ROWS = 6144
OWN = 192
FAN = 10
TARGETS = 128
HIDDEN = 256
UNION = 24
SLAB = 256
UNROLL = 16
TABLE_STEP = 8
F32 = jnp.float32
BF16 = jnp.bfloat16


def iota(shape, dim):
    return lax.broadcasted_iota(jnp.int32, shape, dim)


def contract(a, b, dim_a, dim_b):
    return lax.dot_general(a, b, (((dim_a,), (dim_b,)), ((), ())), preferred_element_type=F32)


def earlier(size):
    return jnp.where(iota((size, size), 0) < iota((size, size), 1), 1.0, 0.0).astype(BF16)


def add_all(terms):
    while len(terms) > 1:
        paired = [terms[k] + terms[k + 1] for k in range(0, len(terms) - 1, 2)]
        terms = paired + terms[len(terms) - len(terms) % 2 :]
    return terms[0]


def send_kernel(features, weights, neighbours, targets, send, place):
    owners, lanes = [], []
    named = jnp.zeros((FEAT, SLAB), F32)
    for slot in range(FAN + 1):
        index = neighbours[slot] if slot < FAN else targets[...]
        owner = ((index.astype(F32) + 0.5) * (1.0 / OWN)).astype(jnp.int32)
        row = index - owner * OWN
        owner_hot = jnp.where(iota((FEAT, TARGETS), 0) == owner, 1.0, 0.0).astype(BF16)
        row_hot = jnp.where(iota((SLAB, TARGETS), 0) == row, 1.0, 0.0)
        named = named + contract(owner_hot, row_hot.astype(BF16), 1, 1)
        owners.append((owner, owner_hot))
        lanes.append(row_hot)
    marked = jnp.where(named > 0.0, 1.0, 0.0)
    rank = contract(marked.astype(BF16), earlier(SLAB), 1, 0).astype(BF16)
    places = []
    for slot in range(FAN + 1):
        owner, owner_hot = owners[slot]
        mine = jnp.sum(contract(rank, owner_hot, 0, 0) * lanes[slot], axis=0, keepdims=True)
        places.append(owner * UNION + mine.astype(jnp.int32))
    place[...] = jnp.concatenate(places + [jnp.zeros((5, TARGETS), jnp.int32)], axis=0)

    shared = weights[...].astype(F32)
    for pair in range(FEAT // 2):
        block = features[:, pl.ds(pair * 2 * OWN, 2 * OWN)].astype(F32)
        for half in range(2):
            owner = 2 * pair + half
            own = block[:, half * OWN : (half + 1) * OWN]
            marks = marked[owner : owner + 1]
            last = jnp.concatenate(
                [
                    own[24:, 128:],
                    marks[:, :64],
                    marks[:, 64:128],
                    marks[:, 128:192],
                    jnp.zeros((5, 64), F32),
                ],
                axis=0,
            )
            send[owner] = jnp.concatenate(
                [shared, own[:, :128], jnp.concatenate([own[:24, 128:], last], axis=1)], axis=0
            ).astype(BF16)


def gather_kernel(slots, features, send, table, sums):
    def fill(step, carry):
        for part in range(TABLE_STEP):
            at = pl.multiple_of((step * TABLE_STEP + part) * 128, 128)
            block = jnp.concatenate(
                [features[:, pl.ds(at, 128)].astype(F32), jnp.ones((8, 128), F32)], axis=0
            )
            table[pl.ds(at, 128), pl.ds(0, WIDTH + 8)] = block.T
        return carry

    lax.fori_loop(0, INPUTS // 128 // TABLE_STEP, fill, 0)
    table[pl.ds(INPUTS, 8), :] = jnp.zeros((8, 128), F32)

    def owner_step(owner, carry):
        first = owner * OWN

        def block(step, inner):
            at = first + step * UNROLL
            lists = [slots.at[pl.ds(slot * ROWS + at, UNROLL)] for slot in range(FAN)]
            result = sums.at[pl.ds(pl.multiple_of(step * UNROLL, UNROLL), UNROLL), :]
            for row in range(UNROLL):
                result[pl.ds(row, 1), :] = add_all(
                    [table[pl.ds(lists[slot][row], 1), :] for slot in range(FAN)]
                )
            return inner

        lax.fori_loop(0, OWN // UNROLL, block, 0)
        head = sums[pl.ds(0, 128), :].T
        tail = sums[pl.ds(128, 64), :].T
        head = head[:WIDTH] / jnp.maximum(head[WIDTH : WIDTH + 1], 1.0)
        tail = tail[:WIDTH] / jnp.maximum(tail[WIDTH : WIDTH + 1], 1.0)
        last = jnp.concatenate([tail[24:], jnp.zeros((8, 64), F32)], axis=0)
        send[owner] = jnp.concatenate(
            [head, jnp.concatenate([tail[:24], last], axis=1)], axis=0
        ).astype(BF16)
        return carry

    lax.fori_loop(0, FEAT, owner_step, 0)


def hidden_kernel(
    core, mine, theirs, means, bias, hidden, rows, stacked, held, other, marks, chosen
):
    for source in range(FEAT):
        own = mine[source].astype(F32)
        mean = means[source].astype(F32)
        held[pl.ds(source * 80, 80), :] = own[:80].astype(BF16)
        other[pl.ds(source * 80, 80), :] = theirs[source].astype(F32).astype(BF16)
        last, mean_last = own[120:144], mean[40:64]
        stacked[pl.ds(source * 80, 80), pl.ds(0, 128)] = jnp.concatenate(
            [own[80:120], mean[:40]], axis=0
        ).astype(BF16)
        stacked[pl.ds(source * 80, 80), pl.ds(128, 64)] = jnp.concatenate(
            [last[:, :64], last[:16, 64:], mean_last[:, :64], mean_last[:16, 64:]], axis=0
        ).astype(BF16)
        marks[pl.ds(source, 1), :] = jnp.concatenate(
            [last[16:17, 64:], last[17:18, 64:], last[18:19, 64:], jnp.zeros((1, 64), F32)], axis=1
        )
    stacked[:, pl.ds(192, 64)] = jnp.zeros((FEAT * 80, 64), BF16)
    first = contract(stacked[...], held[...], 0, 0)[:OWN]
    second = contract(stacked[...], other[...], 0, 0)[:OWN]
    even = core[0] == 0
    pre = jnp.concatenate(
        [jnp.where(even, first, second), jnp.where(even, second, first)], axis=1
    )
    result = jnp.maximum(pre + bias[...], 0.0).astype(BF16)
    hidden[...] = result
    rank = contract(marks[...].astype(BF16), earlier(SLAB), 1, 0)
    for source in range(FEAT):
        hit = (iota((UNION, SLAB), 0).astype(F32) == rank[source : source + 1]) & (
            marks[pl.ds(source, 1), :] > 0.0
        )
        chosen[pl.ds(source * UNION, UNION), :] = jnp.where(hit, 1.0, 0.0)
    padded = jnp.concatenate([result, jnp.zeros((SLAB - OWN, HIDDEN), BF16)], axis=0)
    rows[...] = contract(chosen[...].astype(BF16), padded, 1, 0).astype(BF16)


def pick_kernel(place, mask, picks):
    spots = iota((FEAT * UNION, TARGETS), 0)
    total = jnp.zeros((FEAT * UNION, TARGETS), F32)
    for slot in range(FAN):
        used = mask[slot].astype(F32)
        total = total + jnp.where(spots == place[pl.ds(slot, 1), :], used, 0.0)
    picks[0] = total.astype(BF16)
    picks[1] = jnp.where(spots == place[pl.ds(FAN, 1), :], 1.0, 0.0).astype(BF16)


def loss_kernel(rows, picks, labels, weights, loss, inputs, wanted, largest, summed, picked):
    step = pl.program_id(0)
    width = weights.shape[2]

    @pl.when(step == 0)
    def _():
        count = contract(picks[0], jnp.ones((FEAT * UNION, 128), BF16), 0, 0)[:, :1]
        agg = contract(picks[0], rows[...], 0, 0) / jnp.maximum(count, 1.0)
        inputs[:, pl.ds(0, HIDDEN)] = contract(picks[1], rows[...], 0, 0).astype(BF16)
        inputs[:, pl.ds(HIDDEN, HIDDEN)] = agg.astype(BF16)
        spread = jnp.broadcast_to(labels[...].astype(F32), (TARGETS, TARGETS)).T
        wanted[...] = spread[:, :1].astype(jnp.int32)
        largest[...] = jnp.full((TARGETS, 1), -jnp.inf, F32)
        summed[...] = jnp.zeros((TARGETS, 1), F32)
        picked[...] = jnp.zeros((TARGETS, 1), F32)

    logits = contract(inputs[...], weights[0], 1, 0)
    before = largest[...]
    now = jnp.maximum(before, jnp.max(logits, axis=1, keepdims=True))
    part = jnp.sum(jnp.exp(logits - now), axis=1, keepdims=True)
    summed[...] = summed[...] * jnp.exp(before - now) + part
    largest[...] = now
    classes = iota((TARGETS, width), 1) + step * width
    picked[...] += jnp.sum(jnp.where(classes == wanted[...], logits, 0.0), axis=1, keepdims=True)

    @pl.when(step == NODE - 1)
    def _():
        column = largest[...] + jnp.log(summed[...]) - picked[...]
        loss[...] = jnp.broadcast_to(column, (TARGETS, TARGETS)).T[:1]


VMEM = pl.BlockSpec(memory_space=pltpu.VMEM)
SMEM = pl.BlockSpec(memory_space=pltpu.SMEM)


def body(
    features,
    first_neighbours,
    first_mask,
    second_neighbours,
    second_mask,
    target_index,
    labels,
    first_weight,
    first_bias,
    class_weight,
):
    slots = jnp.where(first_mask[:, 0, :] > 0, first_neighbours[:, 0, :], INPUTS).reshape(-1)
    core = lax.rem(lax.axis_index("node"), 2).astype(jnp.int32)
    half = lax.dynamic_slice(first_weight, (0, 0, core * 128), (2, WIDTH, 128))
    all_class = lax.all_gather(class_weight, "node", axis=0)
    table = features[:, 0, :]
    own, place = pl.pallas_call(
        send_kernel,
        out_shape=(
            jax.ShapeDtypeStruct((FEAT, 144, 128), BF16),
            jax.ShapeDtypeStruct((16, TARGETS), jnp.int32),
        ),
        grid=(1,),
        in_specs=[
            pl.BlockSpec((WIDTH, ROWS), lambda i: (0, 0)),
            pl.BlockSpec((2 * WIDTH, 128), lambda i: (0, 0)),
            pl.BlockSpec((FAN, 1, TARGETS), lambda i: (0, 0, 0)),
            pl.BlockSpec((1, TARGETS), lambda i: (0, 0)),
        ],
        out_specs=(
            pl.BlockSpec((FEAT, 144, 128), lambda i: (0, 0, 0)),
            pl.BlockSpec((16, TARGETS), lambda i: (0, 0)),
        ),
        compiler_params=pltpu.CompilerParams(vmem_limit_bytes=24 * 2**20),
        cost_estimate=pl.CostEstimate(flops=10**8, bytes_accessed=3 * 10**6, transcendentals=0),
    )(table, half.reshape(2 * WIDTH, 128), second_neighbours, target_index)
    own = lax.all_to_all(own, "feat", 0, 0)
    send = pl.pallas_call(
        gather_kernel,
        out_shape=jax.ShapeDtypeStruct((FEAT, 64, 128), BF16),
        in_specs=[SMEM, VMEM],
        out_specs=VMEM,
        scratch_shapes=[
            pltpu.VMEM((INPUTS + 8, 128), F32),
            pltpu.VMEM((OWN, 128), F32),
        ],
        compiler_params=pltpu.CompilerParams(vmem_limit_bytes=24 * 2**20),
        cost_estimate=pl.CostEstimate(flops=10**9, bytes_accessed=150 * 10**6, transcendentals=0),
    )(slots, table)
    swap = [(device, device ^ 1) for device in range(NODE)]
    theirs = lax.ppermute(own[:, : 2 * WIDTH], "node", swap)
    means = lax.all_to_all(send, "feat", 0, 0)
    hidden, rows = pl.pallas_call(
        hidden_kernel,
        out_shape=(
            jax.ShapeDtypeStruct((OWN, HIDDEN), BF16),
            jax.ShapeDtypeStruct((FEAT * UNION, HIDDEN), BF16),
        ),
        in_specs=[SMEM] + [VMEM] * 4,
        out_specs=(VMEM, VMEM),
        scratch_shapes=[
            pltpu.VMEM((FEAT * 80, 256), BF16),
            pltpu.VMEM((FEAT * 80, 128), BF16),
            pltpu.VMEM((FEAT * 80, 128), BF16),
            pltpu.VMEM((FEAT, SLAB), F32),
            pltpu.VMEM((FEAT * UNION, SLAB), F32),
        ],
        compiler_params=pltpu.CompilerParams(vmem_limit_bytes=24 * 2**20),
    )(core[None], own, theirs, means, first_bias[None, :])
    rows = lax.all_to_all(rows.reshape(FEAT, UNION, HIDDEN), "feat", 0, 0)
    rows = rows.reshape(FEAT * UNION, HIDDEN)
    picks = pl.pallas_call(
        pick_kernel,
        out_shape=jax.ShapeDtypeStruct((2, FEAT * UNION, TARGETS), BF16),
        in_specs=[VMEM] * 2,
        out_specs=VMEM,
        cost_estimate=pl.CostEstimate(flops=10**7, bytes_accessed=4 * 10**6, transcendentals=0),
    )(place, second_mask)
    width = class_weight.shape[1]
    whole = lambda *shape: pl.BlockSpec(shape, lambda i: (0,) * len(shape))
    loss = pl.pallas_call(
        loss_kernel,
        grid=(NODE,),
        out_shape=jax.ShapeDtypeStruct((1, TARGETS), F32),
        in_specs=[
            whole(FEAT * UNION, HIDDEN),
            whole(2, FEAT * UNION, TARGETS),
            whole(1, TARGETS),
            pl.BlockSpec((1, 2 * HIDDEN, width), lambda i: (i, 0, 0)),
        ],
        out_specs=whole(1, TARGETS),
        scratch_shapes=[
            pltpu.VMEM((TARGETS, 2 * HIDDEN), BF16),
            pltpu.VMEM((TARGETS, 1), jnp.int32),
            pltpu.VMEM((TARGETS, 1), F32),
            pltpu.VMEM((TARGETS, 1), F32),
            pltpu.VMEM((TARGETS, 1), F32),
        ],
        compiler_params=pltpu.CompilerParams(vmem_limit_bytes=24 * 2**20),
    )(rows, picks, labels, all_class)
    return (hidden[None], loss)


def solution(mesh):
    placed = (
        P("feat", "node", None),
        P(None, "node", None),
        P(None, "node", None),
        P(None, "node", "feat"),
        P(None, "node", "feat"),
        P("node", "feat"),
        P("node", "feat"),
        P(None, "feat", None),
        P(),
        P(None, "node"),
    )
    return jax.shard_map(
        body,
        mesh=mesh,
        in_specs=placed,
        out_specs=(P("node", "feat", None), P("node", "feat")),
        check_vma=False,
    )
```

```python
import functools

import jax
import jax.numpy as jnp
from jax import lax
from jax.experimental import pallas as pl
from jax.experimental.pallas import tpu as pltpu
from jax.sharding import PartitionSpec as P

FEAT = 32
NODE = 8
WIDTH = 40
INPUTS = 24576
ROWS = 6144
OWN = 192
FAN = 10
TARGETS = 128
HIDDEN = 256
UNION = 24
SLAB = 256
UNROLL = 64
CHUNK = 1024
PAIRS = 4
TABLE_STEP = 8
F32 = jnp.float32
BF16 = jnp.bfloat16


def iota(shape, dim):
    return lax.broadcasted_iota(jnp.int32, shape, dim)


def contract(a, b, dim_a, dim_b):
    return lax.dot_general(a, b, (((dim_a,), (dim_b,)), ((), ())), preferred_element_type=F32)


def earlier(size):
    return jnp.where(iota((size, size), 0) < iota((size, size), 1), 1.0, 0.0).astype(BF16)


def add_all(terms):
    while len(terms) > 1:
        paired = [terms[k] + terms[k + 1] for k in range(0, len(terms) - 1, 2)]
        terms = paired + terms[len(terms) - len(terms) % 2 :]
    return terms[0]


def send_kernel(features, weights, neighbours, targets, send, place):
    owners, lanes = [], []
    named = jnp.zeros((FEAT, SLAB), F32)
    for slot in range(FAN + 1):
        index = neighbours[slot] if slot < FAN else targets[...]
        owner = ((index.astype(F32) + 0.5) * (1.0 / OWN)).astype(jnp.int32)
        row = index - owner * OWN
        owner_hot = jnp.where(iota((FEAT, TARGETS), 0) == owner, 1.0, 0.0).astype(BF16)
        row_hot = jnp.where(iota((SLAB, TARGETS), 0) == row, 1.0, 0.0)
        named = named + contract(owner_hot, row_hot.astype(BF16), 1, 1)
        owners.append((owner, owner_hot))
        lanes.append(row_hot)
    marked = jnp.where(named > 0.0, 1.0, 0.0)
    rank = contract(marked.astype(BF16), earlier(SLAB), 1, 0).astype(BF16)
    places = []
    for slot in range(FAN + 1):
        owner, owner_hot = owners[slot]
        mine = jnp.sum(contract(rank, owner_hot, 0, 0) * lanes[slot], axis=0, keepdims=True)
        places.append(owner * UNION + mine.astype(jnp.int32))
    place[...] = jnp.concatenate(places + [jnp.zeros((5, TARGETS), jnp.int32)], axis=0)

    shared = weights[...].astype(F32)
    for pair in range(FEAT // 2):
        block = features[:, pl.ds(pair * 2 * OWN, 2 * OWN)].astype(F32)
        for half in range(2):
            owner = 2 * pair + half
            marks = [marked[owner : owner + 1, k * 64 : (k + 1) * 64] for k in range(3)]
            last = jnp.concatenate(marks + [jnp.zeros((5, 64), F32)], axis=0)
            send[owner] = jnp.concatenate([shared, folded(block, half, last)], axis=0).astype(BF16)


def folded(block, half, last):
    rest = block[:, 128 + half * 64 : 192 + half * 64]
    rest = jnp.concatenate([rest[:24], jnp.concatenate([rest[24:], last], axis=0)], axis=1)
    return jnp.concatenate([block[:, half * 256 : half * 256 + 128], rest], axis=0)


def mean_of(flipped):
    thirds = [flipped[t * WIDTH : (t + 1) * WIDTH] for t in range(3)]
    return (thirds[0] + thirds[1] + thirds[2]) / jnp.maximum(flipped[3 * WIDTH : 3 * WIDTH + 1], 1.0)


def gather_kernel(slots, features, send, table, sums, lists, arrived):
    def fetch(chunk):
        span = pl.ds(pl.multiple_of(chunk * FAN * CHUNK, FAN * CHUNK), FAN * CHUNK)
        return pltpu.make_async_copy(slots.at[span], lists.at[span], arrived.at[chunk])

    for chunk in range(ROWS // CHUNK):
        fetch(chunk).start()

    lane = iota((128, 128), 1)
    third = INPUTS // 3

    def fill(step, carry):
        for part in range(TABLE_STEP):
            at = pl.multiple_of((step * TABLE_STEP + part) * 128, 128)
            blocks = [features[:, pl.ds(t * third + at, 128)].astype(F32) for t in range(3)]
            flipped = jnp.concatenate(blocks + [jnp.ones((8, 128), F32)], axis=0).T
            for t in range(3):
                kept = ((lane >= t * WIDTH) & (lane < (t + 1) * WIDTH)) | (lane >= 3 * WIDTH)
                table[pl.ds(t * third + at, 128), :] = jnp.where(kept, flipped, 0.0)
        return carry

    lax.fori_loop(0, third // 128 // TABLE_STEP, fill, 0)
    table[pl.ds(INPUTS, 8), :] = jnp.zeros((8, 128), F32)

    def chunk_step(chunk, carry):
        fetch(chunk).wait()

        def block(step, inner):
            first = chunk * FAN * CHUNK + step * UNROLL
            named = [lists.at[pl.ds(first + slot * CHUNK, UNROLL)] for slot in range(FAN)]
            at = pl.multiple_of(chunk * CHUNK + step * UNROLL, UNROLL)
            result = sums.at[pl.ds(at, UNROLL), :]
            for row in range(UNROLL):
                result[pl.ds(row, 1), :] = add_all(
                    [table[pl.ds(named[slot][row], 1), :] for slot in range(FAN)]
                )
            return inner

        return lax.fori_loop(0, CHUNK // UNROLL, block, carry)

    lax.fori_loop(0, ROWS // CHUNK, chunk_step, 0)

    def pair_step(step, carry):
        for part in range(PAIRS):
            pair = step * PAIRS + part
            at = pl.multiple_of(pair * 2 * OWN, 128)
            means = [mean_of(sums[pl.ds(at + k * 128, 128), :].T) for k in range(3)]
            block = jnp.concatenate(means, axis=1)
            for half in range(2):
                send[2 * pair + half] = folded(block, half, jnp.zeros((8, 64), F32)).astype(BF16)
        return carry

    lax.fori_loop(0, FEAT // 2 // PAIRS, pair_step, 0)


def hidden_kernel(
    spot, mine, theirs, means, bias, hidden, rows, stacked, held, other, marks, chosen
):
    for source in range(FEAT):
        own = mine[source].astype(F32)
        mean = means[source].astype(F32)
        held[pl.ds(source * 80, 80), :] = own[:80].astype(BF16)
        other[pl.ds(source * 80, 80), :] = theirs[source].astype(F32).astype(BF16)
        last, mean_last = own[120:144], mean[40:64]
        stacked[pl.ds(source * 80, 80), pl.ds(0, 128)] = jnp.concatenate(
            [own[80:120], mean[:40]], axis=0
        ).astype(BF16)
        stacked[pl.ds(source * 80, 80), pl.ds(128, 64)] = jnp.concatenate(
            [last[:, :64], last[:16, 64:], mean_last[:, :64], mean_last[:16, 64:]], axis=0
        ).astype(BF16)
        marks[pl.ds(source, 1), :] = jnp.concatenate(
            [last[16:17, 64:], last[17:18, 64:], last[18:19, 64:], jnp.zeros((1, 64), F32)], axis=1
        )
    stacked[:, pl.ds(192, 64)] = jnp.zeros((FEAT * 80, 64), BF16)
    first = contract(stacked[...], held[...], 0, 0)[:OWN]
    second = contract(stacked[...], other[...], 0, 0)[:OWN]
    even = spot[0] == 0
    pre = jnp.concatenate(
        [jnp.where(even, first, second), jnp.where(even, second, first)], axis=1
    )
    pre = jnp.where(spot[1] == 0, pre, jnp.concatenate([pre[128:], pre[:128]], axis=0))
    result = jnp.maximum(pre + bias[...], 0.0).astype(BF16)
    hidden[...] = result
    rank = contract(marks[...].astype(BF16), earlier(SLAB), 1, 0)
    for source in range(FEAT):
        hit = (iota((UNION, SLAB), 0).astype(F32) == rank[source : source + 1]) & (
            marks[pl.ds(source, 1), :] > 0.0
        )
        chosen[pl.ds(source * UNION, UNION), :] = jnp.where(hit, 1.0, 0.0)
    padded = jnp.concatenate([result, jnp.zeros((SLAB - OWN, HIDDEN), BF16)], axis=0)
    rows[...] = contract(chosen[...].astype(BF16), padded, 1, 0).astype(BF16)


def pick_kernel(place, mask, picks):
    spots = iota((FEAT * UNION, TARGETS), 0)
    total = jnp.zeros((FEAT * UNION, TARGETS), F32)
    for slot in range(FAN):
        used = mask[slot].astype(F32)
        total = total + jnp.where(spots == place[pl.ds(slot, 1), :], used, 0.0)
    picks[0] = total.astype(BF16)
    picks[1] = jnp.where(spots == place[pl.ds(FAN, 1), :], 1.0, 0.0).astype(BF16)


def loss_kernel(rows, picks, labels, weights, loss, inputs, logits):
    count = contract(picks[0], jnp.ones((FEAT * UNION, 128), BF16), 0, 0)[:, :1]
    agg = contract(picks[0], rows[...], 0, 0) / jnp.maximum(count, 1.0)
    inputs[:, pl.ds(0, HIDDEN)] = contract(picks[1], rows[...], 0, 0).astype(BF16)
    inputs[:, pl.ds(HIDDEN, HIDDEN)] = agg.astype(BF16)
    offset = (
        jnp.broadcast_to(labels[...].astype(F32), (TARGETS, TARGETS)).T.astype(jnp.int32)
        - iota((TARGETS, TARGETS), 1)
    )
    width = weights.shape[2]
    largest = jnp.full((TARGETS, TARGETS), -jnp.inf, F32)
    summed = jnp.zeros((TARGETS, TARGETS), F32)
    picked = jnp.zeros((TARGETS, TARGETS), F32)
    for step in range(NODE + 1):
        if step < NODE:
            logits[step % 2] = contract(inputs[...], weights[step], 1, 0)
        if step > 0:
            spans = [pl.ds(k * 128, 128) for k in range(width // 128)]
            held = logits.at[(step - 1) % 2]
            now = largest
            for span in spans:
                now = jnp.maximum(now, held[:, span])
            summed = summed * jnp.exp(largest - now)
            for k, span in enumerate(spans):
                part = held[:, span]
                summed = summed + jnp.exp(part - now)
                picked = picked + jnp.where(offset == (step - 1) * width + k * 128, part, 0.0)
            largest = now
    most = jnp.max(largest, axis=1, keepdims=True)
    total = jnp.sum(summed * jnp.exp(largest - most), axis=1, keepdims=True)
    column = most + jnp.log(total) - jnp.sum(picked, axis=1, keepdims=True)
    loss[...] = jnp.broadcast_to(column, (TARGETS, TARGETS)).T[:1]


VMEM = pl.BlockSpec(memory_space=pltpu.VMEM)
SMEM = pl.BlockSpec(memory_space=pltpu.SMEM)


def call_gather(slots, table):
    return pl.pallas_call(
        gather_kernel,
        out_shape=jax.ShapeDtypeStruct((FEAT, 64, 128), BF16),
        in_specs=[pl.BlockSpec(memory_space=pl.ANY), VMEM],
        out_specs=VMEM,
        scratch_shapes=[
            pltpu.VMEM((INPUTS + 8, 128), F32),
            pltpu.VMEM((ROWS, 128), F32),
            pltpu.SMEM((FAN * ROWS,), jnp.int32),
            pltpu.SemaphoreType.DMA((ROWS // CHUNK,)),
        ],
        compiler_params=pltpu.CompilerParams(vmem_limit_bytes=24 * 2**20),
        cost_estimate=pl.CostEstimate(flops=10**9, bytes_accessed=150 * 10**6, transcendentals=0),
    )(slots, table)


def call_loss(rows, picks, labels, weights):
    return pl.pallas_call(
        loss_kernel,
        out_shape=jax.ShapeDtypeStruct((1, TARGETS), F32),
        in_specs=[VMEM] * 4,
        out_specs=VMEM,
        scratch_shapes=[
            pltpu.VMEM((TARGETS, 2 * HIDDEN), BF16),
            pltpu.VMEM((2, TARGETS, weights.shape[2]), F32),
        ],
        compiler_params=pltpu.CompilerParams(vmem_limit_bytes=24 * 2**20),
    )(rows, picks, labels, weights)


def body(
    features,
    first_neighbours,
    first_mask,
    second_neighbours,
    second_mask,
    target_index,
    labels,
    first_weight,
    first_bias,
    class_weight,
):
    slots = jnp.where(first_mask[:, 0, :] > 0, first_neighbours[:, 0, :], INPUTS)
    slots = slots.reshape(FAN, ROWS // CHUNK, CHUNK).transpose(1, 0, 2).reshape(-1)
    core = lax.rem(lax.axis_index("node"), 2).astype(jnp.int32)
    half = lax.dynamic_slice(first_weight, (0, 0, core * 128), (2, WIDTH, 128))
    all_class = lax.all_gather(class_weight, "node", axis=0)
    table = features[:, 0, :]
    own, place = pl.pallas_call(
        send_kernel,
        out_shape=(
            jax.ShapeDtypeStruct((FEAT, 144, 128), BF16),
            jax.ShapeDtypeStruct((16, TARGETS), jnp.int32),
        ),
        grid=(1,),
        in_specs=[
            pl.BlockSpec((WIDTH, ROWS), lambda i: (0, 0)),
            pl.BlockSpec((2 * WIDTH, 128), lambda i: (0, 0)),
            pl.BlockSpec((FAN, 1, TARGETS), lambda i: (0, 0, 0)),
            pl.BlockSpec((1, TARGETS), lambda i: (0, 0)),
        ],
        out_specs=(
            pl.BlockSpec((FEAT, 144, 128), lambda i: (0, 0, 0)),
            pl.BlockSpec((16, TARGETS), lambda i: (0, 0)),
        ),
        compiler_params=pltpu.CompilerParams(vmem_limit_bytes=24 * 2**20),
        cost_estimate=pl.CostEstimate(flops=10**8, bytes_accessed=3 * 10**6, transcendentals=0),
    )(table, half.reshape(2 * WIDTH, 128), second_neighbours, target_index)
    own = lax.all_to_all(own, "feat", 0, 0)
    send = call_gather(slots, table)
    swap = [(device, device ^ 1) for device in range(NODE)]
    theirs = lax.ppermute(own[:, : 2 * WIDTH], "node", swap)
    means = lax.all_to_all(send, "feat", 0, 0)
    means, all_class = lax.optimization_barrier((means, all_class))
    spot = jnp.stack([core, lax.rem(lax.axis_index("feat"), 2).astype(jnp.int32)])
    hidden, rows = pl.pallas_call(
        hidden_kernel,
        out_shape=(
            jax.ShapeDtypeStruct((OWN, HIDDEN), BF16),
            jax.ShapeDtypeStruct((FEAT * UNION, HIDDEN), BF16),
        ),
        in_specs=[SMEM] + [VMEM] * 4,
        out_specs=(VMEM, VMEM),
        scratch_shapes=[
            pltpu.VMEM((FEAT * 80, 256), BF16),
            pltpu.VMEM((FEAT * 80, 128), BF16),
            pltpu.VMEM((FEAT * 80, 128), BF16),
            pltpu.VMEM((FEAT, SLAB), F32),
            pltpu.VMEM((FEAT * UNION, SLAB), F32),
        ],
        compiler_params=pltpu.CompilerParams(vmem_limit_bytes=24 * 2**20),
    )(spot, own, theirs, means, first_bias[None, :])
    rows = lax.all_to_all(rows.reshape(FEAT, UNION, HIDDEN), "feat", 0, 0)
    rows = rows.reshape(FEAT * UNION, HIDDEN)
    picks = pl.pallas_call(
        pick_kernel,
        out_shape=jax.ShapeDtypeStruct((2, FEAT * UNION, TARGETS), BF16),
        in_specs=[VMEM] * 2,
        out_specs=VMEM,
        cost_estimate=pl.CostEstimate(flops=10**7, bytes_accessed=4 * 10**6, transcendentals=0),
    )(place, second_mask)
    loss = call_loss(rows, picks, labels, all_class)
    return (hidden[None], loss)


def solution(mesh):
    placed = (
        P("feat", "node", None),
        P(None, "node", None),
        P(None, "node", None),
        P(None, "node", "feat"),
        P(None, "node", "feat"),
        P("node", "feat"),
        P("node", "feat"),
        P(None, "feat", None),
        P(),
        P(None, "node"),
    )
    return jax.shard_map(
        body,
        mesh=mesh,
        in_specs=placed,
        out_specs=(P("node", "feat", None), P("node", "feat")),
        check_vma=False,
    )
```

```python
import functools

import jax
import jax.numpy as jnp
from jax import lax
from jax.experimental import pallas as pl
from jax.experimental.pallas import tpu as pltpu
from jax.sharding import PartitionSpec as P

FEAT = 32
NODE = 8
WIDTH = 40
INPUTS = 24576
ROWS = 6144
OWN = 192
FAN = 10
TARGETS = 128
HIDDEN = 256
UNION = 24
SLAB = 256
UNROLL = 64
LEAST = 3
LINES = ROWS // 128
CHUNK = 1024
PAIRS = 4
TABLE_STEP = 8
F32 = jnp.float32
BF16 = jnp.bfloat16


def iota(shape, dim):
    return lax.broadcasted_iota(jnp.int32, shape, dim)


def contract(a, b, dim_a, dim_b):
    return lax.dot_general(a, b, (((dim_a,), (dim_b,)), ((), ())), preferred_element_type=F32)


def earlier(size):
    return jnp.where(iota((size, size), 0) < iota((size, size), 1), 1.0, 0.0).astype(BF16)


def add_all(terms):
    while len(terms) > 1:
        paired = [terms[k] + terms[k + 1] for k in range(0, len(terms) - 1, 2)]
        terms = paired + terms[len(terms) - len(terms) % 2 :]
    return terms[0]


def send_kernel(features, weights, neighbours, targets, send, place):
    owners, lanes = [], []
    named = jnp.zeros((FEAT, SLAB), F32)
    for slot in range(FAN + 1):
        index = neighbours[slot] if slot < FAN else targets[...]
        owner = ((index.astype(F32) + 0.5) * (1.0 / OWN)).astype(jnp.int32)
        row = index - owner * OWN
        owner_hot = jnp.where(iota((FEAT, TARGETS), 0) == owner, 1.0, 0.0).astype(BF16)
        row_hot = jnp.where(iota((SLAB, TARGETS), 0) == row, 1.0, 0.0)
        named = named + contract(owner_hot, row_hot.astype(BF16), 1, 1)
        owners.append((owner, owner_hot))
        lanes.append(row_hot)
    marked = jnp.where(named > 0.0, 1.0, 0.0)
    rank = contract(marked.astype(BF16), earlier(SLAB), 1, 0).astype(BF16)
    places = []
    for slot in range(FAN + 1):
        owner, owner_hot = owners[slot]
        mine = jnp.sum(contract(rank, owner_hot, 0, 0) * lanes[slot], axis=0, keepdims=True)
        places.append(owner * UNION + mine.astype(jnp.int32))
    place[...] = jnp.concatenate(places + [jnp.zeros((5, TARGETS), jnp.int32)], axis=0)

    shared = weights[...].astype(F32)
    for pair in range(FEAT // 2):
        block = features[:, pl.ds(pair * 2 * OWN, 2 * OWN)].astype(F32)
        for half in range(2):
            owner = 2 * pair + half
            marks = [marked[owner : owner + 1, k * 64 : (k + 1) * 64] for k in range(3)]
            last = jnp.concatenate(marks + [jnp.zeros((5, 64), F32)], axis=0)
            send[owner] = jnp.concatenate([shared, folded(block, half, last)], axis=0).astype(BF16)


def folded(block, half, last):
    rest = block[:, 128 + half * 64 : 192 + half * 64]
    rest = jnp.concatenate([rest[:24], jnp.concatenate([rest[24:], last], axis=0)], axis=1)
    return jnp.concatenate([block[:, half * 256 : half * 256 + 128], rest], axis=0)


def order_kernel(neighbours, mask, lists, ranks, columns):
    used = [jnp.where(mask[slot] > 0, 1, 0) for slot in range(FAN)]
    before = [jnp.zeros((LINES, 128), jnp.int32)]
    for slot in range(FAN):
        before.append(before[slot] + used[slot])
    count = before[FAN]
    for place in range(FAN):
        node = jnp.where(count > place, 0, INPUTS)
        for slot in range(place, FAN):
            here = (used[slot] > 0) & (before[slot] == place)
            node = node + jnp.where(here, neighbours[slot], 0)
        high = node >> 8
        columns[place] = high.astype(F32)
        columns[16 + place] = (node - high * 256).astype(F32)
    columns[FAN] = jnp.zeros((LINES, 128), F32)
    columns[16 + FAN] = count.astype(F32)
    hot = [jnp.where(count == amount, 1.0, 0.0) for amount in range(FAN + 1)]
    stacked = jnp.concatenate(hot, axis=0).astype(BF16)
    second = iota(((FAN + 1) * LINES, 128), 0) % 2 == 1
    earlier_same = contract(stacked, earlier(128), 1, 0)
    all_same = contract(stacked, jnp.ones((128, 128), BF16), 1, 0)
    above = pltpu.roll(all_same, 1, 0)
    below = pltpu.roll(all_same, (FAN + 1) * LINES - 1, 0)
    earlier_same = earlier_same + jnp.where(second, above, 0.0)
    all_same = all_same + jnp.where(second, above, below)
    rank = jnp.zeros((LINES, 128), F32)
    higher = jnp.zeros((LINES, 128), F32)
    for amount in reversed(range(FAN + 1)):
        span = slice(amount * LINES, (amount + 1) * LINES)
        rank = rank + hot[amount] * (earlier_same[span] + higher)
        higher = higher + all_same[span]
    ranks[...] = rank.astype(jnp.int32)
    for line in range(0, LINES, 2):
        part = contract(columns[:, line, :].astype(BF16), moved(ranks, line), 1, 1)
        part += contract(columns[:, line + 1, :].astype(BF16), moved(ranks, line + 1), 1, 1)
        part = (part[:16] * 256.0 + part[16:]).astype(jnp.int32)
        first = line // 8 * 8 * (FAN + 1) + line % 8
        for half in range(2):
            here = part[: FAN + 1, half * 128 : (half + 1) * 128]
            lists[pl.ds(first + half, FAN + 1, stride=8), :] = here


def moved(ranks, line):
    return jnp.where(iota((256, 128), 0) == ranks[pl.ds(line, 1), :], 1.0, 0.0).astype(BF16)


def mean_of(flipped):
    thirds = [flipped[t * WIDTH : (t + 1) * WIDTH] for t in range(3)]
    return (thirds[0] + thirds[1] + thirds[2]) / jnp.maximum(flipped[3 * WIDTH : 3 * WIDTH + 1], 1.0)


def gather_kernel(slots, ranks, features, send, table, sums, lists, arrived):
    size = (FAN + 1) * CHUNK

    def fetch(chunk):
        span = pl.ds(pl.multiple_of(chunk * size, size), size)
        return pltpu.make_async_copy(slots.at[span], lists.at[span], arrived.at[chunk])

    for chunk in range(ROWS // CHUNK):
        fetch(chunk).start()

    lane = iota((128, 128), 1)
    third = INPUTS // 3

    def fill(step, carry):
        for part in range(TABLE_STEP):
            at = pl.multiple_of((step * TABLE_STEP + part) * 128, 128)
            blocks = [features[:, pl.ds(t * third + at, 128)].astype(F32) for t in range(3)]
            flipped = jnp.concatenate(blocks + [jnp.ones((8, 128), F32)], axis=0).T
            for t in range(3):
                kept = ((lane >= t * WIDTH) & (lane < (t + 1) * WIDTH)) | (lane >= 3 * WIDTH)
                table[pl.ds(t * third + at, 128), :] = jnp.where(kept, flipped, 0.0)
        return carry

    lax.fori_loop(0, third // 128 // TABLE_STEP, fill, 0)
    table[pl.ds(INPUTS, 8), :] = jnp.zeros((8, 128), F32)

    def chunk_step(chunk, carry):
        fetch(chunk).wait()

        def block(step, inner):
            first = chunk * size + step * UNROLL
            at = pl.multiple_of(chunk * CHUNK + step * UNROLL, UNROLL)
            result = sums.at[pl.ds(at, UNROLL), :]

            def add(depth):
                named = [lists.at[pl.ds(first + slot * CHUNK, UNROLL)] for slot in range(depth)]
                for row in range(UNROLL):
                    result[pl.ds(row, 1), :] = add_all(
                        [table[pl.ds(named[slot][row], 1), :] for slot in range(depth)]
                    )

            def choose(low, high):
                if low == high:
                    add(low)
                    return
                middle = (low + high) // 2
                lax.cond(
                    deepest <= middle,
                    lambda: choose(low, middle),
                    lambda: choose(middle + 1, high),
                )

            deepest = lists[first + FAN * CHUNK]
            choose(LEAST, FAN)
            return inner

        return lax.fori_loop(0, CHUNK // UNROLL, block, carry)

    lax.fori_loop(0, ROWS // CHUNK, chunk_step, 0)

    def pair_step(step, carry):
        for part in range(0, PAIRS, 2):
            line = (step * PAIRS + part) * 3
            blocks = []
            for k in range(0, 6, 2):
                at = pl.multiple_of((line + k) * 128, 128)
                means = [mean_of(sums[pl.ds(at + half * 128, 128), :].T) for half in range(2)]
                means = jnp.concatenate(means, axis=1).astype(BF16)
                for half in range(2):
                    blocks.append(contract(means, moved(ranks, line + k + half), 1, 0))
            for pair in range(2):
                block = jnp.concatenate(blocks[pair * 3 : pair * 3 + 3], axis=1)
                owner = 2 * (step * PAIRS + part + pair)
                for half in range(2):
                    tile = folded(block, half, jnp.zeros((8, 64), F32))
                    send[owner + half] = tile.astype(BF16)
        return carry

    lax.fori_loop(0, FEAT // 2 // PAIRS, pair_step, 0)


def hidden_kernel(
    spot, mine, theirs, means, bias, hidden, rows, stacked, held, other, marks, chosen
):
    for source in range(FEAT):
        own = mine[source].astype(F32)
        mean = means[source].astype(F32)
        held[pl.ds(source * 80, 80), :] = own[:80].astype(BF16)
        other[pl.ds(source * 80, 80), :] = theirs[source].astype(F32).astype(BF16)
        last, mean_last = own[120:144], mean[40:64]
        stacked[pl.ds(source * 80, 80), pl.ds(0, 128)] = jnp.concatenate(
            [own[80:120], mean[:40]], axis=0
        ).astype(BF16)
        stacked[pl.ds(source * 80, 80), pl.ds(128, 64)] = jnp.concatenate(
            [last[:, :64], last[:16, 64:], mean_last[:, :64], mean_last[:16, 64:]], axis=0
        ).astype(BF16)
        marks[pl.ds(source, 1), :] = jnp.concatenate(
            [last[16:17, 64:], last[17:18, 64:], last[18:19, 64:], jnp.zeros((1, 64), F32)], axis=1
        )
    stacked[:, pl.ds(192, 64)] = jnp.zeros((FEAT * 80, 64), BF16)
    first = contract(stacked[...], held[...], 0, 0)[:OWN]
    second = contract(stacked[...], other[...], 0, 0)[:OWN]
    even = spot[0] == 0
    pre = jnp.concatenate(
        [jnp.where(even, first, second), jnp.where(even, second, first)], axis=1
    )
    pre = jnp.where(spot[1] == 0, pre, jnp.concatenate([pre[128:], pre[:128]], axis=0))
    result = jnp.maximum(pre + bias[...], 0.0).astype(BF16)
    hidden[...] = result
    rank = contract(marks[...].astype(BF16), earlier(SLAB), 1, 0)
    for source in range(FEAT):
        hit = (iota((UNION, SLAB), 0).astype(F32) == rank[source : source + 1]) & (
            marks[pl.ds(source, 1), :] > 0.0
        )
        chosen[pl.ds(source * UNION, UNION), :] = jnp.where(hit, 1.0, 0.0)
    padded = jnp.concatenate([result, jnp.zeros((SLAB - OWN, HIDDEN), BF16)], axis=0)
    rows[...] = contract(chosen[...].astype(BF16), padded, 1, 0).astype(BF16)


def pick_kernel(place, mask, picks):
    spots = iota((FEAT * UNION, TARGETS), 0)
    total = jnp.zeros((FEAT * UNION, TARGETS), F32)
    for slot in range(FAN):
        used = mask[slot].astype(F32)
        total = total + jnp.where(spots == place[pl.ds(slot, 1), :], used, 0.0)
    picks[0] = total.astype(BF16)
    picks[1] = jnp.where(spots == place[pl.ds(FAN, 1), :], 1.0, 0.0).astype(BF16)


def loss_kernel(rows, picks, labels, weights, loss, inputs, logits, held, arrived):
    copies = [
        pltpu.make_async_copy(weights.at[k], held.at[k], arrived.at[k]) for k in range(NODE)
    ]
    for copy in copies:
        copy.start()
    count = contract(picks[0], jnp.ones((FEAT * UNION, 128), BF16), 0, 0)[:, :1]
    agg = contract(picks[0], rows[...], 0, 0) / jnp.maximum(count, 1.0)
    inputs[:, pl.ds(0, HIDDEN)] = contract(picks[1], rows[...], 0, 0).astype(BF16)
    inputs[:, pl.ds(HIDDEN, HIDDEN)] = agg.astype(BF16)
    offset = (
        jnp.broadcast_to(labels[...].astype(F32), (TARGETS, TARGETS)).T.astype(jnp.int32)
        - iota((TARGETS, TARGETS), 1)
    )
    width = weights.shape[2]
    largest = jnp.full((TARGETS, TARGETS), -jnp.inf, F32)
    summed = jnp.zeros((TARGETS, TARGETS), F32)
    picked = jnp.zeros((TARGETS, TARGETS), F32)
    for step in range(NODE + 1):
        if step < NODE:
            copies[step].wait()
            logits[step % 2] = contract(inputs[...], held[step], 1, 0)
        if step > 0:
            spans = [pl.ds(k * 128, 128) for k in range(width // 128)]
            last = logits.at[(step - 1) % 2]
            now = largest
            for span in spans:
                now = jnp.maximum(now, last[:, span])
            summed = summed * jnp.exp(largest - now)
            for k, span in enumerate(spans):
                part = last[:, span]
                summed = summed + jnp.exp(part - now)
                picked = picked + jnp.where(offset == (step - 1) * width + k * 128, part, 0.0)
            largest = now
    most = jnp.max(largest, axis=1, keepdims=True)
    total = jnp.sum(summed * jnp.exp(largest - most), axis=1, keepdims=True)
    column = most + jnp.log(total) - jnp.sum(picked, axis=1, keepdims=True)
    loss[...] = jnp.broadcast_to(column, (TARGETS, TARGETS)).T[:1]


VMEM = pl.BlockSpec(memory_space=pltpu.VMEM)
SMEM = pl.BlockSpec(memory_space=pltpu.SMEM)


def call_order(neighbours, mask):
    return pl.pallas_call(
        order_kernel,
        out_shape=(
            jax.ShapeDtypeStruct((LINES * (FAN + 1), 128), jnp.int32),
            jax.ShapeDtypeStruct((LINES, 128), jnp.int32),
        ),
        in_specs=[VMEM, VMEM],
        out_specs=(VMEM, VMEM),
        scratch_shapes=[pltpu.VMEM((32, LINES, 128), F32)],
        compiler_params=pltpu.CompilerParams(vmem_limit_bytes=24 * 2**20),
        cost_estimate=pl.CostEstimate(flops=10**8, bytes_accessed=10**7, transcendentals=0),
    )(neighbours.reshape(FAN, LINES, 128), mask.reshape(FAN, LINES, 128))


def call_gather(slots, ranks, table):
    return pl.pallas_call(
        gather_kernel,
        out_shape=jax.ShapeDtypeStruct((FEAT, 64, 128), BF16),
        in_specs=[pl.BlockSpec(memory_space=pl.ANY), VMEM, VMEM],
        out_specs=VMEM,
        scratch_shapes=[
            pltpu.VMEM((INPUTS + 8, 128), F32),
            pltpu.VMEM((ROWS, 128), F32),
            pltpu.SMEM(((FAN + 1) * ROWS,), jnp.int32),
            pltpu.SemaphoreType.DMA((ROWS // CHUNK,)),
        ],
        compiler_params=pltpu.CompilerParams(vmem_limit_bytes=24 * 2**20),
        cost_estimate=pl.CostEstimate(flops=10**9, bytes_accessed=150 * 10**6, transcendentals=0),
    )(slots, ranks, table)


def call_loss(rows, picks, labels, weights):
    return pl.pallas_call(
        loss_kernel,
        out_shape=jax.ShapeDtypeStruct((1, TARGETS), F32),
        in_specs=[VMEM] * 3 + [pl.BlockSpec(memory_space=pl.ANY)],
        out_specs=VMEM,
        scratch_shapes=[
            pltpu.VMEM((TARGETS, 2 * HIDDEN), BF16),
            pltpu.VMEM((2, TARGETS, weights.shape[2]), F32),
            pltpu.VMEM(weights.shape, BF16),
            pltpu.SemaphoreType.DMA((NODE,)),
        ],
        compiler_params=pltpu.CompilerParams(vmem_limit_bytes=56 * 2**20),
    )(rows, picks, labels, weights)


def body(
    features,
    first_neighbours,
    first_mask,
    second_neighbours,
    second_mask,
    target_index,
    labels,
    first_weight,
    first_bias,
    class_weight,
):
    core = lax.rem(lax.axis_index("node"), 2).astype(jnp.int32)
    half = lax.dynamic_slice(first_weight, (0, 0, core * 128), (2, WIDTH, 128))
    all_class = lax.all_gather(class_weight, "node", axis=0)
    table = features[:, 0, :]
    own, place = pl.pallas_call(
        send_kernel,
        out_shape=(
            jax.ShapeDtypeStruct((FEAT, 144, 128), BF16),
            jax.ShapeDtypeStruct((16, TARGETS), jnp.int32),
        ),
        grid=(1,),
        in_specs=[
            pl.BlockSpec((WIDTH, ROWS), lambda i: (0, 0)),
            pl.BlockSpec((2 * WIDTH, 128), lambda i: (0, 0)),
            pl.BlockSpec((FAN, 1, TARGETS), lambda i: (0, 0, 0)),
            pl.BlockSpec((1, TARGETS), lambda i: (0, 0)),
        ],
        out_specs=(
            pl.BlockSpec((FEAT, 144, 128), lambda i: (0, 0, 0)),
            pl.BlockSpec((16, TARGETS), lambda i: (0, 0)),
        ),
        compiler_params=pltpu.CompilerParams(vmem_limit_bytes=24 * 2**20),
        cost_estimate=pl.CostEstimate(flops=10**8, bytes_accessed=3 * 10**6, transcendentals=0),
    )(table, half.reshape(2 * WIDTH, 128), second_neighbours, target_index)
    own = lax.all_to_all(own, "feat", 0, 0)
    slots, ranks = call_order(first_neighbours, first_mask)
    send = call_gather(slots.reshape(-1), ranks, table)
    swap = [(device, device ^ 1) for device in range(NODE)]
    theirs = lax.ppermute(own[:, : 2 * WIDTH], "node", swap)
    means = lax.all_to_all(send, "feat", 0, 0)
    means, all_class = lax.optimization_barrier((means, all_class))
    spot = jnp.stack([core, lax.rem(lax.axis_index("feat"), 2).astype(jnp.int32)])
    hidden, rows = pl.pallas_call(
        hidden_kernel,
        out_shape=(
            jax.ShapeDtypeStruct((OWN, HIDDEN), BF16),
            jax.ShapeDtypeStruct((FEAT * UNION, HIDDEN), BF16),
        ),
        in_specs=[SMEM] + [VMEM] * 4,
        out_specs=(VMEM, VMEM),
        scratch_shapes=[
            pltpu.VMEM((FEAT * 80, 256), BF16),
            pltpu.VMEM((FEAT * 80, 128), BF16),
            pltpu.VMEM((FEAT * 80, 128), BF16),
            pltpu.VMEM((FEAT, SLAB), F32),
            pltpu.VMEM((FEAT * UNION, SLAB), F32),
        ],
        compiler_params=pltpu.CompilerParams(vmem_limit_bytes=24 * 2**20),
    )(spot, own, theirs, means, first_bias[None, :])
    rows = lax.all_to_all(rows.reshape(FEAT, UNION, HIDDEN), "feat", 0, 0)
    rows = rows.reshape(FEAT * UNION, HIDDEN)
    picks = pl.pallas_call(
        pick_kernel,
        out_shape=jax.ShapeDtypeStruct((2, FEAT * UNION, TARGETS), BF16),
        in_specs=[VMEM] * 2,
        out_specs=VMEM,
        cost_estimate=pl.CostEstimate(flops=10**7, bytes_accessed=4 * 10**6, transcendentals=0),
    )(place, second_mask)
    loss = call_loss(rows, picks, labels, all_class)
    return (hidden[None], loss)


def solution(mesh):
    placed = (
        P("feat", "node", None),
        P(None, "node", None),
        P(None, "node", None),
        P(None, "node", "feat"),
        P(None, "node", "feat"),
        P("node", "feat"),
        P("node", "feat"),
        P(None, "feat", None),
        P(),
        P(None, "node"),
    )
    return jax.shard_map(
        body,
        mesh=mesh,
        in_specs=placed,
        out_specs=(P("node", "feat", None), P("node", "feat")),
        check_vma=False,
    )
```

```python
import functools

import jax
import jax.numpy as jnp
from jax import lax
from jax.experimental import pallas as pl
from jax.experimental.pallas import tpu as pltpu
from jax.sharding import PartitionSpec as P

FEAT = 32
NODE = 8
WIDTH = 40
INPUTS = 24576
ROWS = 6144
OWN = 192
FAN = 10
TARGETS = 128
HIDDEN = 256
UNION = 24
SLAB = 256
UNROLL = 64
LEAST = 3
LINES = ROWS // 128
CHUNK = 1024
PAIRS = 4
TABLE_STEP = 8
STAGED = [(0, 0), (1, 0), (2, 0), (3, 0), (3, 256), (4, 0), (5, 0), (6, 0), (7, 0), (7, 256)]
F32 = jnp.float32
BF16 = jnp.bfloat16


def iota(shape, dim):
    return lax.broadcasted_iota(jnp.int32, shape, dim)


def contract(a, b, dim_a, dim_b):
    return lax.dot_general(a, b, (((dim_a,), (dim_b,)), ((), ())), preferred_element_type=F32)


def earlier(size):
    return jnp.where(iota((size, size), 0) < iota((size, size), 1), 1.0, 0.0).astype(BF16)


def add_all(terms):
    while len(terms) > 1:
        paired = [terms[k] + terms[k + 1] for k in range(0, len(terms) - 1, 2)]
        terms = paired + terms[len(terms) - len(terms) % 2 :]
    return terms[0]


def send_kernel(features, weights, neighbours, targets, send, place, built, sent):
    owners, lanes = [], []
    named = jnp.zeros((FEAT, SLAB), F32)
    for slot in range(FAN + 1):
        index = neighbours[slot] if slot < FAN else targets[...]
        owner = ((index.astype(F32) + 0.5) * (1.0 / OWN)).astype(jnp.int32)
        row = index - owner * OWN
        owner_hot = jnp.where(iota((FEAT, TARGETS), 0) == owner, 1.0, 0.0).astype(BF16)
        row_hot = jnp.where(iota((SLAB, TARGETS), 0) == row, 1.0, 0.0)
        named = named + contract(owner_hot, row_hot.astype(BF16), 1, 1)
        owners.append((owner, owner_hot))
        lanes.append(row_hot)
    marked = jnp.where(named > 0.0, 1.0, 0.0)
    rank = contract(marked.astype(BF16), earlier(SLAB), 1, 0).astype(BF16)
    places = []
    for slot in range(FAN + 1):
        owner, owner_hot = owners[slot]
        mine = jnp.sum(contract(rank, owner_hot, 0, 0) * lanes[slot], axis=0, keepdims=True)
        places.append(owner * UNION + mine.astype(jnp.int32))
    place[...] = jnp.concatenate(places + [jnp.zeros((5, TARGETS), jnp.int32)], axis=0)

    shared = weights[...].astype(F32)
    for pair in range(FEAT // 2):
        block = features[:, pl.ds(pair * 2 * OWN, 2 * OWN)].astype(F32)
        for half in range(2):
            owner = 2 * pair + half
            marks = [marked[owner : owner + 1, k * 64 : (k + 1) * 64] for k in range(3)]
            last = jnp.concatenate(marks + [jnp.zeros((5, 64), F32)], axis=0)
            built[owner] = jnp.concatenate([shared, folded(block, half, last)], axis=0).astype(BF16)
        if pair % 4 == 3:
            copies_out(built, send, sent, pair // 4).start()
    for step in range(FEAT // 8):
        copies_out(built, send, sent, step).wait()


def copies_out(built, send, sent, step):
    span = pl.ds(step * 8, 8)
    return pltpu.make_async_copy(built.at[span], send.at[span], sent.at[step])


def folded(block, half, last):
    rest = block[:, 128 + half * 64 : 192 + half * 64]
    rest = jnp.concatenate([rest[:24], jnp.concatenate([rest[24:], last], axis=0)], axis=1)
    return jnp.concatenate([block[:, half * 256 : half * 256 + 128], rest], axis=0)


def order_kernel(neighbours, mask, lists, ranks, columns):
    used = [jnp.where(mask[slot] > 0, 1, 0) for slot in range(FAN)]
    before = [jnp.zeros((LINES, 128), jnp.int32)]
    for slot in range(FAN):
        before.append(before[slot] + used[slot])
    count = before[FAN]
    for place in range(FAN):
        node = jnp.where(count > place, 0, INPUTS)
        for slot in range(place, FAN):
            here = (used[slot] > 0) & (before[slot] == place)
            node = node + jnp.where(here, neighbours[slot], 0)
        high = node >> 8
        columns[place] = high.astype(F32)
        columns[16 + place] = (node - high * 256).astype(F32)
    columns[FAN] = jnp.zeros((LINES, 128), F32)
    columns[16 + FAN] = count.astype(F32)
    hot = [jnp.where(count == amount, 1.0, 0.0) for amount in range(FAN + 1)]
    stacked = jnp.concatenate(hot, axis=0).astype(BF16)
    second = iota(((FAN + 1) * LINES, 128), 0) % 2 == 1
    earlier_same = contract(stacked, earlier(128), 1, 0)
    all_same = contract(stacked, jnp.ones((128, 128), BF16), 1, 0)
    above = pltpu.roll(all_same, 1, 0)
    below = pltpu.roll(all_same, (FAN + 1) * LINES - 1, 0)
    earlier_same = earlier_same + jnp.where(second, above, 0.0)
    all_same = all_same + jnp.where(second, above, below)
    rank = jnp.zeros((LINES, 128), F32)
    higher = jnp.zeros((LINES, 128), F32)
    for amount in reversed(range(FAN + 1)):
        span = slice(amount * LINES, (amount + 1) * LINES)
        rank = rank + hot[amount] * (earlier_same[span] + higher)
        higher = higher + all_same[span]
    ranks[...] = rank.astype(jnp.int32)
    for line in range(0, LINES, 2):
        part = contract(columns[:, line, :].astype(BF16), moved(ranks, line), 1, 1)
        part += contract(columns[:, line + 1, :].astype(BF16), moved(ranks, line + 1), 1, 1)
        part = (part[:16] * 256.0 + part[16:]).astype(jnp.int32)
        first = line // 8 * 8 * (FAN + 1) + line % 8
        for half in range(2):
            here = part[: FAN + 1, half * 128 : (half + 1) * 128]
            lists[pl.ds(first + half, FAN + 1, stride=8), :] = here


def moved(ranks, line):
    return jnp.where(iota((256, 128), 0) == ranks[pl.ds(line, 1), :], 1.0, 0.0).astype(BF16)


def mean_of(flipped):
    thirds = [flipped[t * WIDTH : (t + 1) * WIDTH] for t in range(3)]
    return (thirds[0] + thirds[1] + thirds[2]) / jnp.maximum(flipped[3 * WIDTH : 3 * WIDTH + 1], 1.0)


def gather_kernel(
    slots, ranks, features, send, table, sums, lists, built, arrived, sent
):
    size = (FAN + 1) * CHUNK

    def fetch(chunk):
        span = pl.ds(pl.multiple_of(chunk * size, size), size)
        return pltpu.make_async_copy(slots.at[span], lists.at[span], arrived.at[chunk])

    for chunk in range(ROWS // CHUNK):
        fetch(chunk).start()

    lane = iota((128, 128), 1)
    third = INPUTS // 3

    def fill(step, carry):
        for part in range(TABLE_STEP):
            at = pl.multiple_of((step * TABLE_STEP + part) * 128, 128)
            blocks = [features[:, pl.ds(t * third + at, 128)].astype(F32) for t in range(3)]
            flipped = jnp.concatenate(blocks + [jnp.ones((8, 128), F32)], axis=0).T
            for t in range(3):
                kept = ((lane >= t * WIDTH) & (lane < (t + 1) * WIDTH)) | (lane >= 3 * WIDTH)
                table[pl.ds(t * third + at, 128), :] = jnp.where(kept, flipped, 0.0)
        return carry

    lax.fori_loop(0, third // 128 // TABLE_STEP, fill, 0)
    table[pl.ds(INPUTS, 8), :] = jnp.zeros((8, 128), F32)

    def chunk_step(chunk, carry):
        fetch(chunk).wait()

        def block(step, inner):
            first = chunk * size + step * UNROLL
            at = pl.multiple_of(chunk * CHUNK + step * UNROLL, UNROLL)
            result = sums.at[pl.ds(at, UNROLL), :]

            def add(depth):
                named = [lists.at[pl.ds(first + slot * CHUNK, UNROLL)] for slot in range(depth)]
                for row in range(UNROLL):
                    result[pl.ds(row, 1), :] = add_all(
                        [table[pl.ds(named[slot][row], 1), :] for slot in range(depth)]
                    )

            def choose(low, high):
                if low == high:
                    add(low)
                    return
                middle = (low + high) // 2
                lax.cond(
                    deepest <= middle,
                    lambda: choose(low, middle),
                    lambda: choose(middle + 1, high),
                )

            deepest = lists[first + FAN * CHUNK]
            choose(LEAST, FAN)
            return inner

        return lax.fori_loop(0, CHUNK // UNROLL, block, carry)

    lax.fori_loop(0, ROWS // CHUNK, chunk_step, 0)

    def pair_step(step, carry):
        for part in range(0, PAIRS, 2):
            line = (step * PAIRS + part) * 3
            blocks = []
            for k in range(0, 6, 2):
                at = pl.multiple_of((line + k) * 128, 128)
                means = [mean_of(sums[pl.ds(at + half * 128, 128), :].T) for half in range(2)]
                means = jnp.concatenate(means, axis=1).astype(BF16)
                for half in range(2):
                    blocks.append(contract(means, moved(ranks, line + k + half), 1, 0))
            for pair in range(2):
                block = jnp.concatenate(blocks[pair * 3 : pair * 3 + 3], axis=1)
                owner = 2 * (step * PAIRS + part + pair)
                for half in range(2):
                    tile = folded(block, half, jnp.zeros((8, 64), F32))
                    built[owner + half] = tile.astype(BF16)
        copies_out(built, send, sent, step).start()
        return carry

    lax.fori_loop(0, FEAT // 2 // PAIRS, pair_step, 0)
    for step in range(FEAT // 8):
        copies_out(built, send, sent, step).wait()


def hidden_kernel(
    spot, mine, theirs, means, bias, hidden, rows, stacked, held, other, marks, chosen
):
    for source in range(FEAT):
        own = mine[source].astype(F32)
        mean = means[source].astype(F32)
        held[pl.ds(source * 80, 80), :] = own[:80].astype(BF16)
        other[pl.ds(source * 80, 80), :] = theirs[source].astype(F32).astype(BF16)
        last, mean_last = own[120:144], mean[40:64]
        stacked[pl.ds(source * 80, 80), pl.ds(0, 128)] = jnp.concatenate(
            [own[80:120], mean[:40]], axis=0
        ).astype(BF16)
        stacked[pl.ds(source * 80, 80), pl.ds(128, 64)] = jnp.concatenate(
            [last[:, :64], last[:16, 64:], mean_last[:, :64], mean_last[:16, 64:]], axis=0
        ).astype(BF16)
        marks[pl.ds(source, 1), :] = jnp.concatenate(
            [last[16:17, 64:], last[17:18, 64:], last[18:19, 64:], jnp.zeros((1, 64), F32)], axis=1
        )
    stacked[:, pl.ds(192, 64)] = jnp.zeros((FEAT * 80, 64), BF16)
    first = contract(stacked[...], held[...], 0, 0)[:OWN]
    second = contract(stacked[...], other[...], 0, 0)[:OWN]
    even = spot[0] == 0
    pre = jnp.concatenate(
        [jnp.where(even, first, second), jnp.where(even, second, first)], axis=1
    )
    pre = jnp.where(spot[1] == 0, pre, jnp.concatenate([pre[128:], pre[:128]], axis=0))
    result = jnp.maximum(pre + bias[...], 0.0).astype(BF16)
    hidden[...] = result
    rank = contract(marks[...].astype(BF16), earlier(SLAB), 1, 0)
    for source in range(FEAT):
        hit = (iota((UNION, SLAB), 0).astype(F32) == rank[source : source + 1]) & (
            marks[pl.ds(source, 1), :] > 0.0
        )
        chosen[pl.ds(source * UNION, UNION), :] = jnp.where(hit, 1.0, 0.0)
    padded = jnp.concatenate([result, jnp.zeros((SLAB - OWN, HIDDEN), BF16)], axis=0)
    rows[...] = contract(chosen[...].astype(BF16), padded, 1, 0).astype(BF16)


def stage_kernel(place, mask, *refs):
    blocks, (picks, held, arrived) = refs[:-3], refs[-3:]
    copies = []
    for block in blocks:
        slot, first = STAGED[len(copies)]
        span = held.at[slot, pl.ds(first, block.shape[0]), :]
        copies.append(pltpu.make_async_copy(block, span, arrived.at[len(copies)]))
        copies[-1].start()
    spots = iota((FEAT * UNION, TARGETS), 0)
    total = jnp.zeros((FEAT * UNION, TARGETS), F32)
    for slot in range(FAN):
        used = mask[slot].astype(F32)
        total = total + jnp.where(spots == place[pl.ds(slot, 1), :], used, 0.0)
    picks[0] = total.astype(BF16)
    picks[1] = jnp.where(spots == place[pl.ds(FAN, 1), :], 1.0, 0.0).astype(BF16)
    for copy in copies:
        copy.wait()


def loss_kernel(bases, rows, picks, labels, held, loss, inputs, logits):
    count = contract(picks[0], jnp.ones((FEAT * UNION, 128), BF16), 0, 0)[:, :1]
    agg = contract(picks[0], rows[...], 0, 0) / jnp.maximum(count, 1.0)
    inputs[:, pl.ds(0, HIDDEN)] = contract(picks[1], rows[...], 0, 0).astype(BF16)
    inputs[:, pl.ds(HIDDEN, HIDDEN)] = agg.astype(BF16)
    offset = (
        jnp.broadcast_to(labels[...].astype(F32), (TARGETS, TARGETS)).T.astype(jnp.int32)
        - iota((TARGETS, TARGETS), 1)
    )
    width = held.shape[2]
    largest = jnp.full((TARGETS, TARGETS), -jnp.inf, F32)
    summed = jnp.zeros((TARGETS, TARGETS), F32)
    picked = jnp.zeros((TARGETS, TARGETS), F32)
    for step in range(NODE + 1):
        if step < NODE:
            logits[step % 2] = contract(inputs[...], held[step], 1, 0)
        if step > 0:
            spans = [pl.ds(k * 128, 128) for k in range(width // 128)]
            last = logits.at[(step - 1) % 2]
            here = offset - bases[step - 1]
            now = largest
            for span in spans:
                now = jnp.maximum(now, last[:, span])
            summed = summed * jnp.exp(largest - now)
            for k, span in enumerate(spans):
                part = last[:, span]
                summed = summed + jnp.exp(part - now)
                picked = picked + jnp.where(here == k * 128, part, 0.0)
            largest = now
    most = jnp.max(largest, axis=1, keepdims=True)
    total = jnp.sum(summed * jnp.exp(largest - most), axis=1, keepdims=True)
    column = most + jnp.log(total) - jnp.sum(picked, axis=1, keepdims=True)
    loss[...] = jnp.broadcast_to(column, (TARGETS, TARGETS)).T[:1]


VMEM = pl.BlockSpec(memory_space=pltpu.VMEM)
HBM = pl.BlockSpec(memory_space=pltpu.HBM)
SMEM = pl.BlockSpec(memory_space=pltpu.SMEM)


def call_order(neighbours, mask):
    return pl.pallas_call(
        order_kernel,
        out_shape=(
            jax.ShapeDtypeStruct((LINES * (FAN + 1), 128), jnp.int32),
            jax.ShapeDtypeStruct((LINES, 128), jnp.int32),
        ),
        in_specs=[VMEM, VMEM],
        out_specs=(VMEM, VMEM),
        scratch_shapes=[pltpu.VMEM((32, LINES, 128), F32)],
        compiler_params=pltpu.CompilerParams(vmem_limit_bytes=24 * 2**20),
        cost_estimate=pl.CostEstimate(flops=10**8, bytes_accessed=10**7, transcendentals=0),
    )(neighbours.reshape(FAN, LINES, 128), mask.reshape(FAN, LINES, 128))


def call_gather(slots, ranks, table):
    return pl.pallas_call(
        gather_kernel,
        out_shape=jax.ShapeDtypeStruct((FEAT, 64, 128), BF16),
        in_specs=[pl.BlockSpec(memory_space=pl.ANY), VMEM, VMEM],
        out_specs=HBM,
        scratch_shapes=[
            pltpu.VMEM((INPUTS + 8, 128), F32),
            pltpu.VMEM((ROWS, 128), F32),
            pltpu.SMEM(((FAN + 1) * ROWS,), jnp.int32),
            pltpu.VMEM((FEAT, 64, 128), BF16),
            pltpu.SemaphoreType.DMA((ROWS // CHUNK,)),
            pltpu.SemaphoreType.DMA((FEAT // 8,)),
        ],
        compiler_params=pltpu.CompilerParams(vmem_limit_bytes=24 * 2**20),
        cost_estimate=pl.CostEstimate(flops=10**9, bytes_accessed=90 * 10**6, transcendentals=0),
    )(slots, ranks, table)


def call_stage(place, mask, blocks):
    width = blocks[0].shape[1]
    return pl.pallas_call(
        stage_kernel,
        out_shape=(
            jax.ShapeDtypeStruct((2, FEAT * UNION, TARGETS), BF16),
            jax.ShapeDtypeStruct((NODE, 2 * HIDDEN, width), BF16),
        ),
        in_specs=[VMEM] * 2 + [HBM] * len(blocks),
        out_specs=(VMEM, VMEM),
        scratch_shapes=[pltpu.SemaphoreType.DMA((len(blocks),))],
        compiler_params=pltpu.CompilerParams(vmem_limit_bytes=16 * 2**20),
        cost_estimate=pl.CostEstimate(flops=10**7, bytes_accessed=20 * 10**6, transcendentals=0),
    )(place, mask, *blocks)


def call_loss(bases, rows, picks, labels, held):
    return pl.pallas_call(
        loss_kernel,
        out_shape=jax.ShapeDtypeStruct((1, TARGETS), F32),
        in_specs=[SMEM] + [VMEM] * 4,
        out_specs=VMEM,
        scratch_shapes=[
            pltpu.VMEM((TARGETS, 2 * HIDDEN), BF16),
            pltpu.VMEM((2, TARGETS, held.shape[2]), F32),
        ],
        compiler_params=pltpu.CompilerParams(vmem_limit_bytes=16 * 2**20),
    )(bases, rows, picks, labels, held)


def body(
    features,
    first_neighbours,
    first_mask,
    second_neighbours,
    second_mask,
    target_index,
    labels,
    first_weight,
    first_bias,
    class_weight,
):
    spot = lax.axis_index("node").astype(jnp.int32)
    core = spot & 1
    half = lax.dynamic_slice(first_weight, (0, 0, core * 128), (2, WIDTH, 128))
    table = features[:, 0, :]
    slots, ranks = call_order(first_neighbours, first_mask)
    up = [(device, (device + 2) % NODE) for device in range(NODE)]
    down = [(device, (device - 2) % NODE) for device in range(NODE)]
    swap = [(device, device ^ 1) for device in range(NODE)]
    below = lax.ppermute(class_weight, "node", up)
    above = lax.ppermute(class_weight, "node", down)
    swapped = [lax.ppermute(class_weight, "node", swap)]
    table, slots, ranks = lax.optimization_barrier((table, slots, ranks))
    own, place = pl.pallas_call(
        send_kernel,
        out_shape=(
            jax.ShapeDtypeStruct((FEAT, 144, 128), BF16),
            jax.ShapeDtypeStruct((16, TARGETS), jnp.int32),
        ),
        in_specs=[VMEM] * 4,
        out_specs=(HBM, VMEM),
        scratch_shapes=[
            pltpu.VMEM((FEAT, 144, 128), BF16),
            pltpu.SemaphoreType.DMA((FEAT // 8,)),
        ],
        compiler_params=pltpu.CompilerParams(vmem_limit_bytes=16 * 2**20),
        cost_estimate=pl.CostEstimate(flops=10**8, bytes_accessed=3 * 10**6, transcendentals=0),
    )(table, half.reshape(2 * WIDTH, 128), second_neighbours, target_index)
    own = lax.all_to_all(own, "feat", 0, 0)
    send = call_gather(slots.reshape(-1), ranks, table)
    send, below, above, own = lax.optimization_barrier((send, below, above, own))
    far = [
        lax.ppermute(below[:HIDDEN], "node", up),
        lax.ppermute(above[HIDDEN:], "node", down),
    ]
    swapped += [lax.ppermute(below, "node", swap), lax.ppermute(above, "node", swap)]
    theirs = lax.ppermute(own[:, : 2 * WIDTH], "node", swap)
    means = lax.all_to_all(send, "feat", 0, 0)
    means, far = lax.optimization_barrier((means, far))
    swapped += [lax.ppermute(part, "node", swap) for part in far]
    side = jnp.stack([core, lax.axis_index("feat").astype(jnp.int32) & 1])
    hidden, rows = pl.pallas_call(
        hidden_kernel,
        out_shape=(
            jax.ShapeDtypeStruct((OWN, HIDDEN), BF16),
            jax.ShapeDtypeStruct((FEAT * UNION, HIDDEN), BF16),
        ),
        in_specs=[SMEM] + [VMEM] * 4,
        out_specs=(VMEM, VMEM),
        scratch_shapes=[
            pltpu.VMEM((FEAT * 80, 256), BF16),
            pltpu.VMEM((FEAT * 80, 128), BF16),
            pltpu.VMEM((FEAT * 80, 128), BF16),
            pltpu.VMEM((FEAT, SLAB), F32),
            pltpu.VMEM((FEAT * UNION, SLAB), F32),
        ],
        compiler_params=pltpu.CompilerParams(vmem_limit_bytes=24 * 2**20),
    )(side, own, theirs, means, first_bias[None, :])
    rows = lax.all_to_all(rows.reshape(FEAT, UNION, HIDDEN), "feat", 0, 0)
    rows = rows.reshape(FEAT * UNION, HIDDEN)
    picks, held = call_stage(place, second_mask, [class_weight, below, above, *far, *swapped])
    order = jnp.stack([spot, spot + 6, spot + 2, spot + 4]) & 7
    bases = jnp.concatenate([order, order ^ 1]) * class_weight.shape[1]
    loss = call_loss(bases, rows, picks, labels, held)
    return (hidden[None], loss)


def solution(mesh):
    placed = (
        P("feat", "node", None),
        P(None, "node", None),
        P(None, "node", None),
        P(None, "node", "feat"),
        P(None, "node", "feat"),
        P("node", "feat"),
        P("node", "feat"),
        P(None, "feat", None),
        P(),
        P(None, "node"),
    )
    return jax.shard_map(
        body,
        mesh=mesh,
        in_specs=placed,
        out_specs=(P("node", "feat", None), P("node", "feat")),
        check_vma=False,
    )
```

```python
import functools

import jax
import jax.numpy as jnp
from jax import lax
from jax.experimental import pallas as pl
from jax.experimental.pallas import tpu as pltpu
from jax.sharding import PartitionSpec as P

FEAT = 32
NODE = 8
WIDTH = 40
INPUTS = 24576
ROWS = 6144
OWN = 192
FAN = 10
TARGETS = 128
HIDDEN = 256
UNION = 24
NAMED = FEAT * UNION
SLAB = 256
UNROLL = 64
LEAST = 3
LINES = ROWS // 128
CHUNK = 1024
PAIRS = 4
TABLE_STEP = 8
MOST = 60 * 2**20
F32 = jnp.float32
BF16 = jnp.bfloat16


def iota(shape, dim):
    return lax.broadcasted_iota(jnp.int32, shape, dim)


def contract(a, b, dim_a, dim_b):
    return lax.dot_general(a, b, (((dim_a,), (dim_b,)), ((), ())), preferred_element_type=F32)


def earlier(size):
    return jnp.where(iota((size, size), 0) < iota((size, size), 1), 1.0, 0.0).astype(BF16)


def add_all(terms):
    while len(terms) > 1:
        paired = [terms[k] + terms[k + 1] for k in range(0, len(terms) - 1, 2)]
        terms = paired + terms[len(terms) - len(terms) % 2 :]
    return terms[0]


def prepare_kernel(core, *refs):
    sources, (send, place, lists, ranks), held, (built, columns, sent, arrived) = (
        refs[:6],
        refs[6:10],
        refs[10:16],
        refs[16:],
    )
    fetches = []
    for source, ref in zip(sources, held):
        part = source if source.shape == ref.shape else source.at[:, pl.ds(0, ROWS)]
        fetches.append(pltpu.make_async_copy(part, ref, arrived.at[len(fetches)]))
        fetches[-1].start()
    neighbours, targets, weights, features, given, filled = held
    fetches[0].wait()
    fetches[1].wait()
    owners, lanes = [], []
    named = jnp.zeros((FEAT, SLAB), F32)
    for slot in range(FAN + 1):
        index = neighbours[slot] if slot < FAN else targets[...]
        owner = ((index.astype(F32) + 0.5) * (1.0 / OWN)).astype(jnp.int32)
        row = index - owner * OWN
        owner_hot = jnp.where(iota((FEAT, TARGETS), 0) == owner, 1.0, 0.0).astype(BF16)
        row_hot = jnp.where(iota((SLAB, TARGETS), 0) == row, 1.0, 0.0)
        named = named + contract(owner_hot, row_hot.astype(BF16), 1, 1)
        owners.append((owner, owner_hot))
        lanes.append(row_hot)
    marked = jnp.where(named > 0.0, 1.0, 0.0)
    rank = contract(marked.astype(BF16), earlier(SLAB), 1, 0).astype(BF16)
    places = []
    for slot in range(FAN + 1):
        owner, owner_hot = owners[slot]
        mine = jnp.sum(contract(rank, owner_hot, 0, 0) * lanes[slot], axis=0, keepdims=True)
        places.append(owner * UNION + mine.astype(jnp.int32))
    place[...] = jnp.concatenate(places + [jnp.zeros((5, TARGETS), jnp.int32)], axis=0)

    fetches[2].wait()
    fetches[3].wait()
    shared = weights[...].astype(F32)
    shared = jnp.where(core[0] == 0, shared[:, :, :128], shared[:, :, 128:])
    shared = shared.reshape(2 * WIDTH, 128)
    for pair in range(FEAT // 2):
        block = features[:, pl.ds(pair * 2 * OWN, 2 * OWN)].astype(F32)
        for half in range(2):
            owner = 2 * pair + half
            marks = [marked[owner : owner + 1, k * 64 : (k + 1) * 64] for k in range(3)]
            last = jnp.concatenate(marks + [jnp.zeros((5, 64), F32)], axis=0)
            built[owner] = jnp.concatenate([shared, folded(block, half, last)], axis=0).astype(BF16)
        if pair % 4 == 3:
            copies_out(built, send, sent, pair // 4).start()
    fetches[4].wait()
    fetches[5].wait()
    order_rows(given, filled, lists, ranks, columns)
    for step in range(FEAT // 8):
        copies_out(built, send, sent, step).wait()


def order_rows(neighbours, mask, lists, ranks, columns):
    used = [jnp.where(mask[slot] > 0, 1, 0) for slot in range(FAN)]
    before = [jnp.zeros((LINES, 128), jnp.int32)]
    for slot in range(FAN):
        before.append(before[slot] + used[slot])
    count = before[FAN]
    for place in range(FAN):
        node = jnp.where(count > place, 0, INPUTS)
        for slot in range(place, FAN):
            here = (used[slot] > 0) & (before[slot] == place)
            node = node + jnp.where(here, neighbours[slot], 0)
        high = node >> 8
        columns[place] = high.astype(F32)
        columns[16 + place] = (node - high * 256).astype(F32)
    columns[FAN] = jnp.zeros((LINES, 128), F32)
    columns[16 + FAN] = count.astype(F32)
    hot = [jnp.where(count == amount, 1.0, 0.0) for amount in range(FAN + 1)]
    stacked = jnp.concatenate(hot, axis=0).astype(BF16)
    second = iota(((FAN + 1) * LINES, 128), 0) % 2 == 1
    earlier_same = contract(stacked, earlier(128), 1, 0)
    all_same = contract(stacked, jnp.ones((128, 128), BF16), 1, 0)
    above = pltpu.roll(all_same, 1, 0)
    below = pltpu.roll(all_same, (FAN + 1) * LINES - 1, 0)
    earlier_same = earlier_same + jnp.where(second, above, 0.0)
    all_same = all_same + jnp.where(second, above, below)
    rank = jnp.zeros((LINES, 128), F32)
    higher = jnp.zeros((LINES, 128), F32)
    for amount in reversed(range(FAN + 1)):
        span = slice(amount * LINES, (amount + 1) * LINES)
        rank = rank + hot[amount] * (earlier_same[span] + higher)
        higher = higher + all_same[span]
    ranks[...] = rank.astype(jnp.int32)
    for line in range(0, LINES, 2):
        part = contract(columns[:, line, :].astype(BF16), moved(ranks, line), 1, 1)
        part += contract(columns[:, line + 1, :].astype(BF16), moved(ranks, line + 1), 1, 1)
        part = (part[:16] * 256.0 + part[16:]).astype(jnp.int32)
        first = line // 8 * 8 * (FAN + 1) + line % 8
        for half in range(2):
            here = part[: FAN + 1, half * 128 : (half + 1) * 128]
            lists[pl.ds(first + half, FAN + 1, stride=8), :] = here


def copies_out(built, send, sent, step):
    span = pl.ds(step * 8, 8)
    return pltpu.make_async_copy(built.at[span], send.at[span], sent.at[step])


def folded(block, half, last):
    rest = block[:, 128 + half * 64 : 192 + half * 64]
    rest = jnp.concatenate([rest[:24], jnp.concatenate([rest[24:], last], axis=0)], axis=1)
    return jnp.concatenate([block[:, half * 256 : half * 256 + 128], rest], axis=0)


def moved(ranks, line):
    return jnp.where(iota((256, 128), 0) == ranks[pl.ds(line, 1), :], 1.0, 0.0).astype(BF16)


def mean_of(flipped):
    thirds = [flipped[t * WIDTH : (t + 1) * WIDTH] for t in range(3)]
    return (thirds[0] + thirds[1] + thirds[2]) / jnp.maximum(flipped[3 * WIDTH : 3 * WIDTH + 1], 1.0)


def gather_kernel(
    slots, ranks, source, send, table, sums, lists, built, features, arrived, loaded, sent
):
    size = (FAN + 1) * CHUNK

    def fetch(chunk):
        span = pl.ds(pl.multiple_of(chunk * size, size), size)
        return pltpu.make_async_copy(slots.at[span], lists.at[span], arrived.at[chunk])

    third = INPUTS // 3
    piece = 128 * TABLE_STEP

    def load(step, t):
        span = pl.ds(pl.multiple_of(t * third + step * piece, piece), piece)
        return pltpu.make_async_copy(source.at[:, span], features.at[:, span], loaded.at[step, t])

    for step in range(third // piece):
        for t in range(3):
            load(step, t).start()
    for chunk in range(ROWS // CHUNK):
        fetch(chunk).start()

    lane = iota((128, 128), 1)

    def fill(step, carry):
        for t in range(3):
            load(step, t).wait()
        for part in range(TABLE_STEP):
            at = pl.multiple_of((step * TABLE_STEP + part) * 128, 128)
            blocks = [features[:, pl.ds(t * third + at, 128)].astype(F32) for t in range(3)]
            flipped = jnp.concatenate(blocks + [jnp.ones((8, 128), F32)], axis=0).T
            for t in range(3):
                kept = ((lane >= t * WIDTH) & (lane < (t + 1) * WIDTH)) | (lane >= 3 * WIDTH)
                table[pl.ds(t * third + at, 128), :] = jnp.where(kept, flipped, 0.0)
        return carry

    lax.fori_loop(0, third // 128 // TABLE_STEP, fill, 0)
    table[pl.ds(INPUTS, 8), :] = jnp.zeros((8, 128), F32)

    def chunk_step(chunk, carry):
        fetch(chunk).wait()

        def block(step, inner):
            first = chunk * size + step * UNROLL
            at = pl.multiple_of(chunk * CHUNK + step * UNROLL, UNROLL)
            result = sums.at[pl.ds(at, UNROLL), :]

            def add(depth):
                named = [lists.at[pl.ds(first + slot * CHUNK, UNROLL)] for slot in range(depth)]
                for row in range(UNROLL):
                    result[pl.ds(row, 1), :] = add_all(
                        [table[pl.ds(named[slot][row], 1), :] for slot in range(depth)]
                    )

            def choose(low, high):
                if low == high:
                    add(low)
                    return
                middle = (low + high) // 2
                lax.cond(
                    deepest <= middle,
                    lambda: choose(low, middle),
                    lambda: choose(middle + 1, high),
                )

            deepest = lists[first + FAN * CHUNK]
            choose(LEAST, FAN)
            return inner

        return lax.fori_loop(0, CHUNK // UNROLL, block, carry)

    lax.fori_loop(0, ROWS // CHUNK, chunk_step, 0)

    def pair_step(step, carry):
        for part in range(0, PAIRS, 2):
            line = (step * PAIRS + part) * 3
            blocks = []
            for k in range(0, 6, 2):
                at = pl.multiple_of((line + k) * 128, 128)
                means = [mean_of(sums[pl.ds(at + half * 128, 128), :].T) for half in range(2)]
                means = jnp.concatenate(means, axis=1).astype(BF16)
                for half in range(2):
                    blocks.append(contract(means, moved(ranks, line + k + half), 1, 0))
            for pair in range(2):
                block = jnp.concatenate(blocks[pair * 3 : pair * 3 + 3], axis=1)
                owner = 2 * (step * PAIRS + part + pair)
                for half in range(2):
                    tile = folded(block, half, jnp.zeros((8, 64), F32))
                    built[owner + half] = tile.astype(BF16)
        copies_out(built, send, sent, step).start()
        return carry

    lax.fori_loop(0, FEAT // 2 // PAIRS, pair_step, 0)
    for step in range(FEAT // 8):
        copies_out(built, send, sent, step).wait()


def hidden_kernel(
    seen, spot, mine, theirs, means, bias, hidden, rows, stacked, held, other, marks, chosen
):
    for source in range(FEAT):
        own = mine[source].astype(F32)
        mean = means[source].astype(F32)
        held[pl.ds(source * 80, 80), :] = own[:80].astype(BF16)
        other[pl.ds(source * 80, 80), :] = theirs[source].astype(F32).astype(BF16)
        last, mean_last = own[120:144], mean[40:64]
        stacked[pl.ds(source * 80, 80), pl.ds(0, 128)] = jnp.concatenate(
            [own[80:120], mean[:40]], axis=0
        ).astype(BF16)
        stacked[pl.ds(source * 80, 80), pl.ds(128, 64)] = jnp.concatenate(
            [last[:, :64], last[:16, 64:], mean_last[:, :64], mean_last[:16, 64:]], axis=0
        ).astype(BF16)
        marks[pl.ds(source, 1), :] = jnp.concatenate(
            [last[16:17, 64:], last[17:18, 64:], last[18:19, 64:], jnp.zeros((1, 64), F32)], axis=1
        )
    stacked[:, pl.ds(192, 64)] = jnp.zeros((FEAT * 80, 64), BF16)
    first = contract(stacked[...], held[...], 0, 0)[:OWN]
    second = contract(stacked[...], other[...], 0, 0)[:OWN]
    even = spot[0] == 0
    pre = jnp.concatenate(
        [jnp.where(even, first, second), jnp.where(even, second, first)], axis=1
    )
    pre = jnp.where(spot[1] == 0, pre, jnp.concatenate([pre[128:], pre[:128]], axis=0))
    result = jnp.maximum(pre + bias[...], 0.0).astype(BF16)
    hidden[...] = result
    rank = contract(marks[...].astype(BF16), earlier(SLAB), 1, 0)
    for source in range(FEAT):
        hit = (iota((UNION, SLAB), 0).astype(F32) == rank[source : source + 1]) & (
            marks[pl.ds(source, 1), :] > 0.0
        )
        chosen[pl.ds(source * UNION, UNION), :] = jnp.where(hit, 1.0, 0.0)
    padded = jnp.concatenate([result, jnp.zeros((SLAB - OWN, HIDDEN), BF16)], axis=0)
    rows[...] = contract(chosen[...].astype(BF16), padded, 1, 0).astype(BF16)


def pick_kernel(place, mask, labels, picks):
    spots = iota((NAMED, TARGETS), 0)
    total = jnp.zeros((NAMED, TARGETS), F32)
    for slot in range(FAN):
        used = mask[slot].astype(F32)
        total = total + jnp.where(spots == place[pl.ds(slot, 1), :], used, 0.0)
    own = jnp.where(spots == place[pl.ds(FAN, 1), :], 1.0, 0.0)
    line = iota((16, TARGETS), 0)
    label = jnp.broadcast_to(labels[...], (16, TARGETS))
    high = label >> 7
    parts = jnp.where(line == 0, high, jnp.where(line == 1, label - high * 128, 0))
    blank = jnp.zeros((16, TARGETS), F32)
    picks[0] = jnp.concatenate([total, parts.astype(F32)], axis=0).astype(BF16)
    picks[1] = jnp.concatenate([own, blank], axis=0).astype(BF16)


def loss_kernel(bases, *refs):
    sources, (stats, other) = refs[: 4 + NODE // 2], refs[4 + NODE // 2 : 6 + NODE // 2]
    inputs, logits, *held, arrived = refs[6 + NODE // 2 :]
    copies = [
        pltpu.make_async_copy(source, ref, arrived.at[k])
        for k, (source, ref) in enumerate(zip(sources, held))
    ]
    for copy in copies:
        copy.start()
    offsets = []
    for side in range(2):
        copies[2 * side].wait()
        copies[2 * side + 1].wait()
        rows, picks = held[2 * side], held[2 * side + 1]
        total, own = picks[0][:NAMED], picks[1][:NAMED]
        count = contract(total, jnp.ones((NAMED, 128), BF16), 0, 0)[:, :1]
        agg = contract(total, rows[...], 0, 0) / jnp.maximum(count, 1.0)
        span = pl.ds(side * TARGETS, TARGETS)
        inputs[span, pl.ds(0, HIDDEN)] = contract(own, rows[...], 0, 0).astype(BF16)
        inputs[span, pl.ds(HIDDEN, HIDDEN)] = agg.astype(BF16)
        parts = picks[0][NAMED:].astype(F32)
        label = jnp.broadcast_to(parts[:1] * 128.0 + parts[1:2], (TARGETS, TARGETS)).T
        offsets.append(label.astype(jnp.int32) - iota((TARGETS, TARGETS), 1))
    blocks = held[4:]
    width = blocks[0].shape[1]
    start = (
        jnp.full((TARGETS, TARGETS), -jnp.inf, F32),
        jnp.zeros((TARGETS, TARGETS), F32),
        jnp.zeros((TARGETS, TARGETS), F32),
    )
    running = [start, start]
    for step in range(2 * len(blocks) + 1):
        block, side = step // 2, step % 2
        if block < len(blocks):
            if side == 0:
                copies[4 + block].wait()
            mine = inputs[pl.ds(side * TARGETS, TARGETS), :]
            logits[step % 2] = contract(mine, blocks[block][...], 1, 0)
        if step > 0:
            block, side = (step - 1) // 2, (step - 1) % 2
            last = logits.at[(step - 1) % 2]
            largest, summed, picked = running[side]
            spans = [pl.ds(k * 128, 128) for k in range(width // 128)]
            here = offsets[side] - bases[block]
            now = largest
            for span in spans:
                now = jnp.maximum(now, last[:, span])
            summed = summed * jnp.exp(largest - now)
            for k, span in enumerate(spans):
                part = last[:, span]
                summed = summed + jnp.exp(part - now)
                picked = picked + jnp.where(here == k * 128, part, 0.0)
            running[side] = (now, summed, picked)
    for side, ref in ((0, stats), (1, other)):
        largest, summed, picked = running[side]
        most = jnp.max(largest, axis=1, keepdims=True)
        total = jnp.sum(summed * jnp.exp(largest - most), axis=1, keepdims=True)
        found = jnp.sum(picked, axis=1, keepdims=True)
        lane = iota((TARGETS, TARGETS), 1)
        table = jnp.where(lane == 0, most, jnp.where(lane == 1, total, found))
        ref[...] = table.T[:8]


VMEM = pl.BlockSpec(memory_space=pltpu.VMEM)
HBM = pl.BlockSpec(memory_space=pltpu.HBM)
SMEM = pl.BlockSpec(memory_space=pltpu.SMEM)


def call_prepare(core, arrays):
    shapes = [array.shape for array in arrays]
    shapes[3] = (WIDTH, ROWS)
    return pl.pallas_call(
        prepare_kernel,
        out_shape=(
            jax.ShapeDtypeStruct((FEAT, 144, 128), BF16),
            jax.ShapeDtypeStruct((16, TARGETS), jnp.int32),
            jax.ShapeDtypeStruct((LINES * (FAN + 1), 128), jnp.int32),
            jax.ShapeDtypeStruct((LINES, 128), jnp.int32),
        ),
        in_specs=[SMEM] + [HBM] * 6,
        out_specs=(HBM, VMEM, VMEM, VMEM),
        scratch_shapes=[
            *[pltpu.VMEM(shape, array.dtype) for shape, array in zip(shapes, arrays)],
            pltpu.VMEM((FEAT, 144, 128), BF16),
            pltpu.VMEM((32, LINES, 128), F32),
            pltpu.SemaphoreType.DMA((FEAT // 8,)),
            pltpu.SemaphoreType.DMA((6,)),
        ],
        compiler_params=pltpu.CompilerParams(vmem_limit_bytes=MOST),
        cost_estimate=pl.CostEstimate(flops=10**8, bytes_accessed=10**7, transcendentals=0),
    )(core, *arrays)


def call_gather(slots, ranks, table):
    return pl.pallas_call(
        gather_kernel,
        out_shape=jax.ShapeDtypeStruct((FEAT, 64, 128), BF16),
        in_specs=[pl.BlockSpec(memory_space=pl.ANY), VMEM, HBM],
        out_specs=HBM,
        scratch_shapes=[
            pltpu.VMEM((INPUTS + 8, 128), F32),
            pltpu.VMEM((ROWS, 128), F32),
            pltpu.SMEM(((FAN + 1) * ROWS,), jnp.int32),
            pltpu.VMEM((FEAT, 64, 128), BF16),
            pltpu.VMEM((WIDTH, INPUTS), BF16),
            pltpu.SemaphoreType.DMA((ROWS // CHUNK,)),
            pltpu.SemaphoreType.DMA((INPUTS // 3 // 128 // TABLE_STEP, 3)),
            pltpu.SemaphoreType.DMA((FEAT // 8,)),
        ],
        compiler_params=pltpu.CompilerParams(vmem_limit_bytes=MOST),
        cost_estimate=pl.CostEstimate(flops=0, bytes_accessed=0, transcendentals=0),
    )(slots, ranks, table)


def call_pick(place, mask, labels):
    return pl.pallas_call(
        pick_kernel,
        out_shape=jax.ShapeDtypeStruct((2, NAMED + 16, TARGETS), BF16),
        in_specs=[VMEM] * 3,
        out_specs=VMEM,
        compiler_params=pltpu.CompilerParams(vmem_limit_bytes=16 * 2**20),
        cost_estimate=pl.CostEstimate(flops=10**7, bytes_accessed=4 * 10**6, transcendentals=0),
    )(place, mask, labels)


def call_loss(bases, rows, picks, rows_there, picks_there, blocks):
    sources = [rows, picks, rows_there, picks_there, *blocks]
    return pl.pallas_call(
        loss_kernel,
        out_shape=[jax.ShapeDtypeStruct((8, TARGETS), F32)] * 2,
        in_specs=[SMEM] + [HBM] * len(sources),
        out_specs=[VMEM, VMEM],
        scratch_shapes=[
            pltpu.VMEM((2 * TARGETS, 2 * HIDDEN), BF16),
            pltpu.VMEM((2, TARGETS, blocks[0].shape[1]), F32),
            *[pltpu.VMEM(source.shape, BF16) for source in sources],
            pltpu.SemaphoreType.DMA((len(sources),)),
        ],
        compiler_params=pltpu.CompilerParams(vmem_limit_bytes=MOST),
    )(bases, *sources)


def body(
    features,
    first_neighbours,
    first_mask,
    second_neighbours,
    second_mask,
    target_index,
    labels,
    first_weight,
    first_bias,
    class_weight,
):
    spot = lax.axis_index("node").astype(jnp.int32)
    core = spot & 1
    table = features[:, 0, :]
    swap = [(device, device ^ 1) for device in range(NODE)]
    blocks = [class_weight]
    for hops in (4, 2, 6):
        around = [(device, (device + hops) % NODE) for device in range(NODE)]
        blocks.append(lax.ppermute(class_weight, "node", around))
    own, place, slots, ranks = call_prepare(
        core[None],
        [
            second_neighbours,
            target_index,
            first_weight,
            table,
            first_neighbours.reshape(FAN, LINES, 128),
            first_mask.reshape(FAN, LINES, 128),
        ],
    )
    own = lax.all_to_all(own, "feat", 0, 0)
    send = call_gather(slots.reshape(-1), ranks, table)
    theirs = lax.ppermute(own[:, : 2 * WIDTH], "node", swap)
    means = lax.all_to_all(send, "feat", 0, 0)
    seen = jnp.stack([block[0, 0] for block in blocks[2:]]).astype(F32)
    side = jnp.stack([core, lax.axis_index("feat").astype(jnp.int32) & 1])
    hidden, rows = pl.pallas_call(
        hidden_kernel,
        out_shape=(
            jax.ShapeDtypeStruct((OWN, HIDDEN), BF16),
            jax.ShapeDtypeStruct((FEAT * UNION, HIDDEN), BF16),
        ),
        in_specs=[SMEM] * 2 + [VMEM] * 4,
        out_specs=(VMEM, VMEM),
        scratch_shapes=[
            pltpu.VMEM((FEAT * 80, 256), BF16),
            pltpu.VMEM((FEAT * 80, 128), BF16),
            pltpu.VMEM((FEAT * 80, 128), BF16),
            pltpu.VMEM((FEAT, SLAB), F32),
            pltpu.VMEM((FEAT * UNION, SLAB), F32),
        ],
        compiler_params=pltpu.CompilerParams(vmem_limit_bytes=24 * 2**20),
    )(seen, side, own, theirs, means, first_bias[None, :])
    picks = call_pick(place, second_mask, labels)
    picks_there = lax.ppermute(picks, "node", swap)
    rows = lax.all_to_all(rows.reshape(FEAT, UNION, HIDDEN), "feat", 0, 0)
    rows = rows.reshape(FEAT * UNION, HIDDEN)
    rows_there = lax.ppermute(rows, "node", swap)
    bases = (jnp.stack([spot, spot + 4, spot + 6, spot + 2]) & 7) * class_weight.shape[1]
    here, there = call_loss(bases, rows, picks, rows_there, picks_there, blocks)
    there = lax.ppermute(there, "node", swap)
    most = jnp.maximum(here[0:1], there[0:1])
    total = here[1:2] * jnp.exp(here[0:1] - most) + there[1:2] * jnp.exp(there[0:1] - most)
    loss = most + jnp.log(total) - (here[2:3] + there[2:3])
    return (hidden[None], loss)


def solution(mesh):
    placed = (
        P("feat", "node", None),
        P(None, "node", None),
        P(None, "node", None),
        P(None, "node", "feat"),
        P(None, "node", "feat"),
        P("node", "feat"),
        P("node", "feat"),
        P(None, "feat", None),
        P(),
        P(None, "node"),
    )
    return jax.shard_map(
        body,
        mesh=mesh,
        in_specs=placed,
        out_specs=(P("node", "feat", None), P("node", "feat")),
        check_vma=False,
    )
```

```python
import functools

import jax
import jax.numpy as jnp
from jax import lax
from jax.experimental import pallas as pl
from jax.experimental.pallas import tpu as pltpu
from jax.sharding import PartitionSpec as P

FEAT = 32
NODE = 8
WIDTH = 40
INPUTS = 24576
ROWS = 6144
OWN = 192
FAN = 10
TARGETS = 128
HIDDEN = 256
UNION = 24
NAMED = FEAT * UNION
SLAB = 256
HOPS = (0, 4, 6, 2)
UNROLL = 64
LEAST = 3
LINES = ROWS // 128
CHUNK = 1024
PAIRS = 4
TABLE_STEP = 16
MOST = 60 * 2**20
F32 = jnp.float32
BF16 = jnp.bfloat16


def iota(shape, dim):
    return lax.broadcasted_iota(jnp.int32, shape, dim)


def contract(a, b, dim_a, dim_b):
    return lax.dot_general(a, b, (((dim_a,), (dim_b,)), ((), ())), preferred_element_type=F32)


def earlier(size):
    return jnp.where(iota((size, size), 0) < iota((size, size), 1), 1.0, 0.0).astype(BF16)


def add_all(terms):
    while len(terms) > 1:
        paired = [terms[k] + terms[k + 1] for k in range(0, len(terms) - 1, 2)]
        terms = paired + terms[len(terms) - len(terms) % 2 :]
    return terms[0]


def prepare_kernel(core, *refs):
    sources, (send, place, lists, ranks), held, (built, columns, sent, arrived) = (
        refs[:6],
        refs[6:10],
        refs[10:16],
        refs[16:],
    )
    fetches = []
    for source, ref in zip(sources, held):
        part = source if source.shape == ref.shape else source.at[:, pl.ds(0, ROWS)]
        fetches.append(pltpu.make_async_copy(part, ref, arrived.at[len(fetches)]))
        fetches[-1].start()
    neighbours, targets, weights, features, given, filled = held
    fetches[0].wait()
    fetches[1].wait()
    owners, lanes = [], []
    named = jnp.zeros((FEAT, SLAB), F32)
    for slot in range(FAN + 1):
        index = neighbours[slot] if slot < FAN else targets[...]
        owner = ((index.astype(F32) + 0.5) * (1.0 / OWN)).astype(jnp.int32)
        row = index - owner * OWN
        owner_hot = jnp.where(iota((FEAT, TARGETS), 0) == owner, 1.0, 0.0).astype(BF16)
        row_hot = jnp.where(iota((SLAB, TARGETS), 0) == row, 1.0, 0.0)
        named = named + contract(owner_hot, row_hot.astype(BF16), 1, 1)
        owners.append((owner, owner_hot))
        lanes.append(row_hot)
    marked = jnp.where(named > 0.0, 1.0, 0.0)
    rank = contract(marked.astype(BF16), earlier(SLAB), 1, 0).astype(BF16)
    places = []
    for slot in range(FAN + 1):
        owner, owner_hot = owners[slot]
        mine = jnp.sum(contract(rank, owner_hot, 0, 0) * lanes[slot], axis=0, keepdims=True)
        places.append(owner * UNION + mine.astype(jnp.int32))
    place[...] = jnp.concatenate(places + [jnp.zeros((5, TARGETS), jnp.int32)], axis=0)

    fetches[2].wait()
    fetches[3].wait()
    shared = weights[...].astype(F32)
    shared = jnp.where(core[0] == 0, shared[:, :, :128], shared[:, :, 128:])
    shared = shared.reshape(2 * WIDTH, 128)
    for pair in range(FEAT // 2):
        block = features[:, pl.ds(pair * 2 * OWN, 2 * OWN)].astype(F32)
        for half in range(2):
            owner = 2 * pair + half
            marks = [marked[owner : owner + 1, k * 64 : (k + 1) * 64] for k in range(3)]
            last = jnp.concatenate(marks + [jnp.zeros((5, 64), F32)], axis=0)
            built[owner] = jnp.concatenate([shared, folded(block, half, last)], axis=0).astype(BF16)
        if pair % 4 == 3:
            copies_out(built, send, sent, pair // 4).start()
    fetches[4].wait()
    fetches[5].wait()
    order_rows(given, filled, lists, ranks, columns)
    for step in range(FEAT // 8):
        copies_out(built, send, sent, step).wait()


def order_rows(neighbours, mask, lists, ranks, columns):
    used = [jnp.where(mask[slot] > 0, 1, 0) for slot in range(FAN)]
    before = [jnp.zeros((LINES, 128), jnp.int32)]
    for slot in range(FAN):
        before.append(before[slot] + used[slot])
    count = before[FAN]
    for place in range(FAN):
        node = jnp.where(count > place, 0, INPUTS)
        for slot in range(place, FAN):
            here = (used[slot] > 0) & (before[slot] == place)
            node = node + jnp.where(here, neighbours[slot], 0)
        high = node >> 8
        columns[place] = high.astype(F32)
        columns[16 + place] = (node - high * 256).astype(F32)
    columns[FAN] = jnp.zeros((LINES, 128), F32)
    columns[16 + FAN] = count.astype(F32)
    hot = [jnp.where(count == amount, 1.0, 0.0) for amount in range(FAN + 1)]
    stacked = jnp.concatenate(hot, axis=0).astype(BF16)
    second = iota(((FAN + 1) * LINES, 128), 0) % 2 == 1
    earlier_same = contract(stacked, earlier(128), 1, 0)
    all_same = contract(stacked, jnp.ones((128, 128), BF16), 1, 0)
    above = pltpu.roll(all_same, 1, 0)
    below = pltpu.roll(all_same, (FAN + 1) * LINES - 1, 0)
    earlier_same = earlier_same + jnp.where(second, above, 0.0)
    all_same = all_same + jnp.where(second, above, below)
    rank = jnp.zeros((LINES, 128), F32)
    higher = jnp.zeros((LINES, 128), F32)
    for amount in reversed(range(FAN + 1)):
        span = slice(amount * LINES, (amount + 1) * LINES)
        rank = rank + hot[amount] * (earlier_same[span] + higher)
        higher = higher + all_same[span]
    ranks[...] = rank.astype(jnp.int32)
    for line in range(0, LINES, 2):
        part = contract(columns[:, line, :].astype(BF16), moved(ranks, line), 1, 1)
        part += contract(columns[:, line + 1, :].astype(BF16), moved(ranks, line + 1), 1, 1)
        part = (part[:16] * 256.0 + part[16:]).astype(jnp.int32)
        first = line // 8 * 8 * (FAN + 1) + line % 8
        for half in range(2):
            here = part[: FAN + 1, half * 128 : (half + 1) * 128]
            lists[pl.ds(first + half, FAN + 1, stride=8), :] = here


def copies_out(built, send, sent, step):
    span = pl.ds(step * 8, 8)
    return pltpu.make_async_copy(built.at[span], send.at[span], sent.at[step])


def folded(block, half, last):
    rest = block[:, 128 + half * 64 : 192 + half * 64]
    rest = jnp.concatenate([rest[:24], jnp.concatenate([rest[24:], last], axis=0)], axis=1)
    return jnp.concatenate([block[:, half * 256 : half * 256 + 128], rest], axis=0)


def moved(ranks, line):
    return jnp.where(iota((256, 128), 0) == ranks[pl.ds(line, 1), :], 1.0, 0.0).astype(BF16)


def mean_of(flipped):
    thirds = [flipped[t * WIDTH : (t + 1) * WIDTH] for t in range(3)]
    return (thirds[0] + thirds[1] + thirds[2]) / jnp.maximum(flipped[3 * WIDTH : 3 * WIDTH + 1], 1.0)


def gather_kernel(
    slots, ranks, source, send, table, sums, lists, built, features, arrived, loaded, sent
):
    size = (FAN + 1) * CHUNK

    def fetch(chunk):
        span = pl.ds(pl.multiple_of(chunk * size, size), size)
        return pltpu.make_async_copy(slots.at[span], lists.at[span], arrived.at[chunk])

    third = INPUTS // 3
    piece = 128 * TABLE_STEP

    def load(step, t):
        span = pl.ds(pl.multiple_of(t * third + step * piece, piece), piece)
        return pltpu.make_async_copy(source.at[:, span], features.at[:, span], loaded.at[step, t])

    fetch(0).start()
    for step in range(third // piece):
        for t in range(3):
            load(step, t).start()
    for chunk in range(1, ROWS // CHUNK):
        fetch(chunk).start()

    lane = iota((128, 128), 1)

    def fill(step, carry):
        for t in range(3):
            load(step, t).wait()
        for part in range(TABLE_STEP):
            at = pl.multiple_of((step * TABLE_STEP + part) * 128, 128)
            blocks = [features[:, pl.ds(t * third + at, 128)].astype(F32) for t in range(3)]
            flipped = jnp.concatenate(blocks + [jnp.ones((8, 128), F32)], axis=0).T
            for t in range(3):
                kept = ((lane >= t * WIDTH) & (lane < (t + 1) * WIDTH)) | (lane >= 3 * WIDTH)
                table[pl.ds(t * third + at, 128), :] = jnp.where(kept, flipped, 0.0)
        return carry

    lax.fori_loop(0, third // 128 // TABLE_STEP, fill, 0)
    table[pl.ds(INPUTS, 8), :] = jnp.zeros((8, 128), F32)

    def chunk_step(chunk, carry):
        fetch(chunk).wait()

        def block(step, inner):
            first = chunk * size + step * UNROLL
            at = pl.multiple_of(chunk * CHUNK + step * UNROLL, UNROLL)
            result = sums.at[pl.ds(at, UNROLL), :]

            def add(depth):
                named = [lists.at[pl.ds(first + slot * CHUNK, UNROLL)] for slot in range(depth)]
                for row in range(UNROLL):
                    result[pl.ds(row, 1), :] = add_all(
                        [table[pl.ds(named[slot][row], 1), :] for slot in range(depth)]
                    )

            def choose(low, high):
                if low == high:
                    add(low)
                    return
                middle = (low + high) // 2
                lax.cond(
                    deepest <= middle,
                    lambda: choose(low, middle),
                    lambda: choose(middle + 1, high),
                )

            deepest = lists[first + FAN * CHUNK]
            choose(LEAST, FAN)
            return inner

        return lax.fori_loop(0, CHUNK // UNROLL, block, carry)

    lax.fori_loop(0, ROWS // CHUNK, chunk_step, 0)

    def pair_step(step, carry):
        for part in range(0, PAIRS, 2):
            line = (step * PAIRS + part) * 3
            blocks = []
            for k in range(0, 6, 2):
                at = pl.multiple_of((line + k) * 128, 128)
                means = [mean_of(sums[pl.ds(at + half * 128, 128), :].T) for half in range(2)]
                means = jnp.concatenate(means, axis=1).astype(BF16)
                for half in range(2):
                    blocks.append(contract(means, moved(ranks, line + k + half), 1, 0))
            for pair in range(2):
                block = jnp.concatenate(blocks[pair * 3 : pair * 3 + 3], axis=1)
                owner = 2 * (step * PAIRS + part + pair)
                for half in range(2):
                    tile = folded(block, half, jnp.zeros((8, 64), F32))
                    built[owner + half] = tile.astype(BF16)
        copies_out(built, send, sent, step).start()
        return carry

    lax.fori_loop(0, FEAT // 2 // PAIRS, pair_step, 0)
    for step in range(FEAT // 8):
        copies_out(built, send, sent, step).wait()


def hidden_kernel(
    spot, mine, theirs, means, bias, hidden, rows, stacked, held, other, marks, chosen
):
    for source in range(FEAT):
        own = mine[source].astype(F32)
        mean = means[source].astype(F32)
        held[pl.ds(source * 80, 80), :] = own[:80].astype(BF16)
        other[pl.ds(source * 80, 80), :] = theirs[source].astype(F32).astype(BF16)
        last, mean_last = own[120:144], mean[40:64]
        stacked[pl.ds(source * 80, 80), pl.ds(0, 128)] = jnp.concatenate(
            [own[80:120], mean[:40]], axis=0
        ).astype(BF16)
        stacked[pl.ds(source * 80, 80), pl.ds(128, 64)] = jnp.concatenate(
            [last[:, :64], last[:16, 64:], mean_last[:, :64], mean_last[:16, 64:]], axis=0
        ).astype(BF16)
        marks[pl.ds(source, 1), :] = jnp.concatenate(
            [last[16:17, 64:], last[17:18, 64:], last[18:19, 64:], jnp.zeros((1, 64), F32)], axis=1
        )
    stacked[:, pl.ds(192, 64)] = jnp.zeros((FEAT * 80, 64), BF16)
    first = contract(stacked[...], held[...], 0, 0)[:OWN]
    second = contract(stacked[...], other[...], 0, 0)[:OWN]
    even = spot[0] == 0
    pre = jnp.concatenate(
        [jnp.where(even, first, second), jnp.where(even, second, first)], axis=1
    )
    pre = jnp.where(spot[1] == 0, pre, jnp.concatenate([pre[128:], pre[:128]], axis=0))
    result = jnp.maximum(pre + bias[...], 0.0).astype(BF16)
    hidden[...] = result
    rank = contract(marks[...].astype(BF16), earlier(SLAB), 1, 0)
    for source in range(FEAT):
        hit = (iota((UNION, SLAB), 0).astype(F32) == rank[source : source + 1]) & (
            marks[pl.ds(source, 1), :] > 0.0
        )
        chosen[pl.ds(source * UNION, UNION), :] = jnp.where(hit, 1.0, 0.0)
    padded = jnp.concatenate([result, jnp.zeros((SLAB - OWN, HIDDEN), BF16)], axis=0)
    rows[...] = contract(chosen[...].astype(BF16), padded, 1, 0).astype(BF16)


def pick_kernel(place, mask, labels, picks):
    spots = iota((NAMED, TARGETS), 0)
    total = jnp.zeros((NAMED, TARGETS), F32)
    for slot in range(FAN):
        used = mask[slot].astype(F32)
        total = total + jnp.where(spots == place[pl.ds(slot, 1), :], used, 0.0)
    own = jnp.where(spots == place[pl.ds(FAN, 1), :], 1.0, 0.0)
    line = iota((16, TARGETS), 0)
    label = jnp.broadcast_to(labels[...], (16, TARGETS))
    high = label >> 7
    parts = jnp.where(line == 0, high, jnp.where(line == 1, label - high * 128, 0))
    blank = jnp.zeros((16, TARGETS), F32)
    picks[0] = jnp.concatenate([total, parts.astype(F32)], axis=0).astype(BF16)
    picks[1] = jnp.concatenate([own, blank], axis=0).astype(BF16)


def loss_kernel(spot, *refs):
    held, blocks = refs[:4], refs[4 : 4 + NODE // 2]
    stats, other, inputs, logits = refs[4 + NODE // 2 :]
    offsets = []
    for side in range(2):
        rows, picks = held[2 * side], held[2 * side + 1]
        total, own = picks[0][:NAMED], picks[1][:NAMED]
        count = contract(total, jnp.ones((NAMED, 128), BF16), 0, 0)[:, :1]
        agg = contract(total, rows[...], 0, 0) / jnp.maximum(count, 1.0)
        span = pl.ds(side * TARGETS, TARGETS)
        inputs[span, pl.ds(0, HIDDEN)] = contract(own, rows[...], 0, 0).astype(BF16)
        inputs[span, pl.ds(HIDDEN, HIDDEN)] = agg.astype(BF16)
        parts = picks[0][NAMED:].astype(F32)
        label = jnp.broadcast_to(parts[:1] * 128.0 + parts[1:2], (TARGETS, TARGETS)).T
        offsets.append(label.astype(jnp.int32) - iota((TARGETS, TARGETS), 1))
    width = blocks[0].shape[1]
    start = (
        jnp.full((TARGETS, TARGETS), -jnp.inf, F32),
        jnp.zeros((TARGETS, TARGETS), F32),
        jnp.zeros((TARGETS, TARGETS), F32),
    )
    running = [start, start]
    for step in range(2 * len(blocks) + 1):
        block, side = step // 2, step % 2
        if block < len(blocks):
            mine = inputs[pl.ds(side * TARGETS, TARGETS), :]
            logits[step % 2] = contract(mine, blocks[block][...], 1, 0)
        if step > 0:
            block, side = (step - 1) // 2, (step - 1) % 2
            last = logits.at[(step - 1) % 2]
            largest, summed, picked = running[side]
            spans = [pl.ds(k * 128, 128) for k in range(width // 128)]
            here = offsets[side] - ((spot[0] + HOPS[block]) & 7) * width
            now = largest
            for span in spans:
                now = jnp.maximum(now, last[:, span])
            summed = summed * jnp.exp(largest - now)
            for k, span in enumerate(spans):
                part = last[:, span]
                summed = summed + jnp.exp(part - now)
                picked = picked + jnp.where(here == k * 128, part, 0.0)
            running[side] = (now, summed, picked)
    for side, ref in ((0, stats), (1, other)):
        largest, summed, picked = running[side]
        most = jnp.max(largest, axis=1, keepdims=True)
        total = jnp.sum(summed * jnp.exp(largest - most), axis=1, keepdims=True)
        found = jnp.sum(picked, axis=1, keepdims=True)
        lane = iota((TARGETS, TARGETS), 1)
        table = jnp.where(lane == 0, most, jnp.where(lane == 1, total, found))
        ref[...] = table.T[:8]


VMEM = pl.BlockSpec(memory_space=pltpu.VMEM)
HBM = pl.BlockSpec(memory_space=pltpu.HBM)
SMEM = pl.BlockSpec(memory_space=pltpu.SMEM)


def call_prepare(core, arrays):
    shapes = [array.shape for array in arrays]
    shapes[3] = (WIDTH, ROWS)
    return pl.pallas_call(
        prepare_kernel,
        out_shape=(
            jax.ShapeDtypeStruct((FEAT, 144, 128), BF16),
            jax.ShapeDtypeStruct((16, TARGETS), jnp.int32),
            jax.ShapeDtypeStruct((LINES * (FAN + 1), 128), jnp.int32),
            jax.ShapeDtypeStruct((LINES, 128), jnp.int32),
        ),
        in_specs=[SMEM] + [HBM] * 6,
        out_specs=(HBM, VMEM, VMEM, VMEM),
        scratch_shapes=[
            *[pltpu.VMEM(shape, array.dtype) for shape, array in zip(shapes, arrays)],
            pltpu.VMEM((FEAT, 144, 128), BF16),
            pltpu.VMEM((32, LINES, 128), F32),
            pltpu.SemaphoreType.DMA((FEAT // 8,)),
            pltpu.SemaphoreType.DMA((6,)),
        ],
        compiler_params=pltpu.CompilerParams(vmem_limit_bytes=MOST),
        cost_estimate=pl.CostEstimate(flops=10**8, bytes_accessed=10**7, transcendentals=0),
    )(core, *arrays)


def call_gather(slots, ranks, table):
    return pl.pallas_call(
        gather_kernel,
        out_shape=jax.ShapeDtypeStruct((FEAT, 64, 128), BF16),
        in_specs=[pl.BlockSpec(memory_space=pl.ANY), VMEM, HBM],
        out_specs=HBM,
        scratch_shapes=[
            pltpu.VMEM((INPUTS + 8, 128), F32),
            pltpu.VMEM((ROWS, 128), F32),
            pltpu.SMEM(((FAN + 1) * ROWS,), jnp.int32),
            pltpu.VMEM((FEAT, 64, 128), BF16),
            pltpu.VMEM((WIDTH, INPUTS), BF16),
            pltpu.SemaphoreType.DMA((ROWS // CHUNK,)),
            pltpu.SemaphoreType.DMA((INPUTS // 3 // 128 // TABLE_STEP, 3)),
            pltpu.SemaphoreType.DMA((FEAT // 8,)),
        ],
        compiler_params=pltpu.CompilerParams(vmem_limit_bytes=MOST),
        cost_estimate=pl.CostEstimate(flops=0, bytes_accessed=0, transcendentals=0),
    )(slots, ranks, table)


def call_pick(place, mask, labels):
    return pl.pallas_call(
        pick_kernel,
        out_shape=jax.ShapeDtypeStruct((2, NAMED + 16, TARGETS), BF16),
        in_specs=[VMEM] * 3,
        out_specs=VMEM,
        compiler_params=pltpu.CompilerParams(vmem_limit_bytes=16 * 2**20),
        cost_estimate=pl.CostEstimate(flops=10**7, bytes_accessed=4 * 10**6, transcendentals=0),
    )(place, mask, labels)


def call_loss(spot, rows, picks, rows_there, picks_there, blocks):
    sources = [rows, picks, rows_there, picks_there, *blocks]
    return pl.pallas_call(
        loss_kernel,
        out_shape=[jax.ShapeDtypeStruct((8, TARGETS), F32)] * 2,
        in_specs=[SMEM] + [VMEM] * len(sources),
        out_specs=[VMEM, VMEM],
        scratch_shapes=[
            pltpu.VMEM((2 * TARGETS, 2 * HIDDEN), BF16),
            pltpu.VMEM((2, TARGETS, blocks[0].shape[1]), F32),
        ],
        compiler_params=pltpu.CompilerParams(vmem_limit_bytes=16 * 2**20),
    )(spot, *sources)


def join_kernel(here, there, loss):
    most = jnp.maximum(here[0:1], there[0:1])
    total = here[1:2] * jnp.exp(here[0:1] - most) + there[1:2] * jnp.exp(there[0:1] - most)
    loss[...] = most + jnp.log(total) - (here[2:3] + there[2:3])


def call_join(here, there):
    return pl.pallas_call(
        join_kernel,
        out_shape=jax.ShapeDtypeStruct((1, TARGETS), F32),
        in_specs=[VMEM, VMEM],
        out_specs=VMEM,
        compiler_params=pltpu.CompilerParams(vmem_limit_bytes=2**20),
    )(here, there)


def body(
    features,
    first_neighbours,
    first_mask,
    second_neighbours,
    second_mask,
    target_index,
    labels,
    first_weight,
    first_bias,
    class_weight,
):
    spot = lax.axis_index("node").astype(jnp.int32)
    core = spot & 1
    table = features[:, 0, :]
    swap = [(device, device ^ 1) for device in range(NODE)]
    blocks = [class_weight]
    for hops in HOPS[1:]:
        around = [(device, (device - hops) % NODE) for device in range(NODE)]
        blocks.append(lax.ppermute(class_weight, "node", around))
    own, place, slots, ranks = call_prepare(
        core[None],
        [
            second_neighbours,
            target_index,
            first_weight,
            table,
            first_neighbours.reshape(FAN, LINES, 128),
            first_mask.reshape(FAN, LINES, 128),
        ],
    )
    own = lax.all_to_all(own, "feat", 0, 0)
    send = call_gather(slots.reshape(-1), ranks, table)
    theirs = lax.ppermute(own[:, : 2 * WIDTH], "node", swap)
    means = lax.all_to_all(send, "feat", 0, 0)
    means, *blocks[2:] = lax.optimization_barrier((means, *blocks[2:]))
    side = jnp.stack([core, lax.axis_index("feat").astype(jnp.int32) & 1])
    hidden, rows = pl.pallas_call(
        hidden_kernel,
        out_shape=(
            jax.ShapeDtypeStruct((OWN, HIDDEN), BF16),
            jax.ShapeDtypeStruct((FEAT * UNION, HIDDEN), BF16),
        ),
        in_specs=[SMEM] + [VMEM] * 4,
        out_specs=(VMEM, VMEM),
        scratch_shapes=[
            pltpu.VMEM((FEAT * 80, 256), BF16),
            pltpu.VMEM((FEAT * 80, 128), BF16),
            pltpu.VMEM((FEAT * 80, 128), BF16),
            pltpu.VMEM((FEAT, SLAB), F32),
            pltpu.VMEM((FEAT * UNION, SLAB), F32),
        ],
        compiler_params=pltpu.CompilerParams(vmem_limit_bytes=24 * 2**20),
    )(side, own, theirs, means, first_bias[None, :])
    picks = call_pick(place, second_mask, labels)
    picks_there = lax.ppermute(picks, "node", swap)
    rows = lax.all_to_all(rows.reshape(FEAT, UNION, HIDDEN), "feat", 0, 0)
    rows = rows.reshape(FEAT * UNION, HIDDEN)
    rows_there = lax.ppermute(rows, "node", swap)
    here, there = call_loss(spot[None], rows, picks, rows_there, picks_there, blocks)
    there = lax.ppermute(there, "node", swap)
    loss = call_join(here, there)
    return (hidden[None], loss)


def solution(mesh):
    placed = (
        P("feat", "node", None),
        P(None, "node", None),
        P(None, "node", None),
        P(None, "node", "feat"),
        P(None, "node", "feat"),
        P("node", "feat"),
        P("node", "feat"),
        P(None, "feat", None),
        P(),
        P(None, "node"),
    )
    return jax.shard_map(
        body,
        mesh=mesh,
        in_specs=placed,
        out_specs=(P("node", "feat", None), P("node", "feat")),
        check_vma=False,
    )
```

```python
import functools

import jax
import jax.numpy as jnp
from jax import lax
from jax.experimental import pallas as pl
from jax.experimental.pallas import tpu as pltpu
from jax.sharding import PartitionSpec as P

FEAT = 32
NODE = 8
WIDTH = 40
INPUTS = 24576
ROWS = 6144
OWN = 192
FAN = 10
TARGETS = 128
HIDDEN = 256
UNION = 24
NAMED = FEAT * UNION
SLAB = 256
HOPS = (0, 4, 6, 2)
UNROLL = 64
LEAST = 3
LINES = ROWS // 128
CHUNK = 1024
PAIRS = 4
TABLE_STEP = 16
MOST = 60 * 2**20
F32 = jnp.float32
BF16 = jnp.bfloat16


def iota(shape, dim):
    return lax.broadcasted_iota(jnp.int32, shape, dim)


def contract(a, b, dim_a, dim_b):
    return lax.dot_general(a, b, (((dim_a,), (dim_b,)), ((), ())), preferred_element_type=F32)


def earlier(size):
    return jnp.where(iota((size, size), 0) < iota((size, size), 1), 1.0, 0.0).astype(BF16)


def add_all(terms):
    while len(terms) > 1:
        paired = [terms[k] + terms[k + 1] for k in range(0, len(terms) - 1, 2)]
        terms = paired + terms[len(terms) - len(terms) % 2 :]
    return terms[0]


def prepare_kernel(core, *refs):
    sources, (send, place, lists, ranks), held, (built, columns, sent, arrived) = (
        refs[:6],
        refs[6:10],
        refs[10:16],
        refs[16:],
    )
    fetches = []
    for source, ref in zip(sources, held):
        part = source if source.shape == ref.shape else source.at[:, pl.ds(0, ROWS)]
        fetches.append(pltpu.make_async_copy(part, ref, arrived.at[len(fetches)]))
        fetches[-1].start()
    neighbours, targets, weights, features, given, filled = held
    fetches[0].wait()
    fetches[1].wait()
    owners, lanes = [], []
    named = jnp.zeros((FEAT, SLAB), F32)
    for slot in range(FAN + 1):
        index = neighbours[slot] if slot < FAN else targets[...]
        owner = ((index.astype(F32) + 0.5) * (1.0 / OWN)).astype(jnp.int32)
        row = index - owner * OWN
        owner_hot = jnp.where(iota((FEAT, TARGETS), 0) == owner, 1.0, 0.0).astype(BF16)
        row_hot = jnp.where(iota((SLAB, TARGETS), 0) == row, 1.0, 0.0)
        named = named + contract(owner_hot, row_hot.astype(BF16), 1, 1)
        owners.append((owner, owner_hot))
        lanes.append(row_hot)
    marked = jnp.where(named > 0.0, 1.0, 0.0)
    rank = contract(marked.astype(BF16), earlier(SLAB), 1, 0).astype(BF16)
    places = []
    for slot in range(FAN + 1):
        owner, owner_hot = owners[slot]
        mine = jnp.sum(contract(rank, owner_hot, 0, 0) * lanes[slot], axis=0, keepdims=True)
        places.append(owner * UNION + mine.astype(jnp.int32))
    place[...] = jnp.concatenate(places + [jnp.zeros((5, TARGETS), jnp.int32)], axis=0)

    fetches[2].wait()
    fetches[3].wait()
    shared = weights[...].astype(F32)
    shared = jnp.where(core[0] == 0, shared[:, :, :128], shared[:, :, 128:])
    shared = shared.reshape(2 * WIDTH, 128)
    for pair in range(FEAT // 2):
        block = features[:, pl.ds(pair * 2 * OWN, 2 * OWN)].astype(F32)
        for half in range(2):
            owner = 2 * pair + half
            marks = [marked[owner : owner + 1, k * 64 : (k + 1) * 64] for k in range(3)]
            last = jnp.concatenate(marks + [jnp.zeros((5, 64), F32)], axis=0)
            built[owner] = jnp.concatenate([shared, folded(block, half, last)], axis=0).astype(BF16)
        if pair % 4 == 3:
            copies_out(built, send, sent, pair // 4).start()
    fetches[4].wait()
    fetches[5].wait()
    order_rows(given, filled, lists, ranks, columns)
    for step in range(FEAT // 8):
        copies_out(built, send, sent, step).wait()


def order_rows(neighbours, mask, lists, ranks, columns):
    used = [jnp.where(mask[slot] > 0, 1, 0) for slot in range(FAN)]
    before = [jnp.zeros((LINES, 128), jnp.int32)]
    for slot in range(FAN):
        before.append(before[slot] + used[slot])
    count = before[FAN]
    for place in range(FAN):
        node = jnp.where(count > place, 0, INPUTS)
        for slot in range(place, FAN):
            here = (used[slot] > 0) & (before[slot] == place)
            node = node + jnp.where(here, neighbours[slot], 0)
        high = node >> 8
        columns[place] = high.astype(F32)
        columns[16 + place] = (node - high * 256).astype(F32)
    columns[FAN] = jnp.zeros((LINES, 128), F32)
    columns[16 + FAN] = count.astype(F32)
    hot = [jnp.where(count == amount, 1.0, 0.0) for amount in range(FAN + 1)]
    stacked = jnp.concatenate(hot, axis=0).astype(BF16)
    second = iota(((FAN + 1) * LINES, 128), 0) % 2 == 1
    earlier_same = contract(stacked, earlier(128), 1, 0)
    all_same = contract(stacked, jnp.ones((128, 128), BF16), 1, 0)
    above = pltpu.roll(all_same, 1, 0)
    below = pltpu.roll(all_same, (FAN + 1) * LINES - 1, 0)
    earlier_same = earlier_same + jnp.where(second, above, 0.0)
    all_same = all_same + jnp.where(second, above, below)
    rank = jnp.zeros((LINES, 128), F32)
    higher = jnp.zeros((LINES, 128), F32)
    for amount in reversed(range(FAN + 1)):
        span = slice(amount * LINES, (amount + 1) * LINES)
        rank = rank + hot[amount] * (earlier_same[span] + higher)
        higher = higher + all_same[span]
    ranks[...] = rank.astype(jnp.int32)
    for line in range(0, LINES, 2):
        part = contract(columns[:, line, :].astype(BF16), moved(ranks, line), 1, 1)
        part += contract(columns[:, line + 1, :].astype(BF16), moved(ranks, line + 1), 1, 1)
        part = (part[:16] * 256.0 + part[16:]).astype(jnp.int32)
        first = line // 8 * 8 * (FAN + 1) + line % 8
        for half in range(2):
            here = part[: FAN + 1, half * 128 : (half + 1) * 128]
            lists[pl.ds(first + half, FAN + 1, stride=8), :] = here


def copies_out(built, send, sent, step):
    span = pl.ds(step * 8, 8)
    return pltpu.make_async_copy(built.at[span], send.at[span], sent.at[step])


def folded(block, half, last):
    rest = block[:, 128 + half * 64 : 192 + half * 64]
    rest = jnp.concatenate([rest[:24], jnp.concatenate([rest[24:], last], axis=0)], axis=1)
    return jnp.concatenate([block[:, half * 256 : half * 256 + 128], rest], axis=0)


def moved(ranks, line):
    return jnp.where(iota((256, 128), 0) == ranks[pl.ds(line, 1), :], 1.0, 0.0).astype(BF16)


def mean_of(flipped):
    thirds = [flipped[t * WIDTH : (t + 1) * WIDTH] for t in range(3)]
    return (thirds[0] + thirds[1] + thirds[2]) / jnp.maximum(flipped[3 * WIDTH : 3 * WIDTH + 1], 1.0)


def gather_kernel(
    slots, ranks, features, send, table, sums, lists, arrived
):
    size = (FAN + 1) * CHUNK

    def fetch(chunk):
        span = pl.ds(pl.multiple_of(chunk * size, size), size)
        return pltpu.make_async_copy(slots.at[span], lists.at[span], arrived.at[chunk])

    third = INPUTS // 3
    fetch(0).start()
    for chunk in range(1, ROWS // CHUNK):
        fetch(chunk).start()

    lane = iota((128, 128), 1)

    def fill(step, carry):
        for part in range(TABLE_STEP):
            at = pl.multiple_of((step * TABLE_STEP + part) * 128, 128)
            blocks = [features[:, pl.ds(t * third + at, 128)].astype(F32) for t in range(3)]
            flipped = jnp.concatenate(blocks + [jnp.ones((8, 128), F32)], axis=0).T
            for t in range(3):
                kept = ((lane >= t * WIDTH) & (lane < (t + 1) * WIDTH)) | (lane >= 3 * WIDTH)
                table[pl.ds(t * third + at, 128), :] = jnp.where(kept, flipped, 0.0)
        return carry

    lax.fori_loop(0, third // 128 // TABLE_STEP, fill, 0)
    table[pl.ds(INPUTS, 8), :] = jnp.zeros((8, 128), F32)

    def chunk_step(chunk, carry):
        fetch(chunk).wait()

        def block(step, inner):
            first = chunk * size + step * UNROLL
            at = pl.multiple_of(chunk * CHUNK + step * UNROLL, UNROLL)
            result = sums.at[pl.ds(at, UNROLL), :]

            def add(depth):
                named = [lists.at[pl.ds(first + slot * CHUNK, UNROLL)] for slot in range(depth)]
                for row in range(UNROLL):
                    result[pl.ds(row, 1), :] = add_all(
                        [table[pl.ds(named[slot][row], 1), :] for slot in range(depth)]
                    )

            def choose(low, high):
                if low == high:
                    add(low)
                    return
                middle = (low + high) // 2
                lax.cond(
                    deepest <= middle,
                    lambda: choose(low, middle),
                    lambda: choose(middle + 1, high),
                )

            deepest = lists[first + FAN * CHUNK]
            choose(LEAST, FAN)
            return inner

        return lax.fori_loop(0, CHUNK // UNROLL, block, carry)

    lax.fori_loop(0, ROWS // CHUNK, chunk_step, 0)

    def pair_step(step, carry):
        for part in range(0, PAIRS, 2):
            line = (step * PAIRS + part) * 3
            blocks = []
            for k in range(0, 6, 2):
                at = pl.multiple_of((line + k) * 128, 128)
                means = [mean_of(sums[pl.ds(at + half * 128, 128), :].T) for half in range(2)]
                means = jnp.concatenate(means, axis=1).astype(BF16)
                for half in range(2):
                    blocks.append(contract(means, moved(ranks, line + k + half), 1, 0))
            for pair in range(2):
                block = jnp.concatenate(blocks[pair * 3 : pair * 3 + 3], axis=1)
                owner = 2 * (step * PAIRS + part + pair)
                for half in range(2):
                    tile = folded(block, half, jnp.zeros((8, 64), F32))
                    send[owner + half] = tile.astype(BF16)
        return carry

    lax.fori_loop(0, FEAT // 2 // PAIRS, pair_step, 0)


def unfolded(tile):
    rest = jnp.concatenate([tile[40:64, :64], tile[40:56, 64:]], axis=0)
    return jnp.concatenate([tile[:40], rest, jnp.zeros((40, 64), F32)], axis=1)


def choose_kernel(own, chosen, marks):
    for source in range(FEAT):
        last = own[source, pl.ds(128, 16), :].astype(F32)
        marks[pl.ds(source, 1), :] = jnp.concatenate(
            [last[8 + k : 9 + k, 64:] for k in range(3)] + [jnp.zeros((1, 64), F32)], axis=1
        )
    rank = contract(marks[...].astype(BF16), earlier(SLAB), 1, 0)
    for pair in range(FEAT // 2):
        hits = []
        for source in (2 * pair, 2 * pair + 1):
            hit = (iota((UNION, SLAB), 0).astype(F32) == rank[source : source + 1]) & (
                marks[pl.ds(source, 1), :] > 0.0
            )
            hits.append(jnp.where(hit, 1.0, 0.0))
        chosen[pl.ds(pair * 2 * UNION, 2 * UNION), :] = jnp.concatenate(hits, axis=0).astype(BF16)


def hidden_kernel(spot, own, means, mine, theirs, bias, chosen, hidden, rows, stacked):
    for source in range(FEAT):
        tiles = [unfolded(own[source].astype(F32)[80:]), unfolded(means[source].astype(F32))]
        stacked[pl.ds(source * 80, 80), :] = jnp.concatenate(tiles, axis=0).astype(BF16)
    first = contract(stacked[...], mine[...], 0, 0)[:OWN]
    second = contract(stacked[...], theirs[...], 0, 0)[:OWN]
    even = spot[0] == 0
    pre = jnp.concatenate(
        [jnp.where(even, first, second), jnp.where(even, second, first)], axis=1
    )
    pre = jnp.where(spot[1] == 0, pre, jnp.concatenate([pre[128:], pre[:128]], axis=0))
    result = jnp.maximum(pre + bias[...], 0.0).astype(BF16)
    hidden[...] = result
    padded = jnp.concatenate([result, jnp.zeros((SLAB - OWN, HIDDEN), BF16)], axis=0)
    rows[...] = contract(chosen[...], padded, 1, 0).astype(BF16)


def pick_kernel(place, mask, labels, block, picks, held, arrived):
    copy = pltpu.make_async_copy(block, held, arrived)
    copy.start()
    spots = iota((NAMED, TARGETS), 0)
    total = jnp.zeros((NAMED, TARGETS), F32)
    for slot in range(FAN):
        used = mask[slot].astype(F32)
        total = total + jnp.where(spots == place[pl.ds(slot, 1), :], used, 0.0)
    own = jnp.where(spots == place[pl.ds(FAN, 1), :], 1.0, 0.0)
    line = iota((16, TARGETS), 0)
    label = jnp.broadcast_to(labels[...], (16, TARGETS))
    high = label >> 7
    parts = jnp.where(line == 0, high, jnp.where(line == 1, label - high * 128, 0))
    blank = jnp.zeros((16, TARGETS), F32)
    picks[0] = jnp.concatenate([total, parts.astype(F32)], axis=0).astype(BF16)
    picks[1] = jnp.concatenate([own, blank], axis=0).astype(BF16)
    copy.wait()


def loss_kernel(spot, *refs):
    held, blocks = refs[:4], refs[4 : 4 + NODE // 2]
    stats, other, inputs, logits = refs[4 + NODE // 2 :]
    offsets = []
    for side in range(2):
        rows, picks = held[2 * side], held[2 * side + 1]
        total, own = picks[0][:NAMED], picks[1][:NAMED]
        count = contract(total, jnp.ones((NAMED, 128), BF16), 0, 0)[:, :1]
        agg = contract(total, rows[...], 0, 0) / jnp.maximum(count, 1.0)
        span = pl.ds(side * TARGETS, TARGETS)
        inputs[span, pl.ds(0, HIDDEN)] = contract(own, rows[...], 0, 0).astype(BF16)
        inputs[span, pl.ds(HIDDEN, HIDDEN)] = agg.astype(BF16)
        parts = picks[0][NAMED:].astype(F32)
        label = jnp.broadcast_to(parts[:1] * 128.0 + parts[1:2], (TARGETS, TARGETS)).T
        offsets.append(label.astype(jnp.int32) - iota((TARGETS, TARGETS), 1))
    width = blocks[0].shape[1]
    start = (
        jnp.full((TARGETS, TARGETS), -jnp.inf, F32),
        jnp.zeros((TARGETS, TARGETS), F32),
        jnp.zeros((TARGETS, TARGETS), F32),
    )
    running = [start, start]
    for step in range(2 * len(blocks) + 1):
        block, side = step // 2, step % 2
        if block < len(blocks):
            mine = inputs[pl.ds(side * TARGETS, TARGETS), :]
            logits[step % 2] = contract(mine, blocks[block][...], 1, 0)
        if step > 0:
            block, side = (step - 1) // 2, (step - 1) % 2
            last = logits.at[(step - 1) % 2]
            largest, summed, picked = running[side]
            spans = [pl.ds(k * 128, 128) for k in range(width // 128)]
            here = offsets[side] - ((spot[0] + HOPS[block]) & 7) * width
            now = largest
            for span in spans:
                now = jnp.maximum(now, last[:, span])
            summed = summed * jnp.exp(largest - now)
            for k, span in enumerate(spans):
                part = last[:, span]
                summed = summed + jnp.exp(part - now)
                picked = picked + jnp.where(here == k * 128, part, 0.0)
            running[side] = (now, summed, picked)
    for side, ref in ((0, stats), (1, other)):
        largest, summed, picked = running[side]
        most = jnp.max(largest, axis=1, keepdims=True)
        total = jnp.sum(summed * jnp.exp(largest - most), axis=1, keepdims=True)
        found = jnp.sum(picked, axis=1, keepdims=True)
        lane = iota((TARGETS, TARGETS), 1)
        table = jnp.where(lane == 0, most, jnp.where(lane == 1, total, found))
        ref[...] = table.T[:8]


VMEM = pl.BlockSpec(memory_space=pltpu.VMEM)
HBM = pl.BlockSpec(memory_space=pltpu.HBM)
SMEM = pl.BlockSpec(memory_space=pltpu.SMEM)


def call_prepare(core, arrays):
    shapes = [array.shape for array in arrays]
    shapes[3] = (WIDTH, ROWS)
    return pl.pallas_call(
        prepare_kernel,
        out_shape=(
            jax.ShapeDtypeStruct((FEAT, 144, 128), BF16),
            jax.ShapeDtypeStruct((16, TARGETS), jnp.int32),
            jax.ShapeDtypeStruct((LINES * (FAN + 1), 128), jnp.int32),
            jax.ShapeDtypeStruct((LINES, 128), jnp.int32),
        ),
        in_specs=[SMEM] + [HBM] * 6,
        out_specs=(HBM, VMEM, VMEM, VMEM),
        scratch_shapes=[
            *[pltpu.VMEM(shape, array.dtype) for shape, array in zip(shapes, arrays)],
            pltpu.VMEM((FEAT, 144, 128), BF16),
            pltpu.VMEM((32, LINES, 128), F32),
            pltpu.SemaphoreType.DMA((FEAT // 8,)),
            pltpu.SemaphoreType.DMA((6,)),
        ],
        compiler_params=pltpu.CompilerParams(vmem_limit_bytes=MOST),
        cost_estimate=pl.CostEstimate(flops=10**8, bytes_accessed=10**7, transcendentals=0),
    )(core, *arrays)


def call_gather(slots, ranks, table):
    return pl.pallas_call(
        gather_kernel,
        out_shape=jax.ShapeDtypeStruct((FEAT, 64, 128), BF16),
        in_specs=[pl.BlockSpec(memory_space=pl.ANY), VMEM, VMEM],
        out_specs=VMEM,
        scratch_shapes=[
            pltpu.VMEM((INPUTS + 8, 128), F32),
            pltpu.VMEM((ROWS, 128), F32),
            pltpu.SMEM(((FAN + 1) * ROWS,), jnp.int32),
            pltpu.SemaphoreType.DMA((ROWS // CHUNK,)),
        ],
        compiler_params=pltpu.CompilerParams(vmem_limit_bytes=24 * 2**20),
        cost_estimate=pl.CostEstimate(flops=0, bytes_accessed=0, transcendentals=0),
    )(slots, ranks, table)


def call_pick(place, mask, labels, block):
    return pl.pallas_call(
        pick_kernel,
        out_shape=(
            jax.ShapeDtypeStruct((2, NAMED + 16, TARGETS), BF16),
            jax.ShapeDtypeStruct(block.shape, BF16),
        ),
        in_specs=[VMEM] * 3 + [HBM],
        out_specs=(VMEM, VMEM),
        scratch_shapes=[pltpu.SemaphoreType.DMA],
        compiler_params=pltpu.CompilerParams(vmem_limit_bytes=16 * 2**20),
        cost_estimate=pl.CostEstimate(flops=10**7, bytes_accessed=6 * 10**6, transcendentals=0),
    )(place, mask, labels, block)


def call_loss(spot, rows, picks, rows_there, picks_there, blocks):
    sources = [rows, picks, rows_there, picks_there, *blocks]
    return pl.pallas_call(
        loss_kernel,
        out_shape=[jax.ShapeDtypeStruct((8, TARGETS), F32)] * 2,
        in_specs=[SMEM] + [VMEM] * len(sources),
        out_specs=[VMEM, VMEM],
        scratch_shapes=[
            pltpu.VMEM((2 * TARGETS, 2 * HIDDEN), BF16),
            pltpu.VMEM((2, TARGETS, blocks[0].shape[1]), F32),
        ],
        compiler_params=pltpu.CompilerParams(vmem_limit_bytes=16 * 2**20),
    )(spot, *sources)


def join_kernel(here, there, loss):
    most = jnp.maximum(here[0:1], there[0:1])
    total = here[1:2] * jnp.exp(here[0:1] - most) + there[1:2] * jnp.exp(there[0:1] - most)
    loss[...] = most + jnp.log(total) - (here[2:3] + there[2:3])


def call_join(here, there):
    return pl.pallas_call(
        join_kernel,
        out_shape=jax.ShapeDtypeStruct((1, TARGETS), F32),
        in_specs=[VMEM, VMEM],
        out_specs=VMEM,
        compiler_params=pltpu.CompilerParams(vmem_limit_bytes=2**20),
    )(here, there)


def body(
    features,
    first_neighbours,
    first_mask,
    second_neighbours,
    second_mask,
    target_index,
    labels,
    first_weight,
    first_bias,
    class_weight,
):
    spot = lax.axis_index("node").astype(jnp.int32)
    core = spot & 1
    table = features[:, 0, :]
    swap = [(device, device ^ 1) for device in range(NODE)]
    blocks = [class_weight]
    for hops in HOPS[1:]:
        around = [(device, (device - hops) % NODE) for device in range(NODE)]
        blocks.append(lax.ppermute(class_weight, "node", around))
    own, place, slots, ranks = call_prepare(
        core[None],
        [
            second_neighbours,
            target_index,
            first_weight,
            table,
            first_neighbours.reshape(FAN, LINES, 128),
            first_mask.reshape(FAN, LINES, 128),
        ],
    )
    own = lax.all_to_all(own, "feat", 0, 0)
    send = call_gather(slots.reshape(-1), ranks, table)
    send, own = lax.optimization_barrier((send, own))
    mine = own[:, : 2 * WIDTH].reshape(FEAT * 2 * WIDTH, 128)
    theirs = lax.ppermute(mine, "node", swap)
    means = lax.all_to_all(send, "feat", 0, 0)
    means, *blocks[2:] = lax.optimization_barrier((means, *blocks[2:]))
    side = jnp.stack([core, lax.axis_index("feat").astype(jnp.int32) & 1])
    chosen = pl.pallas_call(
        choose_kernel,
        out_shape=jax.ShapeDtypeStruct((NAMED, SLAB), BF16),
        in_specs=[VMEM],
        out_specs=VMEM,
        scratch_shapes=[pltpu.VMEM((FEAT, SLAB), F32)],
        compiler_params=pltpu.CompilerParams(vmem_limit_bytes=16 * 2**20),
        cost_estimate=pl.CostEstimate(flops=10**7, bytes_accessed=2 * 10**6, transcendentals=0),
    )(own)
    hidden, rows = pl.pallas_call(
        hidden_kernel,
        out_shape=(
            jax.ShapeDtypeStruct((OWN, HIDDEN), BF16),
            jax.ShapeDtypeStruct((NAMED, HIDDEN), BF16),
        ),
        in_specs=[SMEM] + [VMEM] * 6,
        out_specs=(VMEM, VMEM),
        scratch_shapes=[pltpu.VMEM((FEAT * 80, 256), BF16)],
        compiler_params=pltpu.CompilerParams(vmem_limit_bytes=24 * 2**20),
    )(side, own, means, mine, theirs, first_bias[None, :], chosen)
    picks, blocks[0] = call_pick(place, second_mask, labels, class_weight)
    picks_there = lax.ppermute(picks, "node", swap)
    rows = lax.all_to_all(rows.reshape(FEAT, UNION, HIDDEN), "feat", 0, 0)
    rows = rows.reshape(FEAT * UNION, HIDDEN)
    rows_there = lax.ppermute(rows, "node", swap)
    here, there = call_loss(spot[None], rows, picks, rows_there, picks_there, blocks)
    there = lax.ppermute(there, "node", swap)
    loss = call_join(here, there)
    return (hidden[None], loss)


def solution(mesh):
    placed = (
        P("feat", "node", None),
        P(None, "node", None),
        P(None, "node", None),
        P(None, "node", "feat"),
        P(None, "node", "feat"),
        P("node", "feat"),
        P("node", "feat"),
        P(None, "feat", None),
        P(),
        P(None, "node"),
    )
    return jax.shard_map(
        body,
        mesh=mesh,
        in_specs=placed,
        out_specs=(P("node", "feat", None), P("node", "feat")),
        check_vma=False,
    )
```

```python
import functools

import jax
import jax.numpy as jnp
from jax import lax
from jax.experimental import pallas as pl
from jax.experimental.pallas import tpu as pltpu
from jax.sharding import PartitionSpec as P

FEAT = 32
NODE = 8
WIDTH = 40
INPUTS = 24576
ROWS = 6144
OWN = 192
FAN = 10
TARGETS = 128
HIDDEN = 256
UNION = 24
NAMED = FEAT * UNION
SLAB = 256
HOPS = (0, 4, 6, 2)
UNROLL = 64
LEAST = 3
LINES = ROWS // 128
CHUNK = 1024
PAIRS = 4
TABLE_STEP = 16
MOST = 60 * 2**20
F32 = jnp.float32
BF16 = jnp.bfloat16


def iota(shape, dim):
    return lax.broadcasted_iota(jnp.int32, shape, dim)


def contract(a, b, dim_a, dim_b):
    return lax.dot_general(a, b, (((dim_a,), (dim_b,)), ((), ())), preferred_element_type=F32)


def earlier(size):
    return jnp.where(iota((size, size), 0) < iota((size, size), 1), 1.0, 0.0).astype(BF16)


def add_all(terms):
    while len(terms) > 1:
        paired = [terms[k] + terms[k + 1] for k in range(0, len(terms) - 1, 2)]
        terms = paired + terms[len(terms) - len(terms) % 2 :]
    return terms[0]


def prepare_kernel(core, *refs):
    sources, (send, place, lists, ranks), held, (built, columns, sent, arrived) = (
        refs[:6],
        refs[6:10],
        refs[10:16],
        refs[16:],
    )
    fetches = []
    for source, ref in zip(sources, held):
        part = source if source.shape == ref.shape else source.at[:, pl.ds(0, ROWS)]
        fetches.append(pltpu.make_async_copy(part, ref, arrived.at[len(fetches)]))
        fetches[-1].start()
    neighbours, targets, weights, features, given, filled = held
    fetches[0].wait()
    fetches[1].wait()
    owners, lanes = [], []
    named = jnp.zeros((FEAT, SLAB), F32)
    for slot in range(FAN + 1):
        index = neighbours[slot] if slot < FAN else targets[...]
        owner = ((index.astype(F32) + 0.5) * (1.0 / OWN)).astype(jnp.int32)
        row = index - owner * OWN
        owner_hot = jnp.where(iota((FEAT, TARGETS), 0) == owner, 1.0, 0.0).astype(BF16)
        row_hot = jnp.where(iota((SLAB, TARGETS), 0) == row, 1.0, 0.0)
        named = named + contract(owner_hot, row_hot.astype(BF16), 1, 1)
        owners.append((owner, owner_hot))
        lanes.append(row_hot)
    marked = jnp.where(named > 0.0, 1.0, 0.0)
    rank = contract(marked.astype(BF16), earlier(SLAB), 1, 0).astype(BF16)
    places = []
    for slot in range(FAN + 1):
        owner, owner_hot = owners[slot]
        mine = jnp.sum(contract(rank, owner_hot, 0, 0) * lanes[slot], axis=0, keepdims=True)
        places.append(owner * UNION + mine.astype(jnp.int32))
    place[...] = jnp.concatenate(places + [jnp.zeros((5, TARGETS), jnp.int32)], axis=0)

    fetches[2].wait()
    fetches[3].wait()
    shared = weights[...].astype(F32)
    shared = jnp.where(core[0] == 0, shared[:, :, :128], shared[:, :, 128:])
    shared = shared.reshape(2 * WIDTH, 128)
    for pair in range(FEAT // 2):
        block = features[:, pl.ds(pair * 2 * OWN, 2 * OWN)].astype(F32)
        for half in range(2):
            owner = 2 * pair + half
            marks = [marked[owner : owner + 1, k * 64 : (k + 1) * 64] for k in range(3)]
            last = jnp.concatenate(marks + [jnp.zeros((5, 64), F32)], axis=0)
            built[owner] = jnp.concatenate([shared, folded(block, half, last)], axis=0).astype(BF16)
        if pair % 4 == 3:
            copies_out(built, send, sent, pair // 4).start()
    fetches[4].wait()
    fetches[5].wait()
    order_rows(given, filled, lists, ranks, columns)
    for step in range(FEAT // 8):
        copies_out(built, send, sent, step).wait()


def order_rows(neighbours, mask, lists, ranks, columns):
    used = [jnp.where(mask[slot] > 0, 1, 0) for slot in range(FAN)]
    before = [jnp.zeros((LINES, 128), jnp.int32)]
    for slot in range(FAN):
        before.append(before[slot] + used[slot])
    count = before[FAN]
    for place in range(FAN):
        node = jnp.where(count > place, 0, INPUTS)
        for slot in range(place, FAN):
            here = (used[slot] > 0) & (before[slot] == place)
            node = node + jnp.where(here, neighbours[slot], 0)
        high = node >> 8
        columns[place] = high.astype(F32)
        columns[16 + place] = (node - high * 256).astype(F32)
    columns[FAN] = jnp.zeros((LINES, 128), F32)
    columns[16 + FAN] = count.astype(F32)
    hot = [jnp.where(count == amount, 1.0, 0.0) for amount in range(FAN + 1)]
    stacked = jnp.concatenate(hot, axis=0).astype(BF16)
    second = iota(((FAN + 1) * LINES, 128), 0) % 2 == 1
    earlier_same = contract(stacked, earlier(128), 1, 0)
    all_same = contract(stacked, jnp.ones((128, 128), BF16), 1, 0)
    above = pltpu.roll(all_same, 1, 0)
    below = pltpu.roll(all_same, (FAN + 1) * LINES - 1, 0)
    earlier_same = earlier_same + jnp.where(second, above, 0.0)
    all_same = all_same + jnp.where(second, above, below)
    rank = jnp.zeros((LINES, 128), F32)
    higher = jnp.zeros((LINES, 128), F32)
    for amount in reversed(range(FAN + 1)):
        span = slice(amount * LINES, (amount + 1) * LINES)
        rank = rank + hot[amount] * (earlier_same[span] + higher)
        higher = higher + all_same[span]
    ranks[...] = rank.astype(jnp.int32)
    for line in range(0, LINES, 2):
        part = contract(columns[:, line, :].astype(BF16), moved(ranks, line), 1, 1)
        part += contract(columns[:, line + 1, :].astype(BF16), moved(ranks, line + 1), 1, 1)
        part = (part[:16] * 256.0 + part[16:]).astype(jnp.int32)
        first = line // 8 * 8 * (FAN + 1) + line % 8
        for half in range(2):
            here = part[: FAN + 1, half * 128 : (half + 1) * 128]
            lists[pl.ds(first + half, FAN + 1, stride=8), :] = here


def copies_out(built, send, sent, step):
    span = pl.ds(step * 8, 8)
    return pltpu.make_async_copy(built.at[span], send.at[span], sent.at[step])


def folded(block, half, last):
    rest = block[:, 128 + half * 64 : 192 + half * 64]
    rest = jnp.concatenate([rest[:24], jnp.concatenate([rest[24:], last], axis=0)], axis=1)
    return jnp.concatenate([block[:, half * 256 : half * 256 + 128], rest], axis=0)


def moved(ranks, line):
    return jnp.where(iota((256, 128), 0) == ranks[pl.ds(line, 1), :], 1.0, 0.0).astype(BF16)


def mean_of(flipped):
    thirds = [flipped[t * WIDTH : (t + 1) * WIDTH] for t in range(3)]
    return (thirds[0] + thirds[1] + thirds[2]) / jnp.maximum(flipped[3 * WIDTH : 3 * WIDTH + 1], 1.0)


def gather_kernel(
    slots, ranks, features, send, table, sums, lists, arrived
):
    size = (FAN + 1) * CHUNK

    def fetch(chunk):
        span = pl.ds(pl.multiple_of(chunk * size, size), size)
        return pltpu.make_async_copy(slots.at[span], lists.at[span], arrived.at[chunk])

    third = INPUTS // 3
    fetch(0).start()
    for chunk in range(1, ROWS // CHUNK):
        fetch(chunk).start()

    lane = iota((128, 128), 1)

    def fill(step, carry):
        for part in range(TABLE_STEP):
            at = pl.multiple_of((step * TABLE_STEP + part) * 128, 128)
            blocks = [features[:, pl.ds(t * third + at, 128)].astype(F32) for t in range(3)]
            flipped = jnp.concatenate(blocks + [jnp.ones((8, 128), F32)], axis=0).T
            for t in range(3):
                kept = ((lane >= t * WIDTH) & (lane < (t + 1) * WIDTH)) | (lane >= 3 * WIDTH)
                table[pl.ds(t * third + at, 128), :] = jnp.where(kept, flipped, 0.0)
        return carry

    lax.fori_loop(0, third // 128 // TABLE_STEP, fill, 0)
    table[pl.ds(INPUTS, 8), :] = jnp.zeros((8, 128), F32)

    def chunk_step(chunk, carry):
        fetch(chunk).wait()

        def block(step, inner):
            first = chunk * size + step * UNROLL
            at = pl.multiple_of(chunk * CHUNK + step * UNROLL, UNROLL)
            result = sums.at[pl.ds(at, UNROLL), :]

            def add(depth):
                named = [lists.at[pl.ds(first + slot * CHUNK, UNROLL)] for slot in range(depth)]
                for row in range(UNROLL):
                    result[pl.ds(row, 1), :] = add_all(
                        [table[pl.ds(named[slot][row], 1), :] for slot in range(depth)]
                    )

            def choose(low, high):
                if low == high:
                    add(low)
                    return
                middle = (low + high) // 2
                lax.cond(
                    deepest <= middle,
                    lambda: choose(low, middle),
                    lambda: choose(middle + 1, high),
                )

            deepest = lists[first + FAN * CHUNK]
            choose(LEAST, FAN)
            return inner

        return lax.fori_loop(0, CHUNK // UNROLL, block, carry)

    lax.fori_loop(0, ROWS // CHUNK, chunk_step, 0)

    def pair_step(step, carry):
        for part in range(0, PAIRS, 2):
            line = (step * PAIRS + part) * 3
            blocks = []
            for k in range(0, 6, 2):
                at = pl.multiple_of((line + k) * 128, 128)
                means = [mean_of(sums[pl.ds(at + half * 128, 128), :].T) for half in range(2)]
                means = jnp.concatenate(means, axis=1).astype(BF16)
                for half in range(2):
                    blocks.append(contract(means, moved(ranks, line + k + half), 1, 0))
            for pair in range(2):
                block = jnp.concatenate(blocks[pair * 3 : pair * 3 + 3], axis=1)
                owner = 2 * (step * PAIRS + part + pair)
                for half in range(2):
                    tile = folded(block, half, jnp.zeros((8, 64), F32))
                    send[owner + half] = tile.astype(BF16)
        return carry

    lax.fori_loop(0, FEAT // 2 // PAIRS, pair_step, 0)


def unfolded(tile):
    rest = jnp.concatenate([tile[40:64, :64], tile[40:56, 64:]], axis=0)
    return jnp.concatenate([tile[:40], rest, jnp.zeros((40, 64), F32)], axis=1)


def choose_kernel(own, chosen, marks):
    for source in range(FEAT):
        last = own[source, pl.ds(128, 16), :].astype(F32)
        marks[pl.ds(source, 1), :] = jnp.concatenate(
            [last[8 + k : 9 + k, 64:] for k in range(3)] + [jnp.zeros((1, 64), F32)], axis=1
        )
    rank = contract(marks[...].astype(BF16), earlier(SLAB), 1, 0)
    for pair in range(FEAT // 2):
        hits = []
        for source in (2 * pair, 2 * pair + 1):
            hit = (iota((UNION, SLAB), 0).astype(F32) == rank[source : source + 1]) & (
                marks[pl.ds(source, 1), :] > 0.0
            )
            hits.append(jnp.where(hit, 1.0, 0.0))
        chosen[pl.ds(pair * 2 * UNION, 2 * UNION), :] = jnp.concatenate(hits, axis=0).astype(BF16)


def hidden_kernel(spot, own, means, mine, theirs, bias, chosen, hidden, rows, stacked):
    for source in range(FEAT):
        tiles = [unfolded(own[source].astype(F32)[80:]), unfolded(means[source].astype(F32))]
        stacked[pl.ds(source * 80, 80), :] = jnp.concatenate(tiles, axis=0).astype(BF16)
    first = contract(stacked[...], mine[...], 0, 0)[:OWN]
    second = contract(stacked[...], theirs[...], 0, 0)[:OWN]
    even = spot[0] == 0
    pre = jnp.concatenate(
        [jnp.where(even, first, second), jnp.where(even, second, first)], axis=1
    )
    pre = jnp.where(spot[1] == 0, pre, jnp.concatenate([pre[128:], pre[:128]], axis=0))
    result = jnp.maximum(pre + bias[...], 0.0).astype(BF16)
    hidden[...] = result
    padded = jnp.concatenate([result, jnp.zeros((SLAB - OWN, HIDDEN), BF16)], axis=0)
    rows[...] = contract(chosen[...], padded, 1, 0).astype(BF16)


def pick_kernel(place, mask, labels, near, far, picks, held, held_far, arrived):
    copies = [
        pltpu.make_async_copy(near, held, arrived.at[0]),
        pltpu.make_async_copy(far, held_far, arrived.at[1]),
    ]
    for copy in copies:
        copy.start()
    spots = iota((NAMED, TARGETS), 0)
    total = jnp.zeros((NAMED, TARGETS), F32)
    for slot in range(FAN):
        used = mask[slot].astype(F32)
        total = total + jnp.where(spots == place[pl.ds(slot, 1), :], used, 0.0)
    own = jnp.where(spots == place[pl.ds(FAN, 1), :], 1.0, 0.0)
    line = iota((16, TARGETS), 0)
    label = jnp.broadcast_to(labels[...], (16, TARGETS))
    high = label >> 7
    parts = jnp.where(line == 0, high, jnp.where(line == 1, label - high * 128, 0))
    blank = jnp.zeros((16, TARGETS), F32)
    picks[0] = jnp.concatenate([total, parts.astype(F32)], axis=0).astype(BF16)
    picks[1] = jnp.concatenate([own, blank], axis=0).astype(BF16)
    for copy in copies:
        copy.wait()


def loss_kernel(spot, *refs):
    held, blocks = refs[:4], refs[4 : 4 + NODE // 2]
    stats, other, inputs, logits = refs[4 + NODE // 2 :]
    offsets = []
    for side in range(2):
        rows, picks = held[2 * side], held[2 * side + 1]
        total, own = picks[0][:NAMED], picks[1][:NAMED]
        count = contract(total, jnp.ones((NAMED, 128), BF16), 0, 0)[:, :1]
        agg = contract(total, rows[...], 0, 0) / jnp.maximum(count, 1.0)
        span = pl.ds(side * TARGETS, TARGETS)
        inputs[span, pl.ds(0, HIDDEN)] = contract(own, rows[...], 0, 0).astype(BF16)
        inputs[span, pl.ds(HIDDEN, HIDDEN)] = agg.astype(BF16)
        parts = picks[0][NAMED:].astype(F32)
        label = jnp.broadcast_to(parts[:1] * 128.0 + parts[1:2], (TARGETS, TARGETS)).T
        offsets.append(label.astype(jnp.int32) - iota((TARGETS, TARGETS), 1))
    width = blocks[0].shape[1]
    start = (
        jnp.full((TARGETS, TARGETS), -jnp.inf, F32),
        jnp.zeros((TARGETS, TARGETS), F32),
        jnp.zeros((TARGETS, TARGETS), F32),
    )
    running = [start, start]
    for step in range(2 * len(blocks) + 1):
        block, side = step // 2, step % 2
        if block < len(blocks):
            mine = inputs[pl.ds(side * TARGETS, TARGETS), :]
            logits[step % 2] = contract(mine, blocks[block][...], 1, 0)
        if step > 0:
            block, side = (step - 1) // 2, (step - 1) % 2
            last = logits.at[(step - 1) % 2]
            largest, summed, picked = running[side]
            spans = [pl.ds(k * 128, 128) for k in range(width // 128)]
            here = offsets[side] - ((spot[0] + HOPS[block]) & 7) * width
            now = largest
            for span in spans:
                now = jnp.maximum(now, last[:, span])
            summed = summed * jnp.exp(largest - now)
            for k, span in enumerate(spans):
                part = last[:, span]
                summed = summed + jnp.exp(part - now)
                picked = picked + jnp.where(here == k * 128, part, 0.0)
            running[side] = (now, summed, picked)
    for side, ref in ((0, stats), (1, other)):
        largest, summed, picked = running[side]
        most = jnp.max(largest, axis=1, keepdims=True)
        total = jnp.sum(summed * jnp.exp(largest - most), axis=1, keepdims=True)
        found = jnp.sum(picked, axis=1, keepdims=True)
        lane = iota((TARGETS, TARGETS), 1)
        table = jnp.where(lane == 0, most, jnp.where(lane == 1, total, found))
        ref[...] = table.T[:8]


VMEM = pl.BlockSpec(memory_space=pltpu.VMEM)
HBM = pl.BlockSpec(memory_space=pltpu.HBM)
SMEM = pl.BlockSpec(memory_space=pltpu.SMEM)


def call_prepare(core, arrays):
    shapes = [array.shape for array in arrays]
    shapes[3] = (WIDTH, ROWS)
    return pl.pallas_call(
        prepare_kernel,
        out_shape=(
            jax.ShapeDtypeStruct((FEAT, 144, 128), BF16),
            jax.ShapeDtypeStruct((16, TARGETS), jnp.int32),
            jax.ShapeDtypeStruct((LINES * (FAN + 1), 128), jnp.int32),
            jax.ShapeDtypeStruct((LINES, 128), jnp.int32),
        ),
        in_specs=[SMEM] + [HBM] * 6,
        out_specs=(HBM, VMEM, VMEM, VMEM),
        scratch_shapes=[
            *[pltpu.VMEM(shape, array.dtype) for shape, array in zip(shapes, arrays)],
            pltpu.VMEM((FEAT, 144, 128), BF16),
            pltpu.VMEM((32, LINES, 128), F32),
            pltpu.SemaphoreType.DMA((FEAT // 8,)),
            pltpu.SemaphoreType.DMA((6,)),
        ],
        compiler_params=pltpu.CompilerParams(vmem_limit_bytes=MOST),
        cost_estimate=pl.CostEstimate(flops=10**8, bytes_accessed=10**7, transcendentals=0),
    )(core, *arrays)


def call_gather(slots, ranks, table):
    return pl.pallas_call(
        gather_kernel,
        out_shape=jax.ShapeDtypeStruct((FEAT, 64, 128), BF16),
        in_specs=[pl.BlockSpec(memory_space=pl.ANY), VMEM, VMEM],
        out_specs=VMEM,
        scratch_shapes=[
            pltpu.VMEM((INPUTS + 8, 128), F32),
            pltpu.VMEM((ROWS, 128), F32),
            pltpu.SMEM(((FAN + 1) * ROWS,), jnp.int32),
            pltpu.SemaphoreType.DMA((ROWS // CHUNK,)),
        ],
        compiler_params=pltpu.CompilerParams(vmem_limit_bytes=24 * 2**20),
        cost_estimate=pl.CostEstimate(flops=0, bytes_accessed=0, transcendentals=0),
    )(slots, ranks, table)


def call_pick(place, mask, labels, near, far):
    return pl.pallas_call(
        pick_kernel,
        out_shape=(
            jax.ShapeDtypeStruct((2, NAMED + 16, TARGETS), BF16),
            jax.ShapeDtypeStruct(near.shape, BF16),
            jax.ShapeDtypeStruct(far.shape, BF16),
        ),
        in_specs=[VMEM] * 3 + [HBM] * 2,
        out_specs=(VMEM,) * 3,
        scratch_shapes=[pltpu.SemaphoreType.DMA((2,))],
        compiler_params=pltpu.CompilerParams(vmem_limit_bytes=16 * 2**20),
        cost_estimate=pl.CostEstimate(flops=10**7, bytes_accessed=6 * 10**6, transcendentals=0),
    )(place, mask, labels, near, far)


def call_loss(spot, rows, picks, rows_there, picks_there, blocks):
    sources = [rows, picks, rows_there, picks_there, *blocks]
    return pl.pallas_call(
        loss_kernel,
        out_shape=[jax.ShapeDtypeStruct((8, TARGETS), F32)] * 2,
        in_specs=[SMEM] + [VMEM] * len(sources),
        out_specs=[VMEM, VMEM],
        scratch_shapes=[
            pltpu.VMEM((2 * TARGETS, 2 * HIDDEN), BF16),
            pltpu.VMEM((2, TARGETS, blocks[0].shape[1]), F32),
        ],
        compiler_params=pltpu.CompilerParams(vmem_limit_bytes=16 * 2**20),
    )(spot, *sources)


def join_kernel(here, there, loss):
    most = jnp.maximum(here[0:1], there[0:1])
    total = here[1:2] * jnp.exp(here[0:1] - most) + there[1:2] * jnp.exp(there[0:1] - most)
    loss[...] = most + jnp.log(total) - (here[2:3] + there[2:3])


def call_join(here, there):
    return pl.pallas_call(
        join_kernel,
        out_shape=jax.ShapeDtypeStruct((1, TARGETS), F32),
        in_specs=[VMEM, VMEM],
        out_specs=VMEM,
        compiler_params=pltpu.CompilerParams(vmem_limit_bytes=2**20),
    )(here, there)


def body(
    features,
    first_neighbours,
    first_mask,
    second_neighbours,
    second_mask,
    target_index,
    labels,
    first_weight,
    first_bias,
    class_weight,
):
    spot = lax.axis_index("node").astype(jnp.int32)
    core = spot & 1
    table = features[:, 0, :]
    swap = [(device, device ^ 1) for device in range(NODE)]
    blocks = [class_weight]
    for hops in HOPS[1:]:
        around = [(device, (device - hops) % NODE) for device in range(NODE)]
        blocks.append(lax.ppermute(class_weight, "node", around))
    own, place, slots, ranks = call_prepare(
        core[None],
        [
            second_neighbours,
            target_index,
            first_weight,
            table,
            first_neighbours.reshape(FAN, LINES, 128),
            first_mask.reshape(FAN, LINES, 128),
        ],
    )
    own = lax.all_to_all(own, "feat", 0, 0)
    send = call_gather(slots.reshape(-1), ranks, table)
    send, own = lax.optimization_barrier((send, own))
    mine = own[:, : 2 * WIDTH].reshape(FEAT * 2 * WIDTH, 128)
    theirs = lax.ppermute(mine, "node", swap)
    means = lax.all_to_all(send, "feat", 0, 0)
    means, blocks[1] = lax.optimization_barrier((means, blocks[1]))
    side = jnp.stack([core, lax.axis_index("feat").astype(jnp.int32) & 1])
    chosen = pl.pallas_call(
        choose_kernel,
        out_shape=jax.ShapeDtypeStruct((NAMED, SLAB), BF16),
        in_specs=[VMEM],
        out_specs=VMEM,
        scratch_shapes=[pltpu.VMEM((FEAT, SLAB), F32)],
        compiler_params=pltpu.CompilerParams(vmem_limit_bytes=16 * 2**20),
        cost_estimate=pl.CostEstimate(flops=10**7, bytes_accessed=2 * 10**6, transcendentals=0),
    )(own)
    hidden, rows = pl.pallas_call(
        hidden_kernel,
        out_shape=(
            jax.ShapeDtypeStruct((OWN, HIDDEN), BF16),
            jax.ShapeDtypeStruct((NAMED, HIDDEN), BF16),
        ),
        in_specs=[SMEM] + [VMEM] * 6,
        out_specs=(VMEM, VMEM),
        scratch_shapes=[pltpu.VMEM((FEAT * 80, 256), BF16)],
        compiler_params=pltpu.CompilerParams(vmem_limit_bytes=24 * 2**20),
    )(side, own, means, mine, theirs, first_bias[None, :], chosen)
    picks, *blocks[:2] = call_pick(place, second_mask, labels, *blocks[:2])
    picks_there = lax.ppermute(picks, "node", swap)
    rows = lax.all_to_all(rows.reshape(FEAT, UNION, HIDDEN), "feat", 0, 0)
    rows = rows.reshape(FEAT * UNION, HIDDEN)
    rows_there = lax.ppermute(rows, "node", swap)
    here, there = call_loss(spot[None], rows, picks, rows_there, picks_there, blocks)
    there = lax.ppermute(there, "node", swap)
    loss = call_join(here, there)
    return (hidden[None], loss)


def solution(mesh):
    placed = (
        P("feat", "node", None),
        P(None, "node", None),
        P(None, "node", None),
        P(None, "node", "feat"),
        P(None, "node", "feat"),
        P("node", "feat"),
        P("node", "feat"),
        P(None, "feat", None),
        P(),
        P(None, "node"),
    )
    return jax.shard_map(
        body,
        mesh=mesh,
        in_specs=placed,
        out_specs=(P("node", "feat", None), P("node", "feat")),
        check_vma=False,
    )
```

```python
import functools

import jax
import jax.numpy as jnp
from jax import lax
from jax.experimental import pallas as pl
from jax.experimental.pallas import tpu as pltpu
from jax.sharding import PartitionSpec as P

FEAT = 32
NODE = 8
WIDTH = 40
INPUTS = 24576
ROWS = 6144
OWN = 192
FAN = 10
TARGETS = 128
HIDDEN = 256
UNION = 24
NAMED = FEAT * UNION
SLAB = 256
HOPS = (0, 4, 6, 2)
UNROLL = 64
LEAST = 3
LINES = ROWS // 128
CHUNK = 1024
PAIRS = 4
TABLE_STEP = 16
MOST = 60 * 2**20
F32 = jnp.float32
BF16 = jnp.bfloat16


def iota(shape, dim):
    return lax.broadcasted_iota(jnp.int32, shape, dim)


def contract(a, b, dim_a, dim_b):
    return lax.dot_general(a, b, (((dim_a,), (dim_b,)), ((), ())), preferred_element_type=F32)


def earlier(size):
    return jnp.where(iota((size, size), 0) < iota((size, size), 1), 1.0, 0.0).astype(BF16)


def add_all(terms):
    while len(terms) > 1:
        paired = [terms[k] + terms[k + 1] for k in range(0, len(terms) - 1, 2)]
        terms = paired + terms[len(terms) - len(terms) % 2 :]
    return terms[0]


def prepare_kernel(core, *refs):
    sources, (send, place, lists, ranks), held, (built, columns, sent, arrived) = (
        refs[:6],
        refs[6:10],
        refs[10:16],
        refs[16:],
    )
    fetches = []
    for source, ref in zip(sources, held):
        part = source if source.shape == ref.shape else source.at[:, pl.ds(0, ROWS)]
        fetches.append(pltpu.make_async_copy(part, ref, arrived.at[len(fetches)]))
        fetches[-1].start()
    neighbours, targets, weights, features, given, filled = held
    fetches[0].wait()
    fetches[1].wait()
    owners, lanes = [], []
    named = jnp.zeros((FEAT, SLAB), F32)
    for slot in range(FAN + 1):
        index = neighbours[slot] if slot < FAN else targets[...]
        owner = ((index.astype(F32) + 0.5) * (1.0 / OWN)).astype(jnp.int32)
        row = index - owner * OWN
        owner_hot = jnp.where(iota((FEAT, TARGETS), 0) == owner, 1.0, 0.0).astype(BF16)
        row_hot = jnp.where(iota((SLAB, TARGETS), 0) == row, 1.0, 0.0)
        named = named + contract(owner_hot, row_hot.astype(BF16), 1, 1)
        owners.append((owner, owner_hot))
        lanes.append(row_hot)
    marked = jnp.where(named > 0.0, 1.0, 0.0)
    rank = contract(marked.astype(BF16), earlier(SLAB), 1, 0).astype(BF16)
    places = []
    for slot in range(FAN + 1):
        owner, owner_hot = owners[slot]
        mine = jnp.sum(contract(rank, owner_hot, 0, 0) * lanes[slot], axis=0, keepdims=True)
        places.append(owner * UNION + mine.astype(jnp.int32))
    place[...] = jnp.concatenate(places + [jnp.zeros((5, TARGETS), jnp.int32)], axis=0)

    fetches[2].wait()
    fetches[3].wait()
    shared = weights[...].astype(F32)
    shared = jnp.where(core[0] == 0, shared[:, :, :128], shared[:, :, 128:])
    shared = shared.reshape(2 * WIDTH, 128)
    for pair in range(FEAT // 2):
        block = features[:, pl.ds(pair * 2 * OWN, 2 * OWN)].astype(F32)
        for half in range(2):
            owner = 2 * pair + half
            marks = [marked[owner : owner + 1, k * 64 : (k + 1) * 64] for k in range(3)]
            last = jnp.concatenate(marks + [jnp.zeros((5, 64), F32)], axis=0)
            built[owner] = jnp.concatenate([shared, folded(block, half, last)], axis=0).astype(BF16)
        if pair % 4 == 3:
            copies_out(built, send, sent, pair // 4).start()
    fetches[4].wait()
    fetches[5].wait()
    order_rows(given, filled, lists, ranks, columns)
    for step in range(FEAT // 8):
        copies_out(built, send, sent, step).wait()


def order_rows(neighbours, mask, lists, ranks, columns):
    used = [jnp.where(mask[slot] > 0, 1, 0) for slot in range(FAN)]
    before = [jnp.zeros((LINES, 128), jnp.int32)]
    for slot in range(FAN):
        before.append(before[slot] + used[slot])
    count = before[FAN]
    for place in range(FAN):
        node = jnp.where(count > place, 0, INPUTS)
        for slot in range(place, FAN):
            here = (used[slot] > 0) & (before[slot] == place)
            node = node + jnp.where(here, neighbours[slot], 0)
        high = node >> 8
        columns[place] = high.astype(F32)
        columns[16 + place] = (node - high * 256).astype(F32)
    columns[FAN] = jnp.zeros((LINES, 128), F32)
    columns[16 + FAN] = count.astype(F32)
    hot = [jnp.where(count == amount, 1.0, 0.0) for amount in range(FAN + 1)]
    stacked = jnp.concatenate(hot, axis=0).astype(BF16)
    second = iota(((FAN + 1) * LINES, 128), 0) % 2 == 1
    earlier_same = contract(stacked, earlier(128), 1, 0)
    all_same = contract(stacked, jnp.ones((128, 128), BF16), 1, 0)
    above = pltpu.roll(all_same, 1, 0)
    below = pltpu.roll(all_same, (FAN + 1) * LINES - 1, 0)
    earlier_same = earlier_same + jnp.where(second, above, 0.0)
    all_same = all_same + jnp.where(second, above, below)
    rank = jnp.zeros((LINES, 128), F32)
    higher = jnp.zeros((LINES, 128), F32)
    for amount in reversed(range(FAN + 1)):
        span = slice(amount * LINES, (amount + 1) * LINES)
        rank = rank + hot[amount] * (earlier_same[span] + higher)
        higher = higher + all_same[span]
    ranks[...] = rank.astype(jnp.int32)
    for line in range(0, LINES, 2):
        part = contract(columns[:, line, :].astype(BF16), moved(ranks, line), 1, 1)
        part += contract(columns[:, line + 1, :].astype(BF16), moved(ranks, line + 1), 1, 1)
        part = (part[:16] * 256.0 + part[16:]).astype(jnp.int32)
        first = line // 8 * 8 * (FAN + 1) + line % 8
        for half in range(2):
            here = part[: FAN + 1, half * 128 : (half + 1) * 128]
            lists[pl.ds(first + half, FAN + 1, stride=8), :] = here


def copies_out(built, send, sent, step):
    span = pl.ds(step * 8, 8)
    return pltpu.make_async_copy(built.at[span], send.at[span], sent.at[step])


def folded(block, half, last):
    rest = block[:, 128 + half * 64 : 192 + half * 64]
    rest = jnp.concatenate([rest[:24], jnp.concatenate([rest[24:], last], axis=0)], axis=1)
    return jnp.concatenate([block[:, half * 256 : half * 256 + 128], rest], axis=0)


def moved(ranks, line):
    return jnp.where(iota((256, 128), 0) == ranks[pl.ds(line, 1), :], 1.0, 0.0).astype(BF16)


def mean_of(flipped):
    thirds = [flipped[t * WIDTH : (t + 1) * WIDTH] for t in range(3)]
    return (thirds[0] + thirds[1] + thirds[2]) / jnp.maximum(flipped[3 * WIDTH : 3 * WIDTH + 1], 1.0)


def gather_kernel(
    slots, ranks, features, send, table, sums, lists, arrived
):
    size = (FAN + 1) * CHUNK

    def fetch(chunk):
        span = pl.ds(pl.multiple_of(chunk * size, size), size)
        return pltpu.make_async_copy(slots.at[span], lists.at[span], arrived.at[chunk])

    third = INPUTS // 3
    fetch(0).start()
    for chunk in range(1, ROWS // CHUNK):
        fetch(chunk).start()

    lane = iota((128, 128), 1)

    def fill(step, carry):
        for part in range(TABLE_STEP):
            at = pl.multiple_of((step * TABLE_STEP + part) * 128, 128)
            blocks = [features[:, pl.ds(t * third + at, 128)].astype(F32) for t in range(3)]
            flipped = jnp.concatenate(blocks + [jnp.ones((8, 128), F32)], axis=0).T
            for t in range(3):
                kept = ((lane >= t * WIDTH) & (lane < (t + 1) * WIDTH)) | (lane >= 3 * WIDTH)
                table[pl.ds(t * third + at, 128), :] = jnp.where(kept, flipped, 0.0)
        return carry

    lax.fori_loop(0, third // 128 // TABLE_STEP, fill, 0)
    table[pl.ds(INPUTS, 8), :] = jnp.zeros((8, 128), F32)

    def chunk_step(chunk, carry):
        fetch(chunk).wait()

        def block(step, inner):
            first = chunk * size + step * UNROLL
            at = pl.multiple_of(chunk * CHUNK + step * UNROLL, UNROLL)
            result = sums.at[pl.ds(at, UNROLL), :]

            def add(depth):
                named = [lists.at[pl.ds(first + slot * CHUNK, UNROLL)] for slot in range(depth)]
                for row in range(UNROLL):
                    result[pl.ds(row, 1), :] = add_all(
                        [table[pl.ds(named[slot][row], 1), :] for slot in range(depth)]
                    )

            def choose(low, high):
                if low == high:
                    add(low)
                    return
                middle = (low + high) // 2
                lax.cond(
                    deepest <= middle,
                    lambda: choose(low, middle),
                    lambda: choose(middle + 1, high),
                )

            deepest = lists[first + FAN * CHUNK]
            choose(LEAST, FAN)
            return inner

        return lax.fori_loop(0, CHUNK // UNROLL, block, carry)

    lax.fori_loop(0, ROWS // CHUNK, chunk_step, 0)

    def pair_step(step, carry):
        for part in range(0, PAIRS, 2):
            line = (step * PAIRS + part) * 3
            blocks = []
            for k in range(0, 6, 2):
                at = pl.multiple_of((line + k) * 128, 128)
                means = [mean_of(sums[pl.ds(at + half * 128, 128), :].T) for half in range(2)]
                means = jnp.concatenate(means, axis=1).astype(BF16)
                for half in range(2):
                    blocks.append(contract(means, moved(ranks, line + k + half), 1, 0))
            for pair in range(2):
                block = jnp.concatenate(blocks[pair * 3 : pair * 3 + 3], axis=1)
                owner = 2 * (step * PAIRS + part + pair)
                for half in range(2):
                    tile = folded(block, half, jnp.zeros((8, 64), F32))
                    send[owner + half] = tile.astype(BF16)
        return carry

    lax.fori_loop(0, FEAT // 2 // PAIRS, pair_step, 0)


def unfolded(tile):
    rest = jnp.concatenate([tile[40:64, :64], tile[40:56, 64:]], axis=0)
    return jnp.concatenate([tile[:40], rest, jnp.zeros((40, 64), F32)], axis=1)


def choose_kernel(own, chosen, marks):
    for source in range(FEAT):
        last = own[source, pl.ds(128, 16), :].astype(F32)
        marks[pl.ds(source, 1), :] = jnp.concatenate(
            [last[8 + k : 9 + k, 64:] for k in range(3)] + [jnp.zeros((1, 64), F32)], axis=1
        )
    rank = contract(marks[...].astype(BF16), earlier(SLAB), 1, 0)
    for pair in range(FEAT // 2):
        hits = []
        for source in (2 * pair, 2 * pair + 1):
            hit = (iota((UNION, SLAB), 0).astype(F32) == rank[source : source + 1]) & (
                marks[pl.ds(source, 1), :] > 0.0
            )
            hits.append(jnp.where(hit, 1.0, 0.0))
        chosen[pl.ds(pair * 2 * UNION, 2 * UNION), :] = jnp.concatenate(hits, axis=0).astype(BF16)


def hidden_kernel(spot, own, means, mine, theirs, bias, chosen, hidden, rows, stacked):
    for source in range(FEAT):
        tiles = [unfolded(own[source].astype(F32)[80:]), unfolded(means[source].astype(F32))]
        stacked[pl.ds(source * 80, 80), :] = jnp.concatenate(tiles, axis=0).astype(BF16)
    first = contract(stacked[...], mine[...], 0, 0)[:OWN]
    second = contract(stacked[...], theirs[...], 0, 0)[:OWN]
    even = spot[0] == 0
    pre = jnp.concatenate(
        [jnp.where(even, first, second), jnp.where(even, second, first)], axis=1
    )
    pre = jnp.where(spot[1] == 0, pre, jnp.concatenate([pre[128:], pre[:128]], axis=0))
    result = jnp.maximum(pre + bias[...], 0.0).astype(BF16)
    hidden[...] = result
    padded = jnp.concatenate([result, jnp.zeros((SLAB - OWN, HIDDEN), BF16)], axis=0)
    rows[...] = contract(chosen[...], padded, 1, 0).astype(BF16)


def pick_kernel(place, mask, labels, block, picks, held, arrived):
    copy = pltpu.make_async_copy(block, held, arrived)
    copy.start()
    spots = iota((NAMED, TARGETS), 0)
    total = jnp.zeros((NAMED, TARGETS), F32)
    for slot in range(FAN):
        used = mask[slot].astype(F32)
        total = total + jnp.where(spots == place[pl.ds(slot, 1), :], used, 0.0)
    own = jnp.where(spots == place[pl.ds(FAN, 1), :], 1.0, 0.0)
    line = iota((16, TARGETS), 0)
    label = jnp.broadcast_to(labels[...], (16, TARGETS))
    high = label >> 7
    parts = jnp.where(line == 0, high, jnp.where(line == 1, label - high * 128, 0))
    blank = jnp.zeros((16, TARGETS), F32)
    picks[0] = jnp.concatenate([total, parts.astype(F32)], axis=0).astype(BF16)
    picks[1] = jnp.concatenate([own, blank], axis=0).astype(BF16)
    copy.wait()


def loss_kernel(spot, *refs):
    held, blocks = refs[:4], refs[4 : 4 + NODE // 2]
    stats, other, inputs, logits = refs[4 + NODE // 2 :]
    offsets = []
    for side in range(2):
        rows, picks = held[2 * side], held[2 * side + 1]
        total, own = picks[0][:NAMED], picks[1][:NAMED]
        count = contract(total, jnp.ones((NAMED, 128), BF16), 0, 0)[:, :1]
        agg = contract(total, rows[...], 0, 0) / jnp.maximum(count, 1.0)
        span = pl.ds(side * TARGETS, TARGETS)
        inputs[span, pl.ds(0, HIDDEN)] = contract(own, rows[...], 0, 0).astype(BF16)
        inputs[span, pl.ds(HIDDEN, HIDDEN)] = agg.astype(BF16)
        parts = picks[0][NAMED:].astype(F32)
        label = jnp.broadcast_to(parts[:1] * 128.0 + parts[1:2], (TARGETS, TARGETS)).T
        offsets.append(label.astype(jnp.int32) - iota((TARGETS, TARGETS), 1))
    width = blocks[0].shape[1]
    start = (
        jnp.full((TARGETS, TARGETS), -jnp.inf, F32),
        jnp.zeros((TARGETS, TARGETS), F32),
        jnp.zeros((TARGETS, TARGETS), F32),
    )
    running = [start, start]
    for step in range(2 * len(blocks) + 1):
        block, side = step // 2, step % 2
        if block < len(blocks):
            mine = inputs[pl.ds(side * TARGETS, TARGETS), :]
            logits[step % 2] = contract(mine, blocks[block][...], 1, 0)
        if step > 0:
            block, side = (step - 1) // 2, (step - 1) % 2
            last = logits.at[(step - 1) % 2]
            largest, summed, picked = running[side]
            spans = [pl.ds(k * 128, 128) for k in range(width // 128)]
            here = offsets[side] - ((spot[0] + HOPS[block]) & 7) * width
            now = largest
            for span in spans:
                now = jnp.maximum(now, last[:, span])
            summed = summed * jnp.exp(largest - now)
            for k, span in enumerate(spans):
                part = last[:, span]
                summed = summed + jnp.exp(part - now)
                picked = picked + jnp.where(here == k * 128, part, 0.0)
            running[side] = (now, summed, picked)
    for side, ref in ((0, stats), (1, other)):
        largest, summed, picked = running[side]
        most = jnp.max(largest, axis=1, keepdims=True)
        total = jnp.sum(summed * jnp.exp(largest - most), axis=1, keepdims=True)
        found = jnp.sum(picked, axis=1, keepdims=True)
        lane = iota((TARGETS, TARGETS), 1)
        table = jnp.where(lane == 0, most, jnp.where(lane == 1, total, found))
        ref[...] = table.T[:8]


VMEM = pl.BlockSpec(memory_space=pltpu.VMEM)
HBM = pl.BlockSpec(memory_space=pltpu.HBM)
SMEM = pl.BlockSpec(memory_space=pltpu.SMEM)


def call_prepare(core, arrays):
    shapes = [array.shape for array in arrays]
    shapes[3] = (WIDTH, ROWS)
    return pl.pallas_call(
        prepare_kernel,
        out_shape=(
            jax.ShapeDtypeStruct((FEAT, 144, 128), BF16),
            jax.ShapeDtypeStruct((16, TARGETS), jnp.int32),
            jax.ShapeDtypeStruct((LINES * (FAN + 1), 128), jnp.int32),
            jax.ShapeDtypeStruct((LINES, 128), jnp.int32),
        ),
        in_specs=[SMEM] + [HBM] * 6,
        out_specs=(HBM, VMEM, VMEM, VMEM),
        scratch_shapes=[
            *[pltpu.VMEM(shape, array.dtype) for shape, array in zip(shapes, arrays)],
            pltpu.VMEM((FEAT, 144, 128), BF16),
            pltpu.VMEM((32, LINES, 128), F32),
            pltpu.SemaphoreType.DMA((FEAT // 8,)),
            pltpu.SemaphoreType.DMA((6,)),
        ],
        compiler_params=pltpu.CompilerParams(vmem_limit_bytes=MOST),
        cost_estimate=pl.CostEstimate(flops=10**8, bytes_accessed=10**7, transcendentals=0),
    )(core, *arrays)


def call_gather(slots, ranks, table):
    return pl.pallas_call(
        gather_kernel,
        out_shape=jax.ShapeDtypeStruct((FEAT, 64, 128), BF16),
        in_specs=[pl.BlockSpec(memory_space=pl.ANY), VMEM, VMEM],
        out_specs=VMEM,
        scratch_shapes=[
            pltpu.VMEM((INPUTS + 8, 128), F32),
            pltpu.VMEM((ROWS, 128), F32),
            pltpu.SMEM(((FAN + 1) * ROWS,), jnp.int32),
            pltpu.SemaphoreType.DMA((ROWS // CHUNK,)),
        ],
        compiler_params=pltpu.CompilerParams(vmem_limit_bytes=24 * 2**20),
        cost_estimate=pl.CostEstimate(flops=0, bytes_accessed=0, transcendentals=0),
    )(slots, ranks, table)


def call_pick(place, mask, labels, block):
    return pl.pallas_call(
        pick_kernel,
        out_shape=(
            jax.ShapeDtypeStruct((2, NAMED + 16, TARGETS), BF16),
            jax.ShapeDtypeStruct(block.shape, BF16),
        ),
        in_specs=[VMEM] * 3 + [HBM],
        out_specs=(VMEM, VMEM),
        scratch_shapes=[pltpu.SemaphoreType.DMA],
        compiler_params=pltpu.CompilerParams(vmem_limit_bytes=16 * 2**20),
        cost_estimate=pl.CostEstimate(flops=10**7, bytes_accessed=6 * 10**6, transcendentals=0),
    )(place, mask, labels, block)


def call_loss(spot, rows, picks, rows_there, picks_there, blocks):
    sources = [rows, picks, rows_there, picks_there, *blocks]
    return pl.pallas_call(
        loss_kernel,
        out_shape=[jax.ShapeDtypeStruct((8, TARGETS), F32)] * 2,
        in_specs=[SMEM] + [VMEM] * len(sources),
        out_specs=[VMEM, VMEM],
        scratch_shapes=[
            pltpu.VMEM((2 * TARGETS, 2 * HIDDEN), BF16),
            pltpu.VMEM((2, TARGETS, blocks[0].shape[1]), F32),
        ],
        compiler_params=pltpu.CompilerParams(vmem_limit_bytes=16 * 2**20),
    )(spot, *sources)


def join_kernel(here, there, loss):
    most = jnp.maximum(here[0:1], there[0:1])
    total = here[1:2] * jnp.exp(here[0:1] - most) + there[1:2] * jnp.exp(there[0:1] - most)
    loss[...] = most + jnp.log(total) - (here[2:3] + there[2:3])


def call_join(here, there):
    return pl.pallas_call(
        join_kernel,
        out_shape=jax.ShapeDtypeStruct((1, TARGETS), F32),
        in_specs=[VMEM, VMEM],
        out_specs=VMEM,
        compiler_params=pltpu.CompilerParams(vmem_limit_bytes=2**20),
    )(here, there)


def body(
    features,
    first_neighbours,
    first_mask,
    second_neighbours,
    second_mask,
    target_index,
    labels,
    first_weight,
    first_bias,
    class_weight,
):
    spot = lax.axis_index("node").astype(jnp.int32)
    core = spot & 1
    table = features[:, 0, :]
    swap = [(device, device ^ 1) for device in range(NODE)]
    blocks = [class_weight]
    for hops in HOPS[1:]:
        around = [(device, (device - hops) % NODE) for device in range(NODE)]
        blocks.append(lax.ppermute(class_weight, "node", around))
    own, place, slots, ranks = call_prepare(
        core[None],
        [
            second_neighbours,
            target_index,
            first_weight,
            table,
            first_neighbours.reshape(FAN, LINES, 128),
            first_mask.reshape(FAN, LINES, 128),
        ],
    )
    own = lax.all_to_all(own, "feat", 0, 0)
    send = call_gather(slots.reshape(-1), ranks, table)
    send, own = lax.optimization_barrier((send, own))
    mine = own[:, : 2 * WIDTH].reshape(FEAT * 2 * WIDTH, 128)
    theirs = lax.ppermute(mine, "node", swap)
    means = lax.all_to_all(send, "feat", 0, 0)
    means, *blocks[2:] = lax.optimization_barrier((means, *blocks[2:]))
    side = jnp.stack([core, lax.axis_index("feat").astype(jnp.int32) & 1])
    chosen = pl.pallas_call(
        choose_kernel,
        out_shape=jax.ShapeDtypeStruct((NAMED, SLAB), BF16),
        in_specs=[VMEM],
        out_specs=VMEM,
        scratch_shapes=[pltpu.VMEM((FEAT, SLAB), F32)],
        compiler_params=pltpu.CompilerParams(vmem_limit_bytes=16 * 2**20),
        cost_estimate=pl.CostEstimate(flops=10**7, bytes_accessed=2 * 10**6, transcendentals=0),
    )(own)
    hidden, rows = pl.pallas_call(
        hidden_kernel,
        out_shape=(
            jax.ShapeDtypeStruct((OWN, HIDDEN), BF16),
            jax.ShapeDtypeStruct((NAMED, HIDDEN), BF16),
        ),
        in_specs=[SMEM] + [VMEM] * 6,
        out_specs=(VMEM, VMEM),
        scratch_shapes=[pltpu.VMEM((FEAT * 80, 256), BF16)],
        compiler_params=pltpu.CompilerParams(vmem_limit_bytes=51 * 2**20),
    )(side, own, means, mine, theirs, first_bias[None, :], chosen)
    picks, blocks[0] = call_pick(place, second_mask, labels, class_weight)
    picks_there = lax.ppermute(picks, "node", swap)
    rows = lax.all_to_all(rows.reshape(FEAT, UNION, HIDDEN), "feat", 0, 0)
    rows = rows.reshape(FEAT * UNION, HIDDEN)
    rows_there = lax.ppermute(rows, "node", swap)
    here, there = call_loss(spot[None], rows, picks, rows_there, picks_there, blocks)
    there = lax.ppermute(there, "node", swap)
    loss = call_join(here, there)
    return (hidden[None], loss)


def solution(mesh):
    placed = (
        P("feat", "node", None),
        P(None, "node", None),
        P(None, "node", None),
        P(None, "node", "feat"),
        P(None, "node", "feat"),
        P("node", "feat"),
        P("node", "feat"),
        P(None, "feat", None),
        P(),
        P(None, "node"),
    )
    return jax.shard_map(
        body,
        mesh=mesh,
        in_specs=placed,
        out_specs=(P("node", "feat", None), P("node", "feat")),
        check_vma=False,
    )
```
